32 devices in a mesh: mol: 8 (over z, core), stream: 2 (over y), head: 2 (over x).
Axes of the slice: x: 2, y: 2, z: 4, core: 2. Of those that a mesh axis runs over, the one named last changes fastest.
Arguments:
- tokens: bfloat16 [8192, 768], P(('mol', 'stream')), may hold values from -6 to 6
- cotangent: float32 [8192, 768], P(('mol', 'stream')), may hold values from -6 to 6
- attn_gain: float32 [768], replicated, may hold values from 0.25 to 1.75
- attn_shift: float32 [768], replicated, may hold values from -2 to 2
- query_weight: bfloat16 [768, 768], P(None, 'head'), may hold values from -0.21875 to 0.21875
- query_bias: float32 [768], P('head'), may hold values from -3 to 3
- key_weight: bfloat16 [768, 768], P(None, 'head'), may hold values from -0.21875 to 0.21875
- value_weight: bfloat16 [768, 768], P(None, 'head'), may hold values from -0.21875 to 0.21875
- value_bias: float32 [768], P('head'), may hold values from -3 to 3
- out_weight: bfloat16 [768, 768], P('head'), may hold values from -0.875 to 0.875
- out_bias: float32 [768], replicated, may hold values from -3 to 3
- ffn_gain: float32 [768], replicated, may hold values from 0.25 to 1.75
- ffn_shift: float32 [768], replicated, may hold values from -2 to 2
- up_weight: bfloat16 [768, 768], P(None, 'head'), may hold values from -0.21875 to 0.21875
- up_bias: bfloat16 [768], P('head'), may hold values from -3 to 3
- down_weight: bfloat16 [768, 768], P('head'), may hold values from -0.3125 to 0.3125
- down_bias: float32 [768], replicated, may hold values from -3 to 3
- atom_counts: int32 [8, 16], P('mol'), may hold values from 1 to 24, 154 in all within a row
- edge_counts: int32 [8, 16], P('mol'), may hold values from 1 to 64, 512 in all within a row
Outputs:
- output: float32 [8192, 768], P(('mol', 'stream'))
- tokens_grad: float32 [8192, 768], P(('mol', 'stream'))
- attn_gain_grad: float32 [768], P('head')
- attn_shift_grad: float32 [768], P('head')
- query_weight_grad: float32 [768, 768], P(None, 'head')
- query_bias_grad: float32 [768], P('head')
- key_weight_grad: float32 [768, 768], P(None, 'head')
- value_weight_grad: float32 [768, 768], P(None, 'head')
- value_bias_grad: float32 [768], P('head')
- out_weight_grad: float32 [768, 768], P('head')
- out_bias_grad: float32 [768], P('head')
- ffn_gain_grad: float32 [768], P('head')
- ffn_shift_grad: float32 [768], P('head')
- up_weight_grad: float32 [768, 768], P(None, 'head')
- up_bias_grad: float32 [768], P('head')
- down_weight_grad: float32 [768, 768], P('head')
- down_bias_grad: float32 [768], P('head')
The draws below stay inside these ranges and needn't reach their ends.
Inputs may be any that keep to these rules, and one draw needn't show every extreme that they name: `atom_counts`: A row holds the atom counts of the 16 molecules of one mol index; each row sums to exactly 154, and its largest entry is exactly 24. `edge_counts`: A row holds the edge token counts of the 16 molecules of one mol index; each row sums to exactly 512, and its largest entry is exactly 64.
All inputs are finite; a program needn't handle non-finite values.
Results may differ from the reference program's by a relative error of at most 0.013.
Values may be sent and summed in bfloat16 or wider, within the bound.
A program may use at most 256 MiB of HBM per device.

```python
import math
import jax
import jax.numpy as jnp
import numpy as np
from jax import lax

D = 768
HEADS = 32
HEAD_DIM = 24
FF = 768
TOK_DEV = 512
MOL_DEV = 16
ATOM_MOST = 24
EDGE_MOST = 64
ROWS = 8192
N_MOL = 8


def shard_levels(own_key, extent, cuts, low, top_value):
    def one(position, parts):
        steps = jax.random.uniform(jax.random.fold_in(jax.random.fold_in(own_key, 6), position), (parts,), jnp.float32, low / len(cuts), top_value / len(cuts))
        return jnp.repeat(jnp.exp(steps), extent[position] // parts).reshape((-1,) + (1,) * (len(extent) - position - 1))

    factor_of = one(*cuts[0])
    for cut in cuts[1:]:
        factor_of = factor_of * one(*cut)
    return factor_of


def length_profile(amount, total, limit, skew):
    portions = [(1 << 20) // math.isqrt(rank ** skew) + 1 for rank in range(2, amount + 1)]
    rest, given = total - limit - (amount - 1), [1] * (amount - 1)
    while rest > 0:
        free = [i for i in range(amount - 1) if given[i] < limit]
        mass, budget = sum([portions[i] for i in free]), rest
        for i in free:
            extra = min(limit - given[i], max(1, budget * portions[i] // mass), rest)
            given[i] = given[i] + extra
            rest = rest - extra
    return np.array([limit] + given)


def ragged_sizes(rng, count, total, bound, slope):
    if count == 2:
        one = jax.random.randint(rng, (), max(1, total - bound), min(bound, total - 1) + 1)
        return jnp.stack([one, total - one])
    tallies = jnp.asarray(length_profile(count, total, bound, slope), jnp.int32)
    pairs = (count - 1) // 2
    source_of, taker = tallies[1:1 + 2 * pairs:2], tallies[2:2 + 2 * pairs:2]
    slack = jnp.minimum(source_of - 1, bound - taker)
    passed = jax.random.randint(jax.random.fold_in(rng, 1), (pairs,), 0, 1 << 20) % (slack + 1)
    tallies = tallies.at[1:1 + 2 * pairs:2].set(source_of - passed).at[2:2 + 2 * pairs:2].set(taker + passed)
    return tallies[jax.random.permutation(jax.random.fold_in(rng, 2), count)]


def centred(rng, dims, scale, reach, shards=(), kind=jnp.bfloat16):
    array = jax.random.normal(rng, dims, jnp.float32) * scale
    if len(shards) > 0:
        array = shard_levels(rng, dims, shards, -0.22, 0.18) * array
    return jnp.clip(array, min=-reach, max=reach).astype(kind)


def setup_inputs(seed: int = 0) -> dict:
    splits = jax.random.split(jax.random.key(seed), 20)
    return {
        "tokens": centred(splits[0], (ROWS, D), 1.0, 6.0, ((0, 16),)),
        "cotangent": centred(splits[1], (ROWS, D), 1.0, 6.0, ((0, 16),), jnp.float32),
        "attn_gain": jnp.clip(1.0 + 0.15 * jax.random.normal(splits[2], (D,), jnp.float32), 0.25, 1.75),
        "attn_shift": centred(splits[3], (D,), 0.3, 2.0, (), jnp.float32),
        "query_weight": centred(splits[4], (D, D), D ** -0.5, 0.21875, ((1, 2),)),
        "query_bias": centred(splits[5], (D,), 0.5, 3.0, ((0, 2),), jnp.float32),
        "key_weight": centred(splits[6], (D, D), D ** -0.5, 0.21875, ((1, 2),)),
        "value_weight": centred(splits[7], (D, D), D ** -0.5, 0.21875, ((1, 2),)),
        "value_bias": centred(splits[8], (D,), 0.5, 3.0, ((0, 2),), jnp.float32),
        "out_weight": centred(splits[9], (D, D), (D // 16) ** -0.5, 0.875, ((0, 2),)),
        "out_bias": centred(splits[10], (D,), 0.5, 3.0, (), jnp.float32),
        "ffn_gain": jnp.clip(1.0 + 0.15 * jax.random.normal(splits[11], (D,), jnp.float32), 0.25, 1.75),
        "ffn_shift": centred(splits[12], (D,), 0.3, 2.0, (), jnp.float32),
        "up_weight": centred(splits[13], (D, FF), D ** -0.5, 0.21875, ((1, 2),)),
        "up_bias": centred(splits[14], (FF,), 0.5, 3.0, ((0, 2),)),
        "down_weight": centred(splits[15], (FF, D), (FF // 2) ** -0.5, 0.3125, ((0, 2),)),
        "down_bias": centred(splits[16], (D,), 0.5, 3.0, (), jnp.float32),
        "atom_counts": jax.vmap(lambda own: ragged_sizes(own, MOL_DEV, TOK_DEV // 3 - MOL_DEV, ATOM_MOST, 1))(jax.random.split(splits[17], N_MOL)).reshape((N_MOL, MOL_DEV)).astype(jnp.int32),
        "edge_counts": jax.vmap(lambda own: ragged_sizes(own, MOL_DEV, TOK_DEV, EDGE_MOST, 1))(jax.random.split(splits[18], N_MOL)).reshape((N_MOL, MOL_DEV)).astype(jnp.int32),
    }


@jax.custom_vjp
def low(v):
    return lax.optimization_barrier(v.astype(jnp.bfloat16)).astype(jnp.float32)

@jax.custom_vjp
def low_back(v):
    return v

def low_keep(v):
    return (low(v), None)

def low_pass(kept, grad):
    return (grad,)

def back_keep(v):
    return (v, None)

def back_low(kept, grad):
    return (low(grad),)
low.defvjp(low_keep, low_pass)
low_back.defvjp(back_keep, back_low)

def exact_dot(operand, partner):
    return jnp.dot(operand, partner, precision=lax.Precision.HIGHEST)

def norm_apply(values, gain_vec, shift_vec):
    row_mean = lax.optimization_barrier(jnp.mean(values, axis=-1, keepdims=True))
    centered = values - row_mean
    variance = lax.optimization_barrier(jnp.mean(centered * centered, axis=-1, keepdims=True))
    return centered * lax.rsqrt(variance + 1e-05) * gain_vec + shift_vec

def segment_ids(counts, added, slot_count):
    seg_ends = jnp.cumsum(counts + added).astype(jnp.int32)
    positions = jnp.arange(slot_count, dtype=jnp.int32)
    return lax.optimization_barrier(jnp.sum((positions[:, None] >= seg_ends[None, :]).astype(jnp.int32), axis=1)).astype(jnp.int32)

def group_forward(parameters, residual, atoms, edges):
    attn_gain, attn_shift, query_weight, query_bias, key_weight, value_weight, value_bias, out_weight, out_bias, ffn_gain, ffn_shift, up_weight, up_bias, down_weight, down_bias = parameters
    key_seg = jnp.concatenate([segment_ids(atoms, 1, TOK_DEV), segment_ids(edges, 0, TOK_DEV)])
    live_rows = (key_seg < MOL_DEV).astype(residual.dtype)[:, None]
    row_count = residual.shape[0]
    first_in = low(norm_apply(residual, attn_gain, attn_shift))
    queries = low_back(low(exact_dot(first_in, query_weight) + query_bias))
    key_rows = low_back(low(exact_dot(first_in, key_weight)))
    value_rows = low_back(low(exact_dot(first_in, value_weight) + value_bias))
    query_h = queries.reshape(row_count, HEADS, HEAD_DIM)
    key_h = key_rows.reshape(row_count, HEADS, HEAD_DIM)
    value_h = value_rows.reshape(row_count, HEADS, HEAD_DIM)
    scores = jnp.einsum('qhd,khd->hqk', query_h, key_h, precision=lax.Precision.HIGHEST) * HEAD_DIM ** (-0.5)
    scores = low_back(scores)
    same_mol = key_seg[:, None] == key_seg[None, :]
    scores = jnp.where(same_mol[None], scores, -1e+30)
    prob_low = low(jax.nn.softmax(scores, axis=-1))
    attended = jnp.einsum('hqk,khd->qhd', prob_low, value_h, precision=lax.Precision.HIGHEST).reshape(row_count, HEADS * HEAD_DIM)
    attended = low_back(low(attended))
    branch_out = low_back(exact_dot(attended, out_weight) + out_bias)
    middle = residual + live_rows * branch_out
    second_in = low(norm_apply(middle, ffn_gain, ffn_shift))
    inner_pre = low_back(exact_dot(second_in, up_weight) + up_bias)
    hidden = low(jax.nn.gelu(inner_pre, approximate=False))
    ffn_out = low_back(exact_dot(hidden, down_weight) + down_bias)
    return middle + live_rows * ffn_out

def reference(tokens, cotangent, attn_gain, attn_shift, query_weight, query_bias, key_weight, value_weight, value_bias, out_weight, out_bias, ffn_gain, ffn_shift, up_weight, up_bias, down_weight, down_bias, atom_counts, edge_counts):
    parameters = tuple((member.astype(jnp.float32) for member in (attn_gain, attn_shift, query_weight, query_bias, key_weight, value_weight, value_bias, out_weight, out_bias, ffn_gain, ffn_shift, up_weight, up_bias, down_weight, down_bias)))
    residual = tokens.astype(jnp.float32).reshape(N_MOL, 2 * TOK_DEV, D)

    def whole_layer(param_set, resid_all):

        def scan_step(running, group_data):
            resid_group, atoms, edges = group_data
            return (running, jax.checkpoint(group_forward)(param_set, resid_group, atoms, edges))
        _, stacked = lax.scan(scan_step, jnp.zeros((), jnp.float32), (resid_all, atom_counts, edge_counts))
        return stacked
    output, pull_back = jax.vjp(whole_layer, parameters, residual)
    weight_grads, resid_grad = pull_back(cotangent.astype(output.dtype).reshape(N_MOL, 2 * TOK_DEV, D))
    attn_gain_grad, attn_shift_grad, query_weight_grad, query_bias_grad, key_weight_grad, value_weight_grad, value_bias_grad, out_weight_grad, out_bias_grad, ffn_gain_grad, ffn_shift_grad, up_weight_grad, up_bias_grad, down_weight_grad, down_bias_grad = weight_grads
    return (output.reshape(ROWS, D), resid_grad.reshape(ROWS, D), attn_gain_grad, attn_shift_grad, query_weight_grad, query_bias_grad, key_weight_grad, value_weight_grad, value_bias_grad, out_weight_grad, out_bias_grad, ffn_gain_grad, ffn_shift_grad, up_weight_grad, up_bias_grad, down_weight_grad, down_bias_grad)
```

```python
import functools
import math

import jax
import jax.numpy as jnp
from jax import lax
from jax.experimental import pallas as pl
from jax.experimental.pallas import tpu as pltpu
from jax.sharding import PartitionSpec as P

HEAD_DIM = 24
BF = jnp.bfloat16
F32 = jnp.float32
MESH = pl.DeviceIdType.MESH
EDGES = 512
NODES = 192
TOTAL = EDGES + NODES
PADDED = 768
HEADS_HERE = 8
SCALE = HEAD_DIM ** (-0.5)
SCALE2 = SCALE * math.log2(math.e)
BLOCKS = (
    (0, 256, ((0, 384), (512, 256))),
    (256, 256, ((128, 384), (512, 256))),
    (512, 192, ((0, 768),)),
)
OWNERS = (((0, 0), 512, 192), ((1, 0), 0, 256), ((1, 1), 256, 256))


def nn(a, b):
    return jnp.dot(a, b, preferred_element_type=F32)


def nt(a, b):
    return lax.dot_general(a, b, (((1,), (1,)), ((), ())), preferred_element_type=F32)


def tn(a, b):
    return lax.dot_general(a, b, (((0,), (0,)), ((), ())), preferred_element_type=F32)


def row_loop(count, step, fn, init):
    def body(i, carry):
        return fn(pl.ds(pl.multiple_of(i * step, step), step), carry)

    return lax.fori_loop(0, count // step, body, init)


def normed(x):
    mu = jnp.mean(x, axis=-1, keepdims=True)
    xc = x - mu
    var = jnp.mean(xc * xc, axis=-1, keepdims=True)
    r = lax.rsqrt(var + 1e-05)
    return xc * r, r


def col_sum(x):
    return jnp.sum(x, axis=0, keepdims=True)


SEM = {}


def sem_id(name, count=1):
    if name not in SEM:
        SEM[name] = sum(n for _, n in SEM.values()), count
    return SEM[name][0]


N_SEMS = 96
N_LOCAL = 24


def layer_kernel(
    tokens, cot, wq, wk, wv, wo, wu, wd,
    atoms, edges,
    a_gain, a_shift, q_bias, v_bias, o_bias, f_gain, f_shift, u_bias, d_bias,
    d_out, d_tok, f1, f2, vec,
    tok, res, cotv, ww, fwo, fwu, fwd, ub, fin1, qkv, dxw, qm, dam,
    p0, p1, p2, bias, segc, attf, att, ain, da, delta,
    t0, t1, n2s, r2s, mid, sec, hid, dc, ig, ac, ato, ago, mgd,
    ds, dkf, dvf,
    g1, gs1, qr, gq, zr1, g2, gs2, zr2, fp, fin,
    vq, vz, vc,
    ss, rs, ls,
):
    m, s, h = lax.axis_index("mol"), lax.axis_index("stream"), lax.axis_index("head")
    z, c = m // 2, lax.rem(m, 2)
    zc = lax.axis_size("mol") // 2
    me = 2 * s + h
    x_peer, y_peer, xy_peer = (m, s, 1 - h), (m, 1 - s, h), (m, 1 - s, 1 - h)
    quad = (x_peer, y_peer, xy_peer)
    twin = (2 * z + 1 - c, s, h)
    z_peers = [(2 * lax.rem(z + d, zc) + c, s, h) for d in range(1, zc)]

    def remote(name, src, dst, dev, k=0, count=1):
        i = sem_id(name, count) + k
        return pltpu.make_async_remote_copy(
            src_ref=src, dst_ref=dst, send_sem=ss.at[i], recv_sem=rs.at[i],
            device_id=dev, device_id_type=MESH,
        )

    def local(k, src, dst):
        return pltpu.make_async_copy(src, dst, ls.at[k])

    own = pl.multiple_of(256 * h, 256)
    other = pl.multiple_of(256 * (1 - h), 256)
    window = pl.multiple_of(128 * s, 128)

    loads = [
        local(0, tokens.at[pl.ds(own, 256)], res),
        local(1, cot.at[pl.ds(own, 256)], cotv),
        local(2, wq.at[:, pl.ds(window, 256)], ww.at[:, 0:256]),
        local(3, wk.at[:, pl.ds(window, 256)], ww.at[:, 256:512]),
        local(4, wv.at[:, pl.ds(window, 256)], ww.at[:, 512:768]),
        local(5, wo, fwo.at[h]),
        local(6, wu, fwu.at[h]),
        local(7, wd, fwd.at[h]),
    ]
    edge_load = local(8, tokens, tok.at[0:EDGES])
    node_load = local(9, tokens.at[0:NODES], tok.at[EDGES:TOTAL])
    pl.when(s == 1)(edge_load.start)
    pl.when(s == 0)(node_load.start)
    for copy in loads:
        copy.start()
    ub[h] = jnp.broadcast_to(u_bias[...].astype(F32), (8, 384))

    barrier = pltpu.get_barrier_semaphore()
    greeted = [*quad, twin, *z_peers]
    for dev in greeted:
        pl.semaphore_signal(barrier, inc=1, device_id=dev, device_id_type=MESH)
    pl.semaphore_wait(barrier, len(greeted))

    def edge_part(k, half):
        rows = pl.ds(pl.multiple_of(256 * half + 128 * k, 128), 128)
        return rows

    tok_y = [
        remote("tok_y", tokens.at[edge_part(k, h)], tok.at[edge_part(k, h)], y_peer, k, 2)
        for k in range(2)
    ]
    tok_x = [
        remote("tok_x", tok.at[edge_part(k, h)], tok.at[edge_part(k, h)], x_peer, k, 2)
        for k in range(2)
    ]
    tok_x_in = [
        remote("tok_x", tok.at[edge_part(k, 1 - h)], tok.at[edge_part(k, 1 - h)], x_peer, k, 2)
        for k in range(2)
    ]
    tok_n = remote("tok_n", tokens.at[0:NODES], tok.at[EDGES:TOTAL], y_peer)

    @pl.when(s == 1)
    def _():
        for copy in tok_y:
            copy.start()

    pl.when(s == 0)(tok_n.start)
    u_send = remote("ub", ub.at[h], ub.at[h], x_peer)
    u_send.start()
    part_o = pl.ds(pl.multiple_of(192 * c, 192), 192)
    part_u = pl.ds(pl.multiple_of(384 * c, 384), 384)
    w_out = [
        remote("wo_x", wo.at[part_o], fwo.at[h, part_o], x_peer),
        remote("wu_x", wu.at[part_u], fwu.at[h, part_u], x_peer),
        remote("wd_x", wd.at[part_o], fwd.at[h, part_o], x_peer),
    ]
    for copy in w_out:
        copy.start()
    w_in = [
        remote("wo_x", wo.at[part_o], fwo.at[1 - h, part_o], x_peer),
        remote("wu_x", wu.at[part_u], fwu.at[1 - h, part_u], x_peer),
        remote("wd_x", wd.at[part_o], fwd.at[1 - h, part_o], x_peer),
    ]
    w_twin = [
        remote("wo_c", fwo.at[1 - h, part_o], fwo.at[1 - h, part_o], twin),
        remote("wu_c", fwu.at[1 - h, part_u], fwu.at[1 - h, part_u], twin),
        remote("wd_c", fwd.at[1 - h, part_o], fwd.at[1 - h, part_o], twin),
    ]

    def share_weight(k):
        w_in[k].wait_recv()
        w_twin[k].start()

    def ends_of(counts, added):
        total, ends = 0, []
        for j in range(counts.shape[1]):
            total = total + counts[0, j] + added
            ends.append(total)
        return ends

    node_ends, edge_ends = ends_of(atoms, 1), ends_of(edges, 0)
    live_count = jnp.where(s == 0, node_ends[-1], edge_ends[-1])

    def seg_of(position, ends):
        seg = jnp.zeros_like(position)
        for end in ends:
            seg = seg + jnp.where(position >= end, 1, 0)
        return seg

    segc[0:EDGES] = seg_of(lax.broadcasted_iota(jnp.int32, (EDGES, 1), 0), edge_ends)
    segc[EDGES:TOTAL] = seg_of(lax.broadcasted_iota(jnp.int32, (NODES, 1), 0), node_ends)
    at_row = lax.broadcasted_iota(jnp.int32, (1, PADDED), 1)
    seg_r = jnp.where(at_row < EDGES, seg_of(at_row, edge_ends), seg_of(at_row - EDGES, node_ends))
    seg_r = jnp.where(at_row < TOTAL, seg_r, -1)

    lane = lax.broadcasted_iota(jnp.int32, (1, 256), 1) - 64 * s
    head_of = jnp.where((lane >= 0) & (lane < 192), lane // HEAD_DIM, -1)
    zero = jnp.zeros((), BF)

    qkv[TOTAL:PADDED] = jnp.zeros((PADDED - TOTAL, 768), BF)
    bias_row = jnp.concatenate(
        [
            q_bias[:, pl.ds(window, 256)],
            jnp.zeros((1, 256), F32),
            v_bias[:, pl.ds(window, 256)],
        ],
        axis=1,
    )

    def project(first, count):
        def norm_rows(i, carry):
            rows = pl.ds(pl.multiple_of(first + i * 64, 64), 64)
            n1, _ = normed(tok[rows].astype(F32))
            fin1[rows] = (n1 * a_gain[...] + a_shift[...]).astype(BF)
            return carry

        lax.fori_loop(0, count // 64, norm_rows, 0)
        rows = pl.ds(pl.multiple_of(first, 64), count)
        qkv[rows] = (nn(fin1[rows], ww[...]) + bias_row).astype(BF)

    for copy in loads[2:5]:
        copy.wait()

    @pl.when(s == 1)
    def _():
        edge_load.wait()
        project(0, EDGES)
        tok_n.wait_recv()
        project(EDGES, NODES)

    @pl.when(s == 0)
    def _():
        node_load.wait()
        project(EDGES, NODES)
        for k in range(2):
            tok_y[k].wait_recv()
            tok_x[k].start()
        project(own, 256)
        for k in range(2):
            tok_x_in[k].wait_recv()
        project(other, 256)

    for j in range(HEADS_HERE):
        qm[j] = jnp.where(head_of == j, qkv[0:TOTAL, 0:256], zero)

    def send_rows(name, src, dst, k):
        dev_sh, first, count = OWNERS[k]
        target = (m, *dev_sh)
        mine = 2 * dev_sh[0] + dev_sh[1]

        @pl.when(me != mine)
        def _():
            i = sem_id(name + "_s", 3) + k
            j = sem_id(name, 4) + me
            pltpu.make_async_remote_copy(
                src_ref=src.at[first:first + count], dst_ref=dst.at[me, 0:count],
                send_sem=ss.at[i], recv_sem=rs.at[j], device_id=target, device_id_type=MESH,
            ).start()

        @pl.when(me == mine)
        def _():
            dst[mine, 0:count] = src[first:first + count]

    def wait_rows(name, src, dst):
        for k, (dev_sh, first, count) in enumerate(OWNERS):
            mine = 2 * dev_sh[0] + dev_sh[1]

            @pl.when(me == mine)
            def _():
                for r in range(4):
                    if r != mine:
                        j = sem_id(name, 4) + r
                        pltpu.make_async_remote_copy(
                            src_ref=src.at[first:first + count], dst_ref=dst.at[r, 0:count],
                            send_sem=ss.at[j], recv_sem=rs.at[j], device_id=x_peer, device_id_type=MESH,
                        ).wait_recv()

    def wait_sent(name, src, dst):
        for k, (dev_sh, first, count) in enumerate(OWNERS):
            mine = 2 * dev_sh[0] + dev_sh[1]

            @pl.when(me != mine)
            def _():
                i = sem_id(name + "_s", 3) + k
                pltpu.make_async_remote_copy(
                    src_ref=src.at[first:first + count], dst_ref=dst.at[me, 0:count],
                    send_sem=ss.at[i], recv_sem=rs.at[i], device_id=(m, *dev_sh), device_id_type=MESH,
                ).wait_send()

    def pick_heads(stacked, rows):
        total = None
        for j in range(HEADS_HERE):
            part = jnp.where(head_of == j, stacked[j * rows:(j + 1) * rows], 0.0)
            total = part if total is None else total + part
        return total

    probs = (p0, p1, p2)
    to_owner = (1, 2, 0)
    group = 2

    @pl.when(s == 0)
    def _():
        ain[:, NODES:256] = jnp.zeros((4, 256 - NODES, 256), BF)
        fin[:, NODES:256] = jnp.zeros((4, 256 - NODES, 768), BF)

    @pl.when((s == 0) & (h == 1))
    def _():
        ain[:, 0:NODES] = jnp.zeros((4, NODES, 256), BF)
        fin[:, 0:NODES] = jnp.zeros((4, NODES, 768), BF)

    for b, (q0, qn, segs) in enumerate(BLOCKS):
        o = 0
        for a, n in segs:
            bias[0:qn, o:o + n] = jnp.where(segc[q0:q0 + qn] == seg_r[:, a:a + n], 0.0, -1e30)
            o += n
        for j0 in range(0, HEADS_HERE, group):
            qb = qm[j0:j0 + group, q0:q0 + qn, :].reshape(group * qn, 256)
            raw = [nt(qb, qkv[a:a + n, 256:512]) for a, n in segs]
            for g in range(group):
                j, o, parts = j0 + g, 0, []
                for piece, (a, n) in zip(raw, segs):
                    parts.append(piece[g * qn:(g + 1) * qn] * SCALE2 + bias[0:qn, o:o + n])
                    o += n
                top = functools.reduce(
                    jnp.maximum, [jnp.max(x, axis=1, keepdims=True) for x in parts]
                )
                parts = [jnp.exp2(x - top) for x in parts]
                inv = 1.0 / sum(jnp.sum(x, axis=1, keepdims=True) for x in parts)
                o = 0
                for x, (a, n) in zip(parts, segs):
                    probs[b][j * qn:(j + 1) * qn, o:o + n] = (x * inv).astype(BF)
                    o += n
        o, acc = 0, None
        for a, n in segs:
            part = nn(probs[b][:, o:o + n], qkv[a:a + n, 512:768])
            acc = part if acc is None else acc + part
            o += n
        picked = pick_heads(acc, qn)
        attf[q0:q0 + qn] = picked
        att[q0:q0 + qn] = picked.astype(BF)
        send_rows("att", att, ain, to_owner[b])

    share_weight(0)
    share_weight(1)

    for copy in (loads[0], loads[1], *loads[5:8]):
        copy.wait()
    row_at = lax.broadcasted_iota(jnp.int32, (256, 1), 0) + own
    live_all = jnp.where(row_at < live_count, 1.0, 0.0)
    r2s[:, 1:2] = live_all
    wait_rows("att", att, ain)
    for x in range(2):
        ato[:, 384 * x:384 * x + 128] = ain[x, :, 0:128]
        ato[:, 384 * x + 128:384 * x + 256] = ain[x, :, 128:256] + ain[2 + x, :, 0:128]
        ato[:, 384 * x + 256:384 * x + 384] = ain[2 + x, :, 128:256]
    share_weight(2)
    for copy in w_twin:
        pass
    twin_o = pl.ds(pl.multiple_of(192 * (1 - c), 192), 192)
    twin_u = pl.ds(pl.multiple_of(384 * (1 - c), 384), 384)
    w_twin_in = [
        remote("wo_c", fwo.at[1 - h, twin_o], fwo.at[1 - h, twin_o], twin),
        remote("wu_c", fwu.at[1 - h, twin_u], fwu.at[1 - h, twin_u], twin),
        remote("wd_c", fwd.at[1 - h, twin_o], fwd.at[1 - h, twin_o], twin),
    ]
    w_twin_in[0].wait_recv()
    wo_all = fwo[...].reshape(768, 768)
    t0[...] = nn(ato[...], wo_all)
    live_of = lambda rows: r2s[rows, 1:2]

    def middle_rows(rows, carry):
        x = res[rows].astype(F32) + live_of(rows) * (t0[rows] + o_bias[...])
        mid[rows] = x
        n2, r2 = normed(x)
        n2s[rows] = n2
        r2s[rows, 0:1] = r2
        sec[rows] = (n2 * f_gain[...] + f_shift[...]).astype(BF)
        return carry

    row_loop(256, 64, middle_rows, 0)
    w_twin_in[1].wait_recv()
    u_recv = remote("ub", ub.at[1 - h], ub.at[1 - h], x_peer)
    u_recv.wait_recv()
    for x in range(2):
        t0[:, 384 * x:384 * (x + 1)] = nn(sec[...], fwu[x]) + ub[x, 0:1]

    def gelu_rows(rows, carry):
        u = t0[rows]
        cdf = 0.5 * (1.0 + lax.erf(u * math.sqrt(0.5)))
        hid[rows] = (u * cdf).astype(BF)
        t1[rows] = cdf + u * (jnp.exp(-0.5 * u * u) * (1.0 / math.sqrt(2.0 * math.pi)))
        return carry

    row_loop(256, 64, gelu_rows, 0)
    w_twin_in[2].wait_recv()
    wd_all = fwd[...].reshape(768, 768)
    t0[...] = nn(hid[...], wd_all)
    zero_row = jnp.zeros((1, 768), F32)

    def out_rows(rows, carry):
        live = live_of(rows)
        x = (mid[rows] + live * (t0[rows] + d_bias[...])) - res[rows].astype(F32)
        at = pl.ds(pl.multiple_of(own + rows.start, 64), 64)
        d_out[at] = x.astype(BF)
        down = (live * cotv[rows]).astype(BF)
        dc[rows] = down
        return carry + col_sum(down.astype(F32))

    down_bias_sum = row_loop(256, 64, out_rows, zero_row)
    own_rows = pl.ds(own, 256)
    other_rows = pl.ds(other, 256)
    out_send = remote("out", d_out.at[own_rows], d_out.at[own_rows], x_peer)
    out_send.start()
    t0[...] = nt(dc[...], wd_all)

    def inner_rows(rows, carry):
        x = (t0[rows] * t1[rows]).astype(BF)
        ig[rows] = x
        return carry + col_sum(x.astype(F32))

    up_bias_sum = row_loop(256, 64, inner_rows, zero_row)
    t0[...] = nt(ig[:, 0:384], fwu[0]) + nt(ig[:, 384:768], fwu[1])

    def second_rows(rows, carry):
        gain_sum, shift_sum, bias_sum = carry
        sg, n2 = t0[rows], n2s[rows]
        g = sg * f_gain[...]
        back = r2s[rows, 0:1] * (
            g - jnp.mean(g, axis=-1, keepdims=True) - n2 * jnp.mean(g * n2, axis=-1, keepdims=True)
        )
        mgd[rows] = back
        x = (live_of(rows) * (cotv[rows] + back)).astype(BF)
        ac[rows] = x
        return gain_sum + col_sum(sg * n2), shift_sum + col_sum(sg), bias_sum + col_sum(x.astype(F32))

    f_gain_sum, f_shift_sum, out_bias_sum = row_loop(
        256, 64, second_rows, (zero_row, zero_row, zero_row)
    )
    ago[...] = nt(ac[...], wo_all).astype(BF)

    for k, (dev_sh, first, count) in enumerate(OWNERS):
        mine = 2 * dev_sh[0] + dev_sh[1]

        @pl.when(me == mine)
        def _():
            for r in range(4):
                cols = slice(384 * (r % 2) + 128 * (r // 2), 384 * (r % 2) + 128 * (r // 2) + 256)
                if r == mine:
                    da[first:first + count] = ago[0:count, cols]
                else:
                    i, j = sem_id("da_s", 4) + r, sem_id("da", 3) + k
                    pltpu.make_async_remote_copy(
                        src_ref=ago.at[0:count, cols], dst_ref=da.at[first:first + count],
                        send_sem=ss.at[i], recv_sem=rs.at[j],
                        device_id=(m, r // 2, r % 2), device_id_type=MESH,
                    ).start()

    for cc in range(2):
        for xh in range(2):
            f = slice(384 * xh, 384 * (xh + 1))
            d = slice(384 * cc, 384 * (cc + 1))
            g1[cc, xh, 0:384] = tn(hid[:, f], dc[:, d]).astype(BF)
            g1[cc, xh, 384:768] = tn(ato[:, f], ac[:, d]).astype(BF)
            g1[cc, xh, 768:1152] = tn(sec[:, d], ig[:, f]).astype(BF)
    g1_twin = remote("g1_c", g1.at[1 - c], gs1, twin)
    g1_twin.start()
    g1_twin.wait_recv()

    def twin_sum(i, carry):
        rows = pl.ds(pl.multiple_of(i * 64, 64), 64)
        for xh in range(2):
            gs1[xh, rows] = (g1[c, xh, rows].astype(F32) + gs1[xh, rows].astype(F32)).astype(BF)
        return carry

    lax.fori_loop(0, 1152 // 64, twin_sum, 0)
    half_of = lambda t: pl.ds(pl.multiple_of(576 * t, 576), 576)
    g1_quad = [
        remote("g1_q", gs1.at[1 - h, half_of(s)], qr.at[0], x_peer, 0, 3),
        remote("g1_q", gs1.at[h, half_of(1 - s)], qr.at[1], y_peer, 1, 3),
        remote("g1_q", gs1.at[1 - h, half_of(1 - s)], qr.at[2], xy_peer, 2, 3),
    ]
    for copy in g1_quad:
        copy.start()

    for k, (dev_sh, first, count) in enumerate(OWNERS):
        mine = 2 * dev_sh[0] + dev_sh[1]

        @pl.when(me != mine)
        def _():
            j = sem_id("da", 3) + k
            pltpu.make_async_remote_copy(
                src_ref=ago.at[0:count, 0:256], dst_ref=da.at[first:first + count],
                send_sem=ss.at[j], recv_sem=rs.at[j], device_id=x_peer, device_id_type=MESH,
            ).wait_recv()

    head_col = lax.broadcasted_iota(jnp.int32, (256, 128), 1)
    lane_row = lax.broadcasted_iota(jnp.int32, (256, 128), 0) - 64 * s
    head_pick = jnp.where(
        (lane_row >= 0) & (lane_row < 192) & (lane_row // HEAD_DIM == head_col), 1.0, 0.0
    ).astype(BF)
    prod = da[0:TOTAL].astype(F32) * attf[...]
    prod_hi = prod.astype(BF)
    delta[...] = nn(prod_hi, head_pick) + nn((prod - prod_hi.astype(F32)).astype(BF), head_pick)
    for j in range(HEADS_HERE):
        dam[j] = jnp.where(head_of == j, da[0:TOTAL], zero)
    dkf[...] = jnp.zeros_like(dkf)
    dvf[...] = jnp.zeros_like(dvf)
    for b, (q0, qn, segs) in enumerate(BLOCKS):
        pr = probs[b]
        for j0 in range(0, HEADS_HERE, group):
            ab = dam[j0:j0 + group, q0:q0 + qn, :].reshape(group * qn, 256)
            o = 0
            for a, n in segs:
                pg = nt(ab, qkv[a:a + n, 512:768])
                for g in range(group):
                    j = j0 + g
                    r = slice(j * qn, (j + 1) * qn)
                    ds[r, o:o + n] = (
                        pr[r, o:o + n].astype(F32)
                        * (pg[g * qn:(g + 1) * qn] - delta[q0:q0 + qn, j:j + 1])
                    ).astype(BF)
                o += n
        o, acc = 0, None
        for a, n in segs:
            part = nn(ds[0:HEADS_HERE * qn, o:o + n], qkv[a:a + n, 256:512])
            acc = part if acc is None else acc + part
            o += n
        dxw[q0:q0 + qn, 0:256] = (pick_heads(acc, qn) * SCALE).astype(BF)
        o = 0
        for a, n in segs:
            dk = dv = None
            for j in range(HEADS_HERE):
                r = slice(j * qn, (j + 1) * qn)
                pk = tn(ds[r, o:o + n], qm[j, q0:q0 + qn])
                pv = tn(pr[r, o:o + n], dam[j, q0:q0 + qn])
                dk = pk if dk is None else dk + pk
                dv = pv if dv is None else dv + pv
            dkf[a:a + n] += dk
            dvf[a:a + n] += dv
            o += n
    dxw[:, 256:512] = (dkf[0:TOTAL] * SCALE).astype(BF)
    dxw[:, 512:768] = dvf[0:TOTAL].astype(BF)

    for k in (1, 2, 0):
        _, first, count = OWNERS[k]
        fp[first:first + count] = nt(dxw[first:first + count], ww[...]).astype(BF)
        send_rows("fp", fp, fin, k)

    for cc in range(2):
        g2[cc] = tn(fin1[0:TOTAL, 384 * cc:384 * (cc + 1)], dxw[...]).astype(BF)
    g2_twin = remote("g2_c", g2.at[1 - c], gs2, twin)
    g2_twin.start()
    qkv_bias_sum = col_sum(dxw[...].astype(F32))

    for copy in g1_quad:
        copy.wait_recv()

    def quad_sum(i, carry):
        rows = pl.ds(pl.multiple_of(i * 64, 64), 64)
        at = pl.ds(pl.multiple_of(576 * s + i * 64, 64), 64)
        x = gs1[h, at].astype(F32)
        for k in range(3):
            x = x + qr[k, rows].astype(F32)
        gq[rows] = x.astype(BF)
        return carry

    lax.fori_loop(0, 576 // 64, quad_sum, 0)
    zn1, zn2 = 576 // zc, 384 // zc

    def chunk(t, n):
        return pl.ds(pl.multiple_of(n * t, n), n)

    z1 = [
        remote("g1_z", gq.at[chunk(lax.rem(z + d, zc), zn1)], zr1.at[d - 1], z_peers[d - 1], d - 1, zc - 1)
        for d in range(1, zc)
    ]
    for copy in z1:
        copy.start()
    g2_twin.wait_recv()
    gs2[...] = (g2[c].astype(F32) + gs2[...].astype(F32)).astype(BF)
    z2 = [
        remote("g2_z", gs2.at[chunk(lax.rem(z + d, zc), zn2)], zr2.at[d - 1], z_peers[d - 1], d - 1, zc - 1)
        for d in range(1, zc)
    ]
    for copy in z2:
        copy.start()

    wait_rows("fp", fp, fin)

    def first_rows(rows, carry):
        gain_sum, shift_sum = carry
        fg = fin[0, rows].astype(F32)
        for r in range(1, 4):
            fg = fg + fin[r, rows].astype(F32)
        n1, r1 = normed(res[rows].astype(F32))
        g = fg * a_gain[...]
        back = r1 * (
            g - jnp.mean(g, axis=-1, keepdims=True) - n1 * jnp.mean(g * n1, axis=-1, keepdims=True)
        )
        at = pl.ds(pl.multiple_of(own + rows.start, 64), 64)
        d_tok[at] = (mgd[rows] + back).astype(BF)
        return gain_sum + col_sum(fg * n1), shift_sum + col_sum(fg)

    a_gain_sum, a_shift_sum = row_loop(256, 64, first_rows, (zero_row, zero_row))
    tok_send = remote("dtok", d_tok.at[own_rows], d_tok.at[own_rows], x_peer)
    tok_send.start()

    sums = [f_gain_sum, f_shift_sum, out_bias_sum, down_bias_sum, up_bias_sum, a_gain_sum, a_shift_sum, zero_row]
    sums += [jnp.where(me == r, qkv_bias_sum, 0.0) for r in range(4)] + [zero_row] * 4
    vq[me] = jnp.concatenate(sums, axis=0)
    v1 = [remote("v_q", vq.at[me], vq.at[me], dev, k, 3) for k, dev in enumerate(quad)]
    for copy in v1:
        copy.start()

    def finish(zs, dst_rows, own_part, parts, target):
        for copy in zs:
            copy.wait_recv()
        x = own_part.astype(F32)
        for d in range(zc - 1):
            x = x + parts[d].astype(F32)
        target[dst_rows] = x.astype(BF)

    at1 = pl.ds(pl.multiple_of(576 * s + zn1 * z, 16), zn1)
    at2 = pl.ds(pl.multiple_of(384 * c + zn2 * z, 16), zn2)
    finish(z1, (c, at1), gq[chunk(z, zn1)], zr1, f1)
    ag1 = [remote("f1_z", f1.at[c, at1], f1.at[c, at1], z_peers[d], d, zc - 1) for d in range(zc - 1)]
    for copy in ag1:
        copy.start()
    finish(z2, (s, at2), gs2[chunk(z, zn2)], zr2, f2)
    ag2 = [remote("f2_z", f2.at[s, at2], f2.at[s, at2], z_peers[d], d, zc - 1) for d in range(zc - 1)]
    for copy in ag2:
        copy.start()

    v1_in = [
        remote("v_q", vq.at[r], vq.at[r], dev, k, 3)
        for k, (dev, r) in enumerate(zip(quad, (2 * s + 1 - h, 2 - 2 * s + h, 3 - 2 * s - h)))
    ]
    for copy in v1_in:
        copy.wait_recv()
    vz[z] = vq[0] + vq[1] + vq[2] + vq[3]
    v2 = [remote("v_z", vz.at[z], vz.at[z], z_peers[d], d, zc - 1) for d in range(zc - 1)]
    for copy in v2:
        copy.start()

    for copy in ag1:
        copy.wait_recv()
    half1 = half_of(s)
    y1 = remote("f1_y", f1.at[c, half1], f1.at[c, half1], y_peer)
    y1.start()
    c1 = [remote("f1_c", f1.at[c, half1], f1.at[c, half1], twin, 0, 2)]
    c1[0].start()
    for copy in ag2:
        copy.wait_recv()
    half2 = pl.ds(pl.multiple_of(384 * c, 384), 384)
    y2 = remote("f2_y", f2.at[s, half2], f2.at[s, half2], y_peer)
    y2.start()
    c2 = [remote("f2_c", f2.at[s, half2], f2.at[s, half2], twin, 0, 2)]
    c2[0].start()
    for copy in v2:
        copy.wait_recv()
    vsum = vz[0]
    for d in range(1, zc):
        vsum = vsum + vz[d]
    vc[c] = vsum
    v3 = remote("v_c", vc.at[c], vc.at[c], twin)
    v3.start()
    y1.wait_recv()
    c1.append(remote("f1_c", f1.at[c, half_of(1 - s)], f1.at[c, half_of(1 - s)], twin, 1, 2))
    c1[1].start()
    y2.wait_recv()
    c2.append(remote("f2_c", f2.at[1 - s, half2], f2.at[1 - s, half2], twin, 1, 2))
    c2[1].start()
    v3.wait_recv()
    vec[...] = vc[0] + vc[1]
    for copy in (*c1, *c2):
        copy.wait_recv()
    tok_send.wait_recv()
    out_send.wait_recv()

    @pl.when(s == 1)
    def _():
        for copy in tok_y:
            copy.wait_send()

    @pl.when(s == 0)
    def _():
        tok_n.wait_send()
        for copy in tok_x:
            copy.wait_send()

    wait_sent("att", att, ain)
    wait_sent("fp", fp, fin)
    for k, (dev_sh, first, count) in enumerate(OWNERS):
        mine = 2 * dev_sh[0] + dev_sh[1]

        @pl.when(me == mine)
        def _():
            for r in range(4):
                if r != mine:
                    i = sem_id("da_s", 4) + r
                    pltpu.make_async_remote_copy(
                        src_ref=ago.at[0:count, 0:256], dst_ref=da.at[first:first + count],
                        send_sem=ss.at[i], recv_sem=rs.at[i], device_id=x_peer, device_id_type=MESH,
                    ).wait_send()

    for copy in (
        u_send, *w_out, *w_twin, out_send, g1_twin, *g1_quad, g2_twin, *z1, *z2, tok_send,
        *v1, *ag1, *ag2, *v2, y1, y2, *c1, *c2, v3,
    ):
        copy.wait_send()


def finish_kernel(
    tokens, cot, d_out, d_tok, f1, f2, vec,
    output, tokens_grad, a_gain, a_shift, wq, bq, wk, wv, bv, wo, bo, f_gain, f_shift, wu, bu, wd, bd,
):
    h = lax.axis_index("head")
    output[...] = tokens[...].astype(F32) + d_out[...].astype(F32)
    tokens_grad[...] = cot[...] + d_tok[...].astype(F32)
    for k in range(2):
        lanes = slice(384 * k, 384 * (k + 1))
        wd[:, lanes] = f1[k, 0:384].astype(F32)
        wo[:, lanes] = f1[k, 384:768].astype(F32)
        wu[lanes, :] = f1[k, 768:1152].astype(F32)

    def merge(a, b):
        a, b = a.astype(F32), b.astype(F32)
        return a[:, 0:128], a[:, 128:256] + b[:, 0:128], b[:, 128:256]

    for k, out in enumerate((wq, wk, wv)):
        cols = slice(256 * k, 256 * (k + 1))
        for t, x in enumerate(merge(f2[0, :, cols], f2[1, :, cols])):
            out[:, 128 * t:128 * (t + 1)] = x
    mine = pl.ds(pl.multiple_of(384 * h, 384), 384)
    for row, out in ((0, f_gain), (1, f_shift), (2, bo), (3, bd), (4, bu), (5, a_gain), (6, a_shift)):
        out[...] = vec[row:row + 1, mine]
    low = jnp.where(h == 0, vec[8:9], vec[9:10])
    high = jnp.where(h == 0, vec[10:11], vec[11:12])
    for first, out in ((0, bq), (512, bv)):
        for t, x in enumerate(merge(low[:, first:first + 256], high[:, first:first + 256])):
            out[:, 128 * t:128 * (t + 1)] = x


def fast_layer(
    tokens, cotangent, attn_gain, attn_shift, query_weight, query_bias, key_weight, value_weight,
    value_bias, out_weight, out_bias, ffn_gain, ffn_shift, up_weight, up_bias, down_weight,
    down_bias, atom_counts, edge_counts,
):
    zc = lax.axis_size("mol") // 2
    row = lambda v: v.reshape(1, -1)
    anywhere = pl.BlockSpec(memory_space=pl.ANY)
    vmem = pl.BlockSpec(memory_space=pltpu.VMEM)
    smem = pl.BlockSpec(memory_space=pltpu.SMEM)
    shape = jax.ShapeDtypeStruct
    SEM.clear()
    buf = lambda dtype, *dims: pltpu.VMEM(dims, dtype)
    scratch = [
        buf(BF, PADDED, 768), buf(BF, 256, 768), buf(F32, 256, 768), buf(BF, 768, 768),
        buf(BF, 2, 384, 768), buf(BF, 2, 768, 384), buf(BF, 2, 384, 768), buf(F32, 2, 8, 384),
        buf(BF, PADDED, 768), buf(BF, PADDED, 768), buf(BF, TOTAL, 768),
        buf(BF, HEADS_HERE, TOTAL, 256), buf(BF, HEADS_HERE, TOTAL, 256),
        buf(BF, 2048, 640), buf(BF, 2048, 640), buf(BF, 1536, 768),
        buf(F32, 256, 768), buf(jnp.int32, TOTAL, 1),
        buf(F32, TOTAL, 256), buf(BF, TOTAL, 256), buf(BF, 4, 256, 256), buf(BF, TOTAL, 256), buf(F32, TOTAL, 128),
        buf(F32, 256, 768), buf(F32, 256, 768), buf(F32, 256, 768), buf(F32, 256, 128), buf(F32, 256, 768),
        buf(BF, 256, 768), buf(BF, 256, 768), buf(BF, 256, 768), buf(BF, 256, 768), buf(BF, 256, 768),
        buf(BF, 256, 768), buf(BF, 256, 768), buf(F32, 256, 768),
        buf(BF, 2048, 768), buf(F32, PADDED, 256), buf(F32, PADDED, 256),
        buf(BF, 2, 2, 1152, 384), buf(BF, 2, 1152, 384), buf(BF, 3, 576, 384),
        buf(BF, 576, 384), buf(BF, zc - 1, 576 // zc, 384),
        buf(BF, 2, 384, 768), buf(BF, 384, 768), buf(BF, zc - 1, 384 // zc, 768),
        buf(BF, TOTAL, 768), buf(BF, 4, 256, 768),
        buf(F32, 4, 16, 768), buf(F32, zc, 16, 768), buf(F32, 2, 16, 768),
        pltpu.SemaphoreType.DMA((N_SEMS,)), pltpu.SemaphoreType.DMA((N_SEMS,)), pltpu.SemaphoreType.DMA((N_LOCAL,)),
    ]
    d_out, d_tok, f1, f2, vec = pl.pallas_call(
        layer_kernel,
        out_shape=[
            shape((512, 768), BF), shape((512, 768), BF), shape((2, 1152, 384), BF),
            shape((2, 768, 768), BF), shape((16, 768), F32),
        ],
        in_specs=[anywhere] * 8 + [smem] * 2 + [vmem] * 9,
        out_specs=[vmem] * 5,
        scratch_shapes=scratch,
        compiler_params=pltpu.CompilerParams(
            collective_id=0, has_side_effects=True, vmem_limit_bytes=60 * 2**20
        ),
        name="layer",
    )(
        tokens, cotangent, query_weight, key_weight, value_weight, out_weight, up_weight, down_weight,
        atom_counts, edge_counts,
        row(attn_gain), row(attn_shift), row(query_bias), row(value_bias), row(out_bias),
        row(ffn_gain), row(ffn_shift), row(up_bias), row(down_bias),
    )
    assert sum(n for _, n in SEM.values()) <= N_SEMS
    mat, tall, line = shape((384, 768), F32), shape((768, 384), F32), shape((1, 384), F32)
    big = shape((512, 768), F32)
    outs = pl.pallas_call(
        finish_kernel,
        out_shape=[big, big, line, line, tall, line, tall, tall, line, mat, line, line, line, tall, line, mat, line],
        in_specs=[vmem] * 7,
        out_specs=[vmem] * 17,
        compiler_params=pltpu.CompilerParams(vmem_limit_bytes=60 * 2**20),
        name="finish",
    )(tokens, cotangent, d_out, d_tok, f1, f2, vec)
    return tuple(o.reshape(-1) if o.shape[0] == 1 else o for o in outs)


def plain_dot(operand, partner):
    return jnp.dot(operand, partner, preferred_element_type=jnp.float32)


def lead_dot(operand, partner):
    return lax.dot_general(
        operand, partner, (((0,), (0,)), ((), ())), preferred_element_type=jnp.float32
    )


def tail_dot(operand, partner):
    return lax.dot_general(
        operand, partner, (((1,), (1,)), ((), ())), preferred_element_type=jnp.float32
    )


def norm_apply(values, gain_vec, shift_vec):
    row_mean = jnp.mean(values, axis=-1, keepdims=True)
    centered = values - row_mean
    variance = jnp.mean(centered * centered, axis=-1, keepdims=True)
    return centered * lax.rsqrt(variance + 1e-05) * gain_vec + shift_vec


def gelu_exact(values):
    return jax.nn.gelu(values, approximate=False)


def segment_ids(counts, added, slot_count):
    members = jnp.arange(counts.shape[0])
    earlier = members[:, None] <= members[None, :]
    seg_ends = jnp.sum(jnp.where(earlier, (counts + added)[:, None], 0), axis=0)
    positions = jnp.arange(slot_count, dtype=jnp.int32)
    return jnp.sum((positions[:, None] >= seg_ends[None, :]).astype(jnp.int32), axis=1)


def head_piece(vector, head_rank, head_share):
    return lax.dynamic_slice_in_dim(vector, head_rank * head_share, head_share)


def on_device(
    tokens,
    cotangent,
    attn_gain,
    attn_shift,
    query_weight,
    query_bias,
    key_weight,
    value_weight,
    value_bias,
    out_weight,
    out_bias,
    ffn_gain,
    ffn_shift,
    up_weight,
    up_bias,
    down_weight,
    down_bias,
    atom_counts,
    edge_counts,
):
    row_count = tokens.shape[0]
    model_width = tokens.shape[1]
    local_width = query_weight.shape[1]
    local_heads = local_width // HEAD_DIM
    head_count = lax.axis_size("head")
    head_rank = lax.axis_index("head")
    stream_rank = lax.axis_index("stream")
    molecules = atom_counts.shape[1]
    head_share = model_width // head_count
    score_scale = HEAD_DIM ** (-0.5)
    seg_node = segment_ids(atom_counts[0], 1, row_count)
    seg_edge = segment_ids(edge_counts[0], 0, row_count)
    key_seg = jnp.concatenate([seg_node, seg_edge])
    own_seg = jnp.where(stream_rank == 0, seg_node, seg_edge)
    live_rows = (own_seg < molecules).astype(jnp.float32)[:, None]
    residual = tokens.astype(jnp.float32)
    normed, norm_pull = jax.vjp(norm_apply, residual, attn_gain, attn_shift)
    first_in = normed.astype(jnp.bfloat16)
    queries = (plain_dot(first_in, query_weight) + query_bias).astype(jnp.bfloat16)
    keys_local = plain_dot(first_in, key_weight).astype(jnp.bfloat16)
    values_local = (plain_dot(first_in, value_weight) + value_bias).astype(jnp.bfloat16)
    all_keys, all_values = (
        lax.all_gather(keys_local, "stream", axis=0, tiled=True),
        lax.all_gather(values_local, "stream", axis=0, tiled=True),
    )
    key_count = all_keys.shape[0]
    key_heads = all_keys.reshape(key_count, local_heads, HEAD_DIM)
    value_heads = all_values.reshape(key_count, local_heads, HEAD_DIM)
    blocks = row_count // 512
    block_rows = row_count // blocks
    query_blocks = queries.reshape(blocks, block_rows, local_heads, HEAD_DIM)
    seg_blocks = own_seg.reshape(blocks, block_rows)

    def forward_block(pieces):
        query_part, seg_part = pieces
        scores = (
            jnp.einsum("qhd,khd->hqk", query_part, key_heads, preferred_element_type=jnp.float32)
            * score_scale
        )
        same_mol = (seg_part[:, None] == key_seg[None, :])[None]
        scores = jnp.where(same_mol, scores, -1e30)
        row_top = jnp.max(scores, axis=-1, keepdims=True)
        shifted = jnp.exp(scores - row_top)
        row_total = jnp.sum(shifted, axis=-1, keepdims=True)
        prob_low = (shifted / row_total).astype(jnp.bfloat16)
        attended_part = jnp.einsum(
            "hqk,khd->qhd", prob_low, value_heads, preferred_element_type=jnp.float32
        )
        return (attended_part.astype(jnp.bfloat16), (row_top + jnp.log(row_total))[..., 0])

    attended_blocks, lse_blocks = lax.map(forward_block, (query_blocks, seg_blocks))
    attended = attended_blocks.reshape(row_count, local_width)
    attn_sum = lax.psum(plain_dot(attended, out_weight), "head")
    middle = residual + live_rows * (attn_sum + out_bias)
    second, second_pull = jax.vjp(norm_apply, middle, ffn_gain, ffn_shift)
    second_in = second.astype(jnp.bfloat16)
    inner_pre = plain_dot(second_in, up_weight) + up_bias.astype(jnp.float32)
    activated, gelu_pull = jax.vjp(gelu_exact, inner_pre)
    hidden = activated.astype(jnp.bfloat16)
    ffn_sum = lax.psum(plain_dot(hidden, down_weight).astype(jnp.bfloat16), "head").astype(
        jnp.float32
    )
    output = middle + live_rows * (ffn_sum + down_bias)
    down_cot = (live_rows * cotangent).astype(jnp.bfloat16)
    down_weight_grad = lead_dot(hidden, down_cot)
    down_bias_full = jnp.sum(down_cot.astype(jnp.float32), axis=0)
    inner_grad = gelu_pull(tail_dot(down_cot, down_weight))[0].astype(jnp.bfloat16)
    up_weight_grad = lead_dot(second_in, inner_grad)
    up_bias_grad = jnp.sum(inner_grad.astype(jnp.float32), axis=0)
    second_grad = lax.psum(tail_dot(inner_grad, up_weight), "head")
    middle_part, ffn_gain_full, ffn_shift_full = second_pull(second_grad)
    mid_grad = cotangent + middle_part
    ffn_gain_grad = head_piece(ffn_gain_full, head_rank, head_share)
    ffn_shift_grad = head_piece(ffn_shift_full, head_rank, head_share)
    down_bias_grad = head_piece(down_bias_full, head_rank, head_share)
    attn_cot = (live_rows * mid_grad).astype(jnp.bfloat16)
    out_weight_grad = lead_dot(attended, attn_cot)
    out_bias_full = jnp.sum(attn_cot.astype(jnp.float32), axis=0)
    attended_grad = tail_dot(attn_cot, out_weight).astype(jnp.bfloat16)
    grad_blocks = attended_grad.reshape(blocks, block_rows, local_heads, HEAD_DIM)

    def backward_block(running, pieces):
        key_acc, value_acc = running
        query_part, seg_part, lse_part, grad_part = pieces
        scores = (
            jnp.einsum("qhd,khd->hqk", query_part, key_heads, preferred_element_type=jnp.float32)
            * score_scale
        )
        same_mol = (seg_part[:, None] == key_seg[None, :])[None]
        prob_full = jnp.where(same_mol, jnp.exp(scores - lse_part[..., None]), 0.0)
        prob_low = prob_full.astype(jnp.bfloat16)
        prob_grad = jnp.einsum(
            "qhd,khd->hqk", grad_part, value_heads, preferred_element_type=jnp.float32
        )
        row_delta = jnp.sum(prob_grad * prob_full, axis=-1, keepdims=True)
        score_grad = (prob_full * (prob_grad - row_delta)).astype(jnp.bfloat16)
        query_part_grad = (
            jnp.einsum("hqk,khd->qhd", score_grad, key_heads, preferred_element_type=jnp.float32)
            * score_scale
        )
        key_acc = (
            key_acc
            + jnp.einsum("hqk,qhd->khd", score_grad, query_part, preferred_element_type=jnp.float32)
            * score_scale
        )
        value_acc = value_acc + jnp.einsum(
            "hqk,qhd->khd", prob_low, grad_part, preferred_element_type=jnp.float32
        )
        return ((key_acc, value_acc), query_part_grad.astype(jnp.bfloat16))

    zero_keys = jnp.zeros((key_count, local_heads, HEAD_DIM), jnp.float32)
    (key_acc, value_acc), query_grads = lax.scan(
        backward_block, (zero_keys, zero_keys), (query_blocks, seg_blocks, lse_blocks, grad_blocks)
    )
    key_sum, value_sum = (
        lax.psum_scatter(
            key_acc.reshape(key_count, local_width), "stream", scatter_dimension=0, tiled=True
        ),
        lax.psum_scatter(
            value_acc.reshape(key_count, local_width), "stream", scatter_dimension=0, tiled=True
        ),
    )
    key_grad = key_sum.astype(jnp.bfloat16)
    value_grad = value_sum.astype(jnp.bfloat16)
    query_grad = query_grads.reshape(row_count, local_width)
    query_weight_grad = lead_dot(first_in, query_grad)
    query_bias_grad = jnp.sum(query_grad.astype(jnp.float32), axis=0)
    key_weight_grad = lead_dot(first_in, key_grad)
    value_weight_grad = lead_dot(first_in, value_grad)
    value_bias_grad = jnp.sum(value_grad.astype(jnp.float32), axis=0)
    first_part = (
        tail_dot(query_grad, query_weight)
        + tail_dot(key_grad, key_weight)
        + tail_dot(value_grad, value_weight)
    )
    first_grad = lax.psum(first_part.astype(jnp.bfloat16), "head").astype(jnp.float32)
    resid_part, attn_gain_full, attn_shift_full = norm_pull(first_grad)
    tokens_grad = mid_grad + resid_part
    attn_gain_grad = head_piece(attn_gain_full, head_rank, head_share)
    attn_shift_grad = head_piece(attn_shift_full, head_rank, head_share)
    out_bias_grad = head_piece(out_bias_full, head_rank, head_share)
    (
        attn_gain_grad,
        attn_shift_grad,
        query_weight_grad,
        query_bias_grad,
        key_weight_grad,
        value_weight_grad,
        value_bias_grad,
        out_weight_grad,
        out_bias_grad,
        ffn_gain_grad,
        ffn_shift_grad,
        up_weight_grad,
        up_bias_grad,
        down_weight_grad,
        down_bias_grad,
    ) = lax.psum(
        (
            attn_gain_grad,
            attn_shift_grad,
            query_weight_grad,
            query_bias_grad,
            key_weight_grad,
            value_weight_grad,
            value_bias_grad,
            out_weight_grad,
            out_bias_grad,
            ffn_gain_grad,
            ffn_shift_grad,
            up_weight_grad,
            up_bias_grad,
            down_weight_grad,
            down_bias_grad,
        ),
        ("mol", "stream"),
    )
    return (
        output,
        tokens_grad,
        attn_gain_grad,
        attn_shift_grad,
        query_weight_grad,
        query_bias_grad,
        key_weight_grad,
        value_weight_grad,
        value_bias_grad,
        out_weight_grad,
        out_bias_grad,
        ffn_gain_grad,
        ffn_shift_grad,
        up_weight_grad,
        up_bias_grad,
        down_weight_grad,
        down_bias_grad,
    )


def solution(mesh):
    in_specs = (
        P(("mol", "stream"), None),
        P(("mol", "stream"), None),
        P(),
        P(),
        P(None, "head"),
        P("head"),
        P(None, "head"),
        P(None, "head"),
        P("head"),
        P("head", None),
        P(),
        P(),
        P(),
        P(None, "head"),
        P("head"),
        P("head", None),
        P(),
        P("mol", None),
        P("mol", None),
    )
    out_specs = (
        P(("mol", "stream"), None),
        P(("mol", "stream"), None),
        P("head"),
        P("head"),
        P(None, "head"),
        P("head"),
        P(None, "head"),
        P(None, "head"),
        P("head"),
        P("head", None),
        P("head"),
        P("head"),
        P("head"),
        P(None, "head"),
        P("head"),
        P("head", None),
        P("head"),
    )
    one_chip_pair = (
        mesh.shape["head"] == 2 and mesh.shape["stream"] == 2 and mesh.shape["mol"] == 8
    )
    return jax.shard_map(
        fast_layer if one_chip_pair else on_device, mesh=mesh, in_specs=in_specs, out_specs=out_specs, check_vma=False
    )
```

```python
import functools
import math

import jax
import jax.numpy as jnp
from jax import lax
from jax.experimental import pallas as pl
from jax.experimental.pallas import tpu as pltpu
from jax.sharding import PartitionSpec as P

HEAD_DIM = 24
BF = jnp.bfloat16
F32 = jnp.float32
MESH = pl.DeviceIdType.MESH
EDGES = 512
NODES = 192
TOTAL = EDGES + NODES
PADDED = 768
HEADS_HERE = 8
SCALE = HEAD_DIM ** (-0.5)
SCALE2 = SCALE * math.log2(math.e)
BLOCKS = (
    (0, 256, ((0, 384), (512, 256))),
    (256, 256, ((128, 384), (512, 256))),
    (512, 192, ((0, 768),)),
)
OWNERS = (((0, 0), 512, 192), ((1, 0), 0, 256), ((1, 1), 256, 256))


def nn(a, b):
    return jnp.dot(a, b, preferred_element_type=F32)


def nt(a, b):
    return lax.dot_general(a, b, (((1,), (1,)), ((), ())), preferred_element_type=F32)


def tn(a, b):
    return lax.dot_general(a, b, (((0,), (0,)), ((), ())), preferred_element_type=F32)


def row_loop(count, step, fn, init):
    def body(i, carry):
        return fn(pl.ds(pl.multiple_of(i * step, step), step), carry)

    return lax.fori_loop(0, count // step, body, init)


def normed(x):
    mu = jnp.mean(x, axis=-1, keepdims=True)
    xc = x - mu
    var = jnp.mean(xc * xc, axis=-1, keepdims=True)
    r = lax.rsqrt(var + 1e-05)
    return xc * r, r


def col_sum(x):
    return jnp.sum(x, axis=0, keepdims=True)


SEM = {}


def sem_id(name, count=1):
    if name not in SEM:
        SEM[name] = sum(n for _, n in SEM.values()), count
    return SEM[name][0]


N_SEMS = 160
N_LOCAL = 24


def layer_kernel(
    tokens, cot, wq, wk, wv, wo, wu, wd,
    atoms, edges,
    a_gain_v, a_shift_v, q_bias_v, v_bias_v, o_bias_v, f_gain_v, f_shift_v, u_bias_v, d_bias_v,
    d_out, d_tok, f1, f2, vec,
    dov, dtv, fz1, fz2, dxp, tok, res, cotv, ww, fwo, fwu, fwd, ub, fin1, qkv, dxw, qm, dam,
    p0, p1, p2, bias, segc, attf, att, ain, da, delta,
    t0, t1, n2s, r2s, mid, sec, hid, dc, ig, ac, ato, ago, mgd,
    ds, dkf, dvf,
    g1, gs1, xr, gx, yr, gq, zr1, g2, gs2, zr2, fp, fx, fs, fy,
    vq, vz, vc,
    ss, rs, ls,
):
    m, s, h = lax.axis_index("mol"), lax.axis_index("stream"), lax.axis_index("head")
    z, c = m // 2, lax.rem(m, 2)
    zc = lax.axis_size("mol") // 2
    me = 2 * s + h
    x_peer, y_peer, xy_peer = (m, s, 1 - h), (m, 1 - s, h), (m, 1 - s, 1 - h)
    quad = (x_peer, y_peer, xy_peer)
    twin = (2 * z + 1 - c, s, h)
    z_peers = [(2 * lax.rem(z + d, zc) + c, s, h) for d in range(1, zc)]

    def remote(name, src, dst, dev, k=0, count=1):
        i = sem_id(name, count) + k
        return pltpu.make_async_remote_copy(
            src_ref=src, dst_ref=dst, send_sem=ss.at[i], recv_sem=rs.at[i],
            device_id=dev, device_id_type=MESH,
        )

    def as_row(ref):
        return ref[...].astype(F32).reshape(1, -1)

    a_gain, a_shift, f_gain, f_shift = (as_row(r) for r in (a_gain_v, a_shift_v, f_gain_v, f_shift_v))
    o_bias, d_bias, q_bias, v_bias = (as_row(r) for r in (o_bias_v, d_bias_v, q_bias_v, v_bias_v))

    def local(k, src, dst):
        return pltpu.make_async_copy(src, dst, ls.at[k])

    own = pl.multiple_of(256 * h, 256)
    other = pl.multiple_of(256 * (1 - h), 256)
    window = pl.multiple_of(128 * s, 128)

    loads = [
        local(0, tokens.at[pl.ds(own, 256)], res),
        local(1, cot.at[pl.ds(own, 256)], cotv),
        local(2, wq.at[:, pl.ds(window, 256)], ww.at[:, 0:256]),
        local(3, wk.at[:, pl.ds(window, 256)], ww.at[:, 256:512]),
        local(4, wv.at[:, pl.ds(window, 256)], ww.at[:, 512:768]),
        local(5, wo, fwo.at[h]),
        local(6, wu, fwu.at[h]),
        local(7, wd, fwd.at[h]),
    ]
    edge_load = local(8, tokens, tok.at[0:EDGES])
    node_load = local(9, tokens.at[0:NODES], tok.at[EDGES:TOTAL])
    pl.when(s == 1)(edge_load.start)
    pl.when(s == 0)(node_load.start)
    for copy in loads:
        copy.start()
    ub[h] = jnp.broadcast_to(as_row(u_bias_v), (8, 384))

    barrier = pltpu.get_barrier_semaphore()
    greeted = [*quad, twin, *z_peers]
    for dev in greeted:
        pl.semaphore_signal(barrier, inc=1, device_id=dev, device_id_type=MESH)
    pl.semaphore_wait(barrier, len(greeted))

    def edge_part(k, half):
        rows = pl.ds(pl.multiple_of(256 * half + 64 * k, 64), 64)
        return rows

    tok_y = [
        remote("tok_y", tokens.at[edge_part(k, h)], tok.at[edge_part(k, h)], y_peer, k, 4)
        for k in range(4)
    ]
    tok_x = [
        remote("tok_x", tok.at[edge_part(k, h)], tok.at[edge_part(k, h)], x_peer, k, 4)
        for k in range(4)
    ]
    tok_x_in = [
        remote("tok_x", tok.at[edge_part(k, 1 - h)], tok.at[edge_part(k, 1 - h)], x_peer, k, 4)
        for k in range(4)
    ]
    tok_n = remote("tok_n", tokens.at[0:NODES], tok.at[EDGES:TOTAL], y_peer)

    @pl.when(s == 1)
    def _():
        for copy in tok_y:
            copy.start()

    pl.when(s == 0)(tok_n.start)
    u_send = remote("ub", ub.at[h], ub.at[h], x_peer)
    u_send.start()
    part_o = pl.ds(pl.multiple_of(192 * c, 192), 192)
    part_u = pl.ds(pl.multiple_of(384 * c, 384), 384)
    w_out = [
        remote("wo_x", wo.at[part_o], fwo.at[h, part_o], x_peer),
        remote("wu_x", wu.at[part_u], fwu.at[h, part_u], x_peer),
        remote("wd_x", wd.at[part_o], fwd.at[h, part_o], x_peer),
    ]

    @pl.when(s == 1)
    def _():
        for k in (2, 0, 1):
            w_out[k].start()

    w_in = [
        remote("wo_x", wo.at[part_o], fwo.at[1 - h, part_o], x_peer),
        remote("wu_x", wu.at[part_u], fwu.at[1 - h, part_u], x_peer),
        remote("wd_x", wd.at[part_o], fwd.at[1 - h, part_o], x_peer),
    ]
    w_twin = [
        remote("wo_c", fwo.at[1 - h, part_o], fwo.at[1 - h, part_o], twin),
        remote("wu_c", fwu.at[1 - h, part_u], fwu.at[1 - h, part_u], twin),
        remote("wd_c", fwd.at[1 - h, part_o], fwd.at[1 - h, part_o], twin),
    ]

    wd_y = remote("wd_y", fwd.at[1 - h, part_o], fwd.at[1 - h, part_o], y_peer)

    def share_weight(k):
        w_in[k].wait_recv()
        w_twin[k].start()

    def share_down():
        pl.when(s == 0)(wd_y.wait_recv)
        w_twin[2].start()

    def ends_of(counts, added):
        total, ends = 0, []
        for j in range(counts.shape[1]):
            total = total + counts[0, j] + added
            ends.append(total)
        return ends

    node_ends, edge_ends = ends_of(atoms, 1), ends_of(edges, 0)
    live_count = jnp.where(s == 0, node_ends[-1], edge_ends[-1])

    def seg_of(position, ends):
        seg = jnp.zeros_like(position)
        for end in ends:
            seg = seg + jnp.where(position >= end, 1, 0)
        return seg

    segc[0:EDGES] = seg_of(lax.broadcasted_iota(jnp.int32, (EDGES, 1), 0), edge_ends)
    segc[EDGES:TOTAL] = seg_of(lax.broadcasted_iota(jnp.int32, (NODES, 1), 0), node_ends)
    at_row = lax.broadcasted_iota(jnp.int32, (1, PADDED), 1)
    seg_r = jnp.where(at_row < EDGES, seg_of(at_row, edge_ends), seg_of(at_row - EDGES, node_ends))
    seg_r = jnp.where(at_row < TOTAL, seg_r, -1)

    lane = lax.broadcasted_iota(jnp.int32, (1, 256), 1) - 64 * s
    head_of = jnp.where((lane >= 0) & (lane < 192), lane // HEAD_DIM, -1)
    zero = jnp.zeros((), BF)

    qkv[TOTAL:PADDED] = jnp.zeros((PADDED - TOTAL, 768), BF)
    bias_row = jnp.concatenate(
        [
            jnp.where(s == 0, q_bias[:, 0:256], q_bias[:, 128:384]),
            jnp.zeros((1, 256), F32),
            jnp.where(s == 0, v_bias[:, 0:256], v_bias[:, 128:384]),
        ],
        axis=1,
    )

    def project(first, count):
        def norm_rows(i, carry):
            rows = pl.ds(pl.multiple_of(first + i * 64, 64), 64)
            n1, _ = normed(tok[rows].astype(F32))
            fin1[rows] = (n1 * a_gain + a_shift).astype(BF)
            return carry

        lax.fori_loop(0, count // 64, norm_rows, 0)
        rows = pl.ds(pl.multiple_of(first, 64), count)
        qkv[rows] = (nn(fin1[rows], ww[...]) + bias_row).astype(BF)

    for copy in loads[2:5]:
        copy.wait()

    @pl.when(s == 1)
    def _():
        edge_load.wait()
        project(0, EDGES)
        tok_n.wait_recv()
        project(EDGES, NODES)
        w_in[2].wait_recv()
        wd_y.start()

    @pl.when(s == 0)
    def _():
        node_load.wait()
        project(EDGES, NODES)
        for k in range(4):
            tok_y[k].wait_recv()
            tok_x[k].start()
        w_out[0].start()
        w_out[1].start()
        project(own, 256)
        for k in range(4):
            tok_x_in[k].wait_recv()
        project(other, 256)

    for j in range(HEADS_HERE):
        qm[j] = jnp.where(head_of == j, qkv[0:TOTAL, 0:256], zero)

    def send_rows(name, src, dst, k):
        dev_sh, first, count = OWNERS[k]
        target = (m, *dev_sh)
        mine = 2 * dev_sh[0] + dev_sh[1]

        @pl.when(me != mine)
        def _():
            i = sem_id(name + "_s", 3) + k
            j = sem_id(name, 4) + me
            pltpu.make_async_remote_copy(
                src_ref=src.at[first:first + count], dst_ref=dst.at[me, 0:count],
                send_sem=ss.at[i], recv_sem=rs.at[j], device_id=target, device_id_type=MESH,
            ).start()

        @pl.when(me == mine)
        def _():
            dst[mine, 0:count] = src[first:first + count]

    def wait_rows(name, src, dst):
        for k, (dev_sh, first, count) in enumerate(OWNERS):
            mine = 2 * dev_sh[0] + dev_sh[1]

            @pl.when(me == mine)
            def _():
                for r in range(4):
                    if r != mine:
                        j = sem_id(name, 4) + r
                        pltpu.make_async_remote_copy(
                            src_ref=src.at[first:first + count], dst_ref=dst.at[r, 0:count],
                            send_sem=ss.at[j], recv_sem=rs.at[j], device_id=x_peer, device_id_type=MESH,
                        ).wait_recv()

    def wait_sent(name, src, dst):
        for k, (dev_sh, first, count) in enumerate(OWNERS):
            mine = 2 * dev_sh[0] + dev_sh[1]

            @pl.when(me != mine)
            def _():
                i = sem_id(name + "_s", 3) + k
                pltpu.make_async_remote_copy(
                    src_ref=src.at[first:first + count], dst_ref=dst.at[me, 0:count],
                    send_sem=ss.at[i], recv_sem=rs.at[i], device_id=(m, *dev_sh), device_id_type=MESH,
                ).wait_send()

    def pick_heads(stacked, rows):
        total = None
        for j in range(HEADS_HERE):
            part = jnp.where(head_of == j, stacked[j * rows:(j + 1) * rows], 0.0)
            total = part if total is None else total + part
        return total

    probs = (p0, p1, p2)
    to_owner = (1, 2, 0)
    group = 2

    @pl.when(s == 0)
    def _():
        ain[:, NODES:256] = jnp.zeros((4, 256 - NODES, 256), BF)

    @pl.when((s == 0) & (h == 1))
    def _():
        ain[:, 0:NODES] = jnp.zeros((4, NODES, 256), BF)

    for b, (q0, qn, segs) in enumerate(BLOCKS):
        o = 0
        for a, n in segs:
            bias[0:qn, o:o + n] = jnp.where(segc[q0:q0 + qn] == seg_r[:, a:a + n], 0.0, -1e30)
            o += n
        for j0 in range(0, HEADS_HERE, group):
            qb = qm[j0:j0 + group, q0:q0 + qn, :].reshape(group * qn, 256)
            raw = [nt(qb, qkv[a:a + n, 256:512]) for a, n in segs]
            for g in range(group):
                j, o, parts = j0 + g, 0, []
                for piece, (a, n) in zip(raw, segs):
                    parts.append(piece[g * qn:(g + 1) * qn] * SCALE2 + bias[0:qn, o:o + n])
                    o += n
                top = functools.reduce(
                    jnp.maximum, [jnp.max(x, axis=1, keepdims=True) for x in parts]
                )
                parts = [jnp.exp2(x - top) for x in parts]
                inv = 1.0 / sum(jnp.sum(x, axis=1, keepdims=True) for x in parts)
                o = 0
                for x, (a, n) in zip(parts, segs):
                    probs[b][j * qn:(j + 1) * qn, o:o + n] = (x * inv).astype(BF)
                    o += n
        o, acc = 0, None
        for a, n in segs:
            part = nn(probs[b][:, o:o + n], qkv[a:a + n, 512:768])
            acc = part if acc is None else acc + part
            o += n
        picked = pick_heads(acc, qn)
        attf[q0:q0 + qn] = picked
        att[q0:q0 + qn] = picked.astype(BF)
        send_rows("att", att, ain, to_owner[b])

    share_weight(0)
    share_down()

    for copy in (loads[0], loads[1], *loads[5:8]):
        copy.wait()
    row_at = lax.broadcasted_iota(jnp.int32, (256, 1), 0) + own
    live_all = jnp.where(row_at < live_count, 1.0, 0.0)
    r2s[:, 1:2] = live_all
    wait_rows("att", att, ain)
    for x in range(2):
        ato[:, 384 * x:384 * x + 128] = ain[x, :, 0:128]
        ato[:, 384 * x + 128:384 * x + 256] = ain[x, :, 128:256] + ain[2 + x, :, 0:128]
        ato[:, 384 * x + 256:384 * x + 384] = ain[2 + x, :, 128:256]
    twin_o = pl.ds(pl.multiple_of(192 * (1 - c), 192), 192)
    twin_u = pl.ds(pl.multiple_of(384 * (1 - c), 384), 384)
    w_twin_in = [
        remote("wo_c", fwo.at[1 - h, twin_o], fwo.at[1 - h, twin_o], twin),
        remote("wu_c", fwu.at[1 - h, twin_u], fwu.at[1 - h, twin_u], twin),
        remote("wd_c", fwd.at[1 - h, twin_o], fwd.at[1 - h, twin_o], twin),
    ]
    w_twin_in[0].wait_recv()
    wo_all = fwo[...].reshape(768, 768)
    t0[...] = nn(ato[...], wo_all)
    share_weight(1)
    live_of = lambda rows: r2s[rows, 1:2]

    def middle_rows(rows, carry):
        x = res[rows].astype(F32) + live_of(rows) * (t0[rows] + o_bias)
        mid[rows] = x
        n2, r2 = normed(x)
        n2s[rows] = n2
        r2s[rows, 0:1] = r2
        sec[rows] = (n2 * f_gain + f_shift).astype(BF)
        return carry

    row_loop(256, 64, middle_rows, 0)
    w_twin_in[1].wait_recv()
    u_recv = remote("ub", ub.at[1 - h], ub.at[1 - h], x_peer)
    u_recv.wait_recv()
    for x in range(2):
        t0[:, 384 * x:384 * (x + 1)] = nn(sec[...], fwu[x]) + ub[x, 0:1]

    def gelu_rows(rows, carry):
        u = t0[rows]
        cdf = 0.5 * (1.0 + lax.erf(u * math.sqrt(0.5)))
        hid[rows] = (u * cdf).astype(BF)
        t1[rows] = cdf + u * (jnp.exp(-0.5 * u * u) * (1.0 / math.sqrt(2.0 * math.pi)))
        return carry

    row_loop(256, 64, gelu_rows, 0)
    w_twin_in[2].wait_recv()
    wd_all = fwd[...].reshape(768, 768)
    t0[...] = nn(hid[...], wd_all)
    zero_row = jnp.zeros((1, 768), F32)

    def out_rows(rows, carry):
        live = live_of(rows)
        x = (mid[rows] + live * (t0[rows] + d_bias)) - res[rows].astype(F32)
        dov[rows] = x.astype(BF)
        down = (live * cotv[rows]).astype(BF)
        dc[rows] = down
        return carry + col_sum(down.astype(F32))

    down_bias_sum = row_loop(256, 64, out_rows, zero_row)
    own_rows = pl.ds(own, 256)
    other_rows = pl.ds(other, 256)
    out_send = remote("out", dov, d_out.at[own_rows], x_peer)
    out_send.start()
    stores = [local(10, dov, d_out.at[own_rows])]
    stores[0].start()
    t0[...] = nt(dc[...], wd_all)

    def inner_rows(rows, carry):
        x = (t0[rows] * t1[rows]).astype(BF)
        ig[rows] = x
        return carry + col_sum(x.astype(F32))

    up_bias_sum = row_loop(256, 64, inner_rows, zero_row)
    t0[...] = nt(ig[:, 0:384], fwu[0]) + nt(ig[:, 384:768], fwu[1])

    def second_rows(rows, carry):
        gain_sum, shift_sum, bias_sum = carry
        sg, n2 = t0[rows], n2s[rows]
        g = sg * f_gain
        back = r2s[rows, 0:1] * (
            g - jnp.mean(g, axis=-1, keepdims=True) - n2 * jnp.mean(g * n2, axis=-1, keepdims=True)
        )
        mgd[rows] = back
        x = (live_of(rows) * (cotv[rows] + back)).astype(BF)
        ac[rows] = x
        return gain_sum + col_sum(sg * n2), shift_sum + col_sum(sg), bias_sum + col_sum(x.astype(F32))

    f_gain_sum, f_shift_sum, out_bias_sum = row_loop(
        256, 64, second_rows, (zero_row, zero_row, zero_row)
    )
    ago[...] = nt(ac[...], wo_all).astype(BF)

    for k, (dev_sh, first, count) in enumerate(OWNERS):
        mine = 2 * dev_sh[0] + dev_sh[1]

        @pl.when(me == mine)
        def _():
            for r in range(4):
                cols = slice(384 * (r % 2) + 128 * (r // 2), 384 * (r % 2) + 128 * (r // 2) + 256)
                if r == mine:
                    da[first:first + count] = ago[0:count, cols]
                else:
                    i, j = sem_id("da_s", 4) + r, sem_id("da", 3) + k
                    pltpu.make_async_remote_copy(
                        src_ref=ago.at[0:count, cols], dst_ref=da.at[first:first + count],
                        send_sem=ss.at[i], recv_sem=rs.at[j],
                        device_id=(m, r // 2, r % 2), device_id_type=MESH,
                    ).start()

    cut = [slice(0, 384), slice(384, 768)]
    for cc in range(2):
        for xh in range(2):
            g1[0, cc, xh] = tn(hid[:, cut[xh]], dc[:, cut[cc]]).astype(BF)
    g1_twin = [remote("g1_c", g1.at[p, 1 - c], gs1.at[p], twin, p, 3) for p in range(3)]
    g1_twin[0].start()
    for cc in range(2):
        for xh in range(2):
            g1[1, cc, xh] = tn(sec[:, cut[cc]], ig[:, cut[xh]]).astype(BF)
    g1_twin[1].start()
    for cc in range(2):
        for xh in range(2):
            g1[2, cc, xh] = tn(ato[:, cut[xh]], ac[:, cut[cc]]).astype(BF)
    g1_twin[2].start()
    g1_x = [remote("g1_x", gs1.at[p, 1 - h], xr.at[p], x_peer, p, 3) for p in range(3)]
    rows_y = pl.ds(pl.multiple_of(192 * (1 - s), 192), 192)
    rows_s = pl.ds(pl.multiple_of(192 * s, 192), 192)
    g1_y = [remote("g1_y", gx.at[p, rows_y], yr.at[p], y_peer, p, 3) for p in range(3)]
    zn1, zn2 = 192 // zc, 384 // zc

    def chunk(t, n):
        return pl.ds(pl.multiple_of(n * t, n), n)

    g1_z = [
        [
            remote("g1_z", gq.at[p, chunk(lax.rem(z + d, zc), zn1)], zr1.at[p, d - 1], z_peers[d - 1],
                   p * (zc - 1) + d - 1, 3 * (zc - 1))
            for d in range(1, zc)
        ]
        for p in range(3)
    ]

    def add_into(dst, *terms):
        x = terms[0].astype(F32)
        for t in terms[1:]:
            x = x + t.astype(F32)
        dst[...] = x.astype(BF)

    def g1_after_twin(p):
        g1_twin[p].wait_recv()
        for xh in range(2):
            add_into(gs1.at[p, xh], g1[p, c, xh], gs1[p, xh])
        g1_x[p].start()

    def g1_after_x(p):
        g1_x[p].wait_recv()
        add_into(gx.at[p], gs1[p, h], xr[p])
        g1_y[p].start()

    def g1_after_y(p):
        g1_y[p].wait_recv()
        add_into(gq.at[p], gx[p, rows_s], yr[p])
        for copy in g1_z[p]:
            copy.start()

    for p in range(3):
        g1_after_twin(p)

    for k, (dev_sh, first, count) in enumerate(OWNERS):
        mine = 2 * dev_sh[0] + dev_sh[1]

        @pl.when(me != mine)
        def _():
            j = sem_id("da", 3) + k
            pltpu.make_async_remote_copy(
                src_ref=ago.at[0:count, 0:256], dst_ref=da.at[first:first + count],
                send_sem=ss.at[j], recv_sem=rs.at[j], device_id=x_peer, device_id_type=MESH,
            ).wait_recv()

    head_col = lax.broadcasted_iota(jnp.int32, (256, 128), 1)
    lane_row = lax.broadcasted_iota(jnp.int32, (256, 128), 0) - 64 * s
    head_pick = jnp.where(
        (lane_row >= 0) & (lane_row < 192) & (lane_row // HEAD_DIM == head_col), 1.0, 0.0
    ).astype(BF)
    prod = da[0:TOTAL].astype(F32) * attf[...]
    prod_hi = prod.astype(BF)
    delta[...] = nn(prod_hi, head_pick) + nn((prod - prod_hi.astype(F32)).astype(BF), head_pick)
    for j in range(HEADS_HERE):
        dam[j] = jnp.where(head_of == j, da[0:TOTAL], zero)
    dkf[...] = jnp.zeros_like(dkf)
    dvf[...] = jnp.zeros_like(dvf)
    for b, (q0, qn, segs) in enumerate(BLOCKS):
        pr = probs[b]
        for j0 in range(0, HEADS_HERE, group):
            ab = dam[j0:j0 + group, q0:q0 + qn, :].reshape(group * qn, 256)
            o = 0
            for a, n in segs:
                pg = nt(ab, qkv[a:a + n, 512:768])
                for g in range(group):
                    j = j0 + g
                    r = slice(j * qn, (j + 1) * qn)
                    ds[r, o:o + n] = (
                        pr[r, o:o + n].astype(F32)
                        * (pg[g * qn:(g + 1) * qn] - delta[q0:q0 + qn, j:j + 1])
                    ).astype(BF)
                o += n
        o, acc = 0, None
        for a, n in segs:
            part = nn(ds[0:HEADS_HERE * qn, o:o + n], qkv[a:a + n, 256:512])
            acc = part if acc is None else acc + part
            o += n
        dxw[q0:q0 + qn, 0:256] = (pick_heads(acc, qn) * SCALE).astype(BF)
        o = 0
        for a, n in segs:
            dk = dv = None
            for j in range(HEADS_HERE):
                r = slice(j * qn, (j + 1) * qn)
                pk = tn(ds[r, o:o + n], qm[j, q0:q0 + qn])
                pv = tn(pr[r, o:o + n], dam[j, q0:q0 + qn])
                dk = pk if dk is None else dk + pk
                dv = pv if dv is None else dv + pv
            dkf[a:a + n] += dk
            dvf[a:a + n] += dv
            o += n
        if b < 2:
            g1_after_x(b)
    dxw[:, 256:512] = (dkf[0:TOTAL] * SCALE).astype(BF)
    dxw[:, 512:768] = dvf[0:TOTAL].astype(BF)

    fp_x = [
        remote("fp_x", fp.at[chunk(2 * (1 - h) + k, 128)], fx.at[chunk(k, 128)], x_peer, k, 3)
        for k in range(2)
    ]
    fp_xn = remote("fp_x", fp.at[EDGES:TOTAL], fx.at[256:256 + NODES], x_peer, 2, 3)
    fp_y = [
        remote("fp_y", fs.at[chunk(k, 128)], fy.at[chunk(k, 128)], y_peer, k, 2) for k in range(2)
    ]
    fp_yn = [
        remote("fp_yn", fs.at[256 + 96 * k:256 + 96 * (k + 1)], fy.at[96 * k:96 * (k + 1)], y_peer, k, 2)
        for k in range(2)
    ]
    for k in range(2):
        rows = chunk(2 * (1 - h) + k, 128)
        fp[rows] = nt(dxw[rows], ww[...]).astype(BF)
        fp_x[k].start()
    fp[EDGES:TOTAL] = nt(dxw[EDGES:TOTAL], ww[...]).astype(BF)
    pl.when(h == 1)(fp_xn.start)
    fp[pl.ds(own, 256)] = nt(dxw[pl.ds(own, 256)], ww[...]).astype(BF)
    g1_after_y(0)

    at_lane = lax.broadcasted_iota(jnp.int32, (1, 128), 1)
    full, half = [], []
    for k in range(3):
        first = dxw[:, 256 * k:256 * k + 128]
        last = dxw[:, 256 * k + 128:256 * k + 256]
        full.append(jnp.where(s == 0, first, last))
        half.append(jnp.where(s == 0, last, first))
    dxp[:, 0:128], dxp[:, 128:256], dxp[:, 256:384] = full
    rolled = pltpu.roll(half[1].astype(F32), 64, 1)
    dxp[:, 384:512] = (half[0].astype(F32) + rolled).astype(BF)
    dxp[:, 512:640] = half[2]
    lanes2 = [slice(0, 256), slice(256, 512), slice(512, 640)]
    g2_twin = [
        remote("g2_c", g2.at[1 - c, :, lanes2[p]], gs2.at[:, lanes2[p]], twin, p, 3) for p in range(3)
    ]
    g2_z = [
        [
            remote("g2_z", gs2.at[chunk(lax.rem(z + d, zc), zn2), lanes2[p]], zr2.at[d - 1, :, lanes2[p]],
                   z_peers[d - 1], p * (zc - 1) + d - 1, 3 * (zc - 1))
            for d in range(1, zc)
        ]
        for p in range(3)
    ]

    def g2_compute(p):
        for cc in range(2):
            g2[cc, :, lanes2[p]] = tn(fin1[0:TOTAL, cut[cc]], dxp[:, lanes2[p]]).astype(BF)
        g2_twin[p].start()

    def g2_after_twin(p):
        g2_twin[p].wait_recv()
        add_into(gs2.at[:, lanes2[p]], g2[c, :, lanes2[p]], gs2[:, lanes2[p]])
        for copy in g2_z[p]:
            copy.start()

    def fp_after_x(k):
        fp_x[k].wait_recv()
        add_into(fs.at[chunk(k, 128)], fp[chunk(2 * h + k, 128)], fx[chunk(k, 128)])
        pl.when(s == 0)(fp_y[k].start)

    g2_compute(0)
    fp_after_x(0)
    g2_compute(1)
    g2_after_twin(0)
    fp_after_x(1)
    g2_compute(2)
    g2_after_twin(1)
    g2_after_twin(2)

    @pl.when(h == 0)
    def _():
        fp_xn.wait_recv()
        add_into(fs.at[256:256 + NODES], fp[EDGES:TOTAL], fx[256:256 + NODES])

        @pl.when(s == 1)
        def _():
            for copy in fp_yn:
                copy.start()

    g1_after_y(1)
    g1_after_x(2)
    qkv_bias_sum = col_sum(dxw[...].astype(F32))

    def first_rows(rows, fg):
        n1, r1 = normed(res[rows].astype(F32))
        g = fg * a_gain
        back = r1 * (
            g - jnp.mean(g, axis=-1, keepdims=True) - n1 * jnp.mean(g * n1, axis=-1, keepdims=True)
        )
        dtv[rows] = (mgd[rows] + back).astype(BF)
        return jnp.concatenate([col_sum(fg * n1), col_sum(fg)], axis=0)

    def own_chunk(k, n):
        return pl.ds(pl.multiple_of(own + n * k, n), n)

    dt_e = [
        remote("dt", dtv.at[128 * k:128 * (k + 1)], d_tok.at[own_chunk(k, 128)], x_peer, k, 2)
        for k in range(2)
    ]
    vz[0, 0:8] = jnp.zeros((8, 768), F32)

    @pl.when(s == 1)
    def _():
        for k in range(2):
            fp_y[k].wait_recv()

            def edge_rows(i, carry):
                rows = pl.ds(pl.multiple_of(128 * k + 64 * i, 64), 64)
                return carry + first_rows(rows, fs[rows].astype(F32) + fy[rows].astype(F32))

            got = lax.fori_loop(0, 2, edge_rows, jnp.zeros((2, 768), F32))
            vz[0, 0:2] += got
            dt_e[k].start()

    @pl.when((s == 0) & (h == 0))
    def _():
        for k in range(2):
            fp_yn[k].wait_recv()

            def node_rows(i, carry):
                rows = pl.ds(pl.multiple_of(96 * k + 32 * i, 32), 32)
                from_fs = pl.ds(pl.multiple_of(256 + 96 * k + 32 * i, 32), 32)
                return carry + first_rows(rows, fs[from_fs].astype(F32) + fy[rows].astype(F32))

            got = lax.fori_loop(0, 3, node_rows, jnp.zeros((2, 768), F32))
            vz[0, 0:2] += got
        dtv[NODES:256] = mgd[NODES:256].astype(BF)
        for k in range(2):
            dt_e[k].start()

    @pl.when((s == 0) & (h == 1))
    def _():
        dtv[...] = mgd[...].astype(BF)
        for k in range(2):
            dt_e[k].start()

    stores.append(local(11, dtv, d_tok.at[own_rows]))
    stores[1].start()

    sums = [f_gain_sum, f_shift_sum, out_bias_sum, down_bias_sum, up_bias_sum, vz[0, 0:1], vz[0, 1:2], zero_row]
    sums += [jnp.where(me == r, qkv_bias_sum, 0.0) for r in range(4)] + [zero_row] * 4
    vq[me] = jnp.concatenate(sums, axis=0)
    v1 = [remote("v_q", vq.at[me], vq.at[me], dev, k, 3) for k, dev in enumerate(quad)]
    for copy in v1:
        copy.start()

    f1_z, f1_y, f1_c, f2_z, f2_y, f2_c = [], [], [], [], [], []

    def f1_at(p, cc, ss_, zz):
        return f1.at[p, cc, pl.ds(pl.multiple_of(192 * ss_ + zn1 * zz, 16), zn1)]

    def f1_half(p, ss_):
        return f1.at[p, c, pl.ds(pl.multiple_of(192 * ss_, 192), 192)]

    def f2_at(p, cc, ss_, zz):
        return f2.at[ss_, pl.ds(pl.multiple_of(384 * cc + zn2 * zz, 16), zn2), lanes2[p]]

    def f2_half(p, ss_):
        return f2.at[ss_, pl.ds(pl.multiple_of(384 * c, 384), 384), lanes2[p]]

    def g1_after_z(p):
        for copy in g1_z[p]:
            copy.wait_recv()
        add_into(fz1.at[p], gq[p, chunk(z, zn1)], *[zr1[p, d] for d in range(zc - 1)])
        f1_z.append([
            remote("f1_z", fz1.at[p], f1_at(p, c, s, z), z_peers[d], p * (zc - 1) + d, 3 * (zc - 1))
            for d in range(zc - 1)
        ])
        for copy in f1_z[p]:
            copy.start()
        stores.append(local(12 + p, fz1.at[p], f1_at(p, c, s, z)))
        stores[-1].start()
        return stores[-1]

    def f1_after_z(p, store):
        for copy in f1_z[p]:
            copy.wait_recv()
        store.wait()
        f1_y.append(remote("f1_y", f1_half(p, s), f1_half(p, s), y_peer, p, 3))
        f1_c.append(remote("f1_c", f1_half(p, s), f1_half(p, s), twin, 2 * p, 6))
        f1_y[p].start()
        f1_c[-1].start()

    def f1_after_y(p):
        f1_y[p].wait_recv()
        f1_c.append(remote("f1_c", f1_half(p, 1 - s), f1_half(p, 1 - s), twin, 2 * p + 1, 6))
        f1_c[-1].start()

    def g2_after_z(p):
        for copy in g2_z[p]:
            copy.wait_recv()
        add_into(
            fz2.at[:, lanes2[p]], gs2[chunk(z, zn2), lanes2[p]], *[zr2[d, :, lanes2[p]] for d in range(zc - 1)]
        )
        f2_z.append([
            remote("f2_z", fz2.at[:, lanes2[p]], f2_at(p, c, s, z), z_peers[d], p * (zc - 1) + d, 3 * (zc - 1))
            for d in range(zc - 1)
        ])
        for copy in f2_z[p]:
            copy.start()
        stores.append(local(15 + p, fz2.at[:, lanes2[p]], f2_at(p, c, s, z)))
        stores[-1].start()
        return stores[-1]

    def f2_after_z(p, store):
        for copy in f2_z[p]:
            copy.wait_recv()
        store.wait()
        f2_y.append(remote("f2_y", f2_half(p, s), f2_half(p, s), y_peer, p, 3))
        f2_c.append(remote("f2_c", f2_half(p, s), f2_half(p, s), twin, 2 * p, 6))
        f2_y[p].start()
        f2_c[-1].start()

    def f2_after_y(p):
        f2_y[p].wait_recv()
        f2_c.append(remote("f2_c", f2_half(p, 1 - s), f2_half(p, 1 - s), twin, 2 * p + 1, 6))
        f2_c[-1].start()

    st1, st2 = [None] * 3, [None] * 3
    g1_after_y(2)
    st1[0] = g1_after_z(0)
    st2[0] = g2_after_z(0)
    st1[1] = g1_after_z(1)
    st2[1] = g2_after_z(1)
    st2[2] = g2_after_z(2)
    f1_after_z(0, st1[0])
    f2_after_z(0, st2[0])
    st1[2] = g1_after_z(2)
    v1_in = [
        remote("v_q", vq.at[r], vq.at[r], dev, k, 3)
        for k, (dev, r) in enumerate(zip(quad, (2 * s + 1 - h, 2 - 2 * s + h, 3 - 2 * s - h)))
    ]
    for copy in v1_in:
        copy.wait_recv()
    vz[z] = vq[0] + vq[1] + vq[2] + vq[3]
    v2 = [remote("v_z", vz.at[z], vz.at[z], z_peers[d], d, zc - 1) for d in range(zc - 1)]
    for copy in v2:
        copy.start()
    f1_after_z(1, st1[1])
    f2_after_z(1, st2[1])
    f2_after_z(2, st2[2])
    f1_after_y(0)
    f2_after_y(0)
    for copy in v2:
        copy.wait_recv()
    vsum = vz[0]
    for d in range(1, zc):
        vsum = vsum + vz[d]
    vc[c] = vsum
    v3 = remote("v_c", vc.at[c], vc.at[c], twin)
    v3.start()
    f1_after_z(2, st1[2])
    f1_after_y(1)
    f2_after_y(1)
    f2_after_y(2)
    f1_after_y(2)
    v3.wait_recv()
    vec[...] = vc[0] + vc[1]
    for copy in (*f1_c, *f2_c, *dt_e, out_send):
        copy.wait_recv()
    for copy in stores[0:2]:
        copy.wait()

    @pl.when(s == 1)
    def _():
        for copy in tok_y:
            copy.wait_send()

    @pl.when(s == 0)
    def _():
        tok_n.wait_send()
        for copy in tok_x:
            copy.wait_send()

    wait_sent("att", att, ain)

    @pl.when(s == 0)
    def _():
        for copy in fp_y:
            copy.wait_send()

    pl.when(h == 1)(fp_xn.wait_send)

    @pl.when((s == 1) & (h == 0))
    def _():
        for copy in fp_yn:
            copy.wait_send()

    @pl.when(s == 1)
    def _():
        w_out[2].wait_send()
        wd_y.wait_send()

    for k, (dev_sh, first, count) in enumerate(OWNERS):
        mine = 2 * dev_sh[0] + dev_sh[1]

        @pl.when(me == mine)
        def _():
            for r in range(4):
                if r != mine:
                    i = sem_id("da_s", 4) + r
                    pltpu.make_async_remote_copy(
                        src_ref=ago.at[0:count, 0:256], dst_ref=da.at[first:first + count],
                        send_sem=ss.at[i], recv_sem=rs.at[i], device_id=x_peer, device_id_type=MESH,
                    ).wait_send()

    for copy in (
        u_send, *w_out[0:2], *w_twin, out_send, *g1_twin, *g1_x, *g1_y, *sum(g1_z, []), *fp_x, *g2_twin,
        *sum(g2_z, []), *dt_e, *v1, *sum(f1_z, []), *f1_y, *f1_c, *sum(f2_z, []), *f2_y, *f2_c, *v2, v3,
    ):
        copy.wait_send()


def finish_kernel(
    tokens, cot, d_out, d_tok, f1, f2, vec,
    output, tokens_grad, a_gain, a_shift, wq, bq, wk, wv, bv, wo, bo, f_gain, f_shift, wu, bu, wd, bd,
):
    h = lax.axis_index("head")
    output[...] = tokens[...].astype(F32) + d_out[...].astype(F32)
    tokens_grad[...] = cot[...] + d_tok[...].astype(F32)
    for k in range(2):
        lanes = slice(384 * k, 384 * (k + 1))
        wd[:, lanes] = f1[0, k].astype(F32)
        wo[:, lanes] = f1[2, k].astype(F32)
        wu[k] = f1[1, k].astype(F32)
    low_half = lax.broadcasted_iota(jnp.int32, (1, 128), 1) < 64
    tile = lambda k, t: f2[k, :, 128 * t:128 * (t + 1)].astype(F32)
    for t, out in enumerate((wq, wk, wv)):
        out[:, 0:128] = tile(0, t)
        out[:, 256:384] = tile(1, t)
    wq[:, 128:256] = jnp.where(low_half, tile(0, 3), tile(1, 3))
    wk[:, 128:256] = pltpu.roll(jnp.where(low_half, tile(1, 3), tile(0, 3)), 64, 1)
    wv[:, 128:256] = jnp.where(low_half, tile(0, 4), tile(1, 4))

    @pl.when(pl.program_id(0) == 0)
    def _():
        mine = pl.ds(pl.multiple_of(384 * h, 384), 384)
        for row, out in ((0, f_gain), (1, f_shift), (2, bo), (3, bd), (4, bu), (5, a_gain), (6, a_shift)):
            out[...] = vec[row:row + 1, mine].reshape(384)
        low = jnp.where(h == 0, vec[8:9], vec[9:10])
        high = jnp.where(h == 0, vec[10:11], vec[11:12])
        for first, out in ((0, bq), (512, bv)):
            a, b = low[:, first:first + 256], high[:, first:first + 256]
            parts = [a[:, 0:128], a[:, 128:256] + b[:, 0:128], b[:, 128:256]]
            out[...] = jnp.concatenate(parts, axis=1).reshape(384)


def fast_layer(
    tokens, cotangent, attn_gain, attn_shift, query_weight, query_bias, key_weight, value_weight,
    value_bias, out_weight, out_bias, ffn_gain, ffn_shift, up_weight, up_bias, down_weight,
    down_bias, atom_counts, edge_counts,
):
    zc = lax.axis_size("mol") // 2
    anywhere = pl.BlockSpec(memory_space=pl.ANY)
    vmem = pl.BlockSpec(memory_space=pltpu.VMEM)
    smem = pl.BlockSpec(memory_space=pltpu.SMEM)
    shape = jax.ShapeDtypeStruct
    SEM.clear()
    buf = lambda dtype, *dims: pltpu.VMEM(dims, dtype)
    scratch = [
        buf(BF, 256, 768), buf(BF, 256, 768), buf(BF, 3, 192 // zc, 384), buf(BF, 384 // zc, 640), buf(BF, TOTAL, 640),
        buf(BF, PADDED, 768), buf(BF, 256, 768), buf(F32, 256, 768), buf(BF, 768, 768),
        buf(BF, 2, 384, 768), buf(BF, 2, 768, 384), buf(BF, 2, 384, 768), buf(F32, 2, 8, 384),
        buf(BF, PADDED, 768), buf(BF, PADDED, 768), buf(BF, TOTAL, 768),
        buf(BF, HEADS_HERE, TOTAL, 256), buf(BF, HEADS_HERE, TOTAL, 256),
        buf(BF, 2048, 640), buf(BF, 2048, 640), buf(BF, 1536, 768),
        buf(F32, 256, 768), buf(jnp.int32, TOTAL, 1),
        buf(F32, TOTAL, 256), buf(BF, TOTAL, 256), buf(BF, 4, 256, 256), buf(BF, TOTAL, 256), buf(F32, TOTAL, 128),
        buf(F32, 256, 768), buf(F32, 256, 768), buf(F32, 256, 768), buf(F32, 256, 128), buf(F32, 256, 768),
        buf(BF, 256, 768), buf(BF, 256, 768), buf(BF, 256, 768), buf(BF, 256, 768), buf(BF, 256, 768),
        buf(BF, 256, 768), buf(BF, 256, 768), buf(F32, 256, 768),
        buf(BF, 2048, 768), buf(F32, PADDED, 256), buf(F32, PADDED, 256),
        buf(BF, 3, 2, 2, 384, 384), buf(BF, 3, 2, 384, 384), buf(BF, 3, 384, 384), buf(BF, 3, 384, 384),
        buf(BF, 3, 192, 384), buf(BF, 3, 192, 384), buf(BF, 3, zc - 1, 192 // zc, 384),
        buf(BF, 2, 384, 640), buf(BF, 384, 640), buf(BF, zc - 1, 384 // zc, 640),
        buf(BF, TOTAL, 768), buf(BF, 256 + NODES, 768), buf(BF, 256 + NODES, 768), buf(BF, 256, 768),
        buf(F32, 4, 16, 768), buf(F32, zc, 16, 768), buf(F32, 2, 16, 768),
        pltpu.SemaphoreType.DMA((N_SEMS,)), pltpu.SemaphoreType.DMA((N_SEMS,)), pltpu.SemaphoreType.DMA((N_LOCAL,)),
    ]
    d_out, d_tok, f1, f2, vec = pl.pallas_call(
        layer_kernel,
        out_shape=[
            shape((512, 768), BF), shape((512, 768), BF), shape((3, 2, 384, 384), BF),
            shape((2, 768, 640), BF), shape((16, 768), F32),
        ],
        in_specs=[anywhere] * 8 + [smem] * 2 + [vmem] * 9,
        out_specs=[anywhere] * 4 + [vmem],
        scratch_shapes=scratch,
        compiler_params=pltpu.CompilerParams(
            collective_id=0, has_side_effects=True, vmem_limit_bytes=61 * 2**20
        ),
        name="layer",
    )(
        tokens, cotangent, query_weight, key_weight, value_weight, out_weight, up_weight, down_weight,
        atom_counts, edge_counts, attn_gain, attn_shift, query_bias, value_bias, out_bias,
        ffn_gain, ffn_shift, up_bias, down_bias,
    )
    assert sum(n for _, n in SEM.values()) <= N_SEMS
    steps = 4
    mat, tall, line = shape((384, 768), F32), shape((768, 384), F32), shape((384,), F32)
    big, pair = shape((512, 768), F32), shape((2, 384, 384), F32)
    by_rows = lambda rows, cols: pl.BlockSpec((rows // steps, cols), lambda i: (i, 0))
    big_spec, mat_spec, tall_spec = by_rows(512, 768), by_rows(384, 768), by_rows(768, 384)
    line_spec = pl.BlockSpec((384,), lambda i: (0,))
    pair_spec = pl.BlockSpec((2, 384 // steps, 384), lambda i: (0, i, 0))
    outs = pl.pallas_call(
        finish_kernel,
        grid=(steps,),
        out_shape=[big, big, line, line, tall, line, tall, tall, line, mat, line, line, line, pair, line, mat, line],
        in_specs=[
            big_spec, big_spec, big_spec, big_spec,
            pl.BlockSpec((3, 2, 384 // steps, 384), lambda i: (0, 0, i, 0)),
            pl.BlockSpec((2, 768 // steps, 640), lambda i: (0, i, 0)),
            pl.BlockSpec((16, 768), lambda i: (0, 0)),
        ],
        out_specs=[
            big_spec, big_spec, line_spec, line_spec, tall_spec, line_spec, tall_spec, tall_spec, line_spec,
            mat_spec, line_spec, line_spec, line_spec, pair_spec, line_spec, mat_spec, line_spec,
        ],
        compiler_params=pltpu.CompilerParams(vmem_limit_bytes=48 * 2**20),
        name="finish",
    )(tokens, cotangent, d_out, d_tok, f1, f2, vec)
    return tuple(o.reshape(768, 384) if o.ndim == 3 else o for o in outs)


def plain_dot(operand, partner):
    return jnp.dot(operand, partner, preferred_element_type=jnp.float32)


def lead_dot(operand, partner):
    return lax.dot_general(
        operand, partner, (((0,), (0,)), ((), ())), preferred_element_type=jnp.float32
    )


def tail_dot(operand, partner):
    return lax.dot_general(
        operand, partner, (((1,), (1,)), ((), ())), preferred_element_type=jnp.float32
    )


def norm_apply(values, gain_vec, shift_vec):
    row_mean = jnp.mean(values, axis=-1, keepdims=True)
    centered = values - row_mean
    variance = jnp.mean(centered * centered, axis=-1, keepdims=True)
    return centered * lax.rsqrt(variance + 1e-05) * gain_vec + shift_vec


def gelu_exact(values):
    return jax.nn.gelu(values, approximate=False)


def segment_ids(counts, added, slot_count):
    members = jnp.arange(counts.shape[0])
    earlier = members[:, None] <= members[None, :]
    seg_ends = jnp.sum(jnp.where(earlier, (counts + added)[:, None], 0), axis=0)
    positions = jnp.arange(slot_count, dtype=jnp.int32)
    return jnp.sum((positions[:, None] >= seg_ends[None, :]).astype(jnp.int32), axis=1)


def head_piece(vector, head_rank, head_share):
    return lax.dynamic_slice_in_dim(vector, head_rank * head_share, head_share)


def on_device(
    tokens,
    cotangent,
    attn_gain,
    attn_shift,
    query_weight,
    query_bias,
    key_weight,
    value_weight,
    value_bias,
    out_weight,
    out_bias,
    ffn_gain,
    ffn_shift,
    up_weight,
    up_bias,
    down_weight,
    down_bias,
    atom_counts,
    edge_counts,
):
    row_count = tokens.shape[0]
    model_width = tokens.shape[1]
    local_width = query_weight.shape[1]
    local_heads = local_width // HEAD_DIM
    head_count = lax.axis_size("head")
    head_rank = lax.axis_index("head")
    stream_rank = lax.axis_index("stream")
    molecules = atom_counts.shape[1]
    head_share = model_width // head_count
    score_scale = HEAD_DIM ** (-0.5)
    seg_node = segment_ids(atom_counts[0], 1, row_count)
    seg_edge = segment_ids(edge_counts[0], 0, row_count)
    key_seg = jnp.concatenate([seg_node, seg_edge])
    own_seg = jnp.where(stream_rank == 0, seg_node, seg_edge)
    live_rows = (own_seg < molecules).astype(jnp.float32)[:, None]
    residual = tokens.astype(jnp.float32)
    normed, norm_pull = jax.vjp(norm_apply, residual, attn_gain, attn_shift)
    first_in = normed.astype(jnp.bfloat16)
    queries = (plain_dot(first_in, query_weight) + query_bias).astype(jnp.bfloat16)
    keys_local = plain_dot(first_in, key_weight).astype(jnp.bfloat16)
    values_local = (plain_dot(first_in, value_weight) + value_bias).astype(jnp.bfloat16)
    all_keys, all_values = (
        lax.all_gather(keys_local, "stream", axis=0, tiled=True),
        lax.all_gather(values_local, "stream", axis=0, tiled=True),
    )
    key_count = all_keys.shape[0]
    key_heads = all_keys.reshape(key_count, local_heads, HEAD_DIM)
    value_heads = all_values.reshape(key_count, local_heads, HEAD_DIM)
    blocks = row_count // 512
    block_rows = row_count // blocks
    query_blocks = queries.reshape(blocks, block_rows, local_heads, HEAD_DIM)
    seg_blocks = own_seg.reshape(blocks, block_rows)

    def forward_block(pieces):
        query_part, seg_part = pieces
        scores = (
            jnp.einsum("qhd,khd->hqk", query_part, key_heads, preferred_element_type=jnp.float32)
            * score_scale
        )
        same_mol = (seg_part[:, None] == key_seg[None, :])[None]
        scores = jnp.where(same_mol, scores, -1e30)
        row_top = jnp.max(scores, axis=-1, keepdims=True)
        shifted = jnp.exp(scores - row_top)
        row_total = jnp.sum(shifted, axis=-1, keepdims=True)
        prob_low = (shifted / row_total).astype(jnp.bfloat16)
        attended_part = jnp.einsum(
            "hqk,khd->qhd", prob_low, value_heads, preferred_element_type=jnp.float32
        )
        return (attended_part.astype(jnp.bfloat16), (row_top + jnp.log(row_total))[..., 0])

    attended_blocks, lse_blocks = lax.map(forward_block, (query_blocks, seg_blocks))
    attended = attended_blocks.reshape(row_count, local_width)
    attn_sum = lax.psum(plain_dot(attended, out_weight), "head")
    middle = residual + live_rows * (attn_sum + out_bias)
    second, second_pull = jax.vjp(norm_apply, middle, ffn_gain, ffn_shift)
    second_in = second.astype(jnp.bfloat16)
    inner_pre = plain_dot(second_in, up_weight) + up_bias.astype(jnp.float32)
    activated, gelu_pull = jax.vjp(gelu_exact, inner_pre)
    hidden = activated.astype(jnp.bfloat16)
    ffn_sum = lax.psum(plain_dot(hidden, down_weight).astype(jnp.bfloat16), "head").astype(
        jnp.float32
    )
    output = middle + live_rows * (ffn_sum + down_bias)
    down_cot = (live_rows * cotangent).astype(jnp.bfloat16)
    down_weight_grad = lead_dot(hidden, down_cot)
    down_bias_full = jnp.sum(down_cot.astype(jnp.float32), axis=0)
    inner_grad = gelu_pull(tail_dot(down_cot, down_weight))[0].astype(jnp.bfloat16)
    up_weight_grad = lead_dot(second_in, inner_grad)
    up_bias_grad = jnp.sum(inner_grad.astype(jnp.float32), axis=0)
    second_grad = lax.psum(tail_dot(inner_grad, up_weight), "head")
    middle_part, ffn_gain_full, ffn_shift_full = second_pull(second_grad)
    mid_grad = cotangent + middle_part
    ffn_gain_grad = head_piece(ffn_gain_full, head_rank, head_share)
    ffn_shift_grad = head_piece(ffn_shift_full, head_rank, head_share)
    down_bias_grad = head_piece(down_bias_full, head_rank, head_share)
    attn_cot = (live_rows * mid_grad).astype(jnp.bfloat16)
    out_weight_grad = lead_dot(attended, attn_cot)
    out_bias_full = jnp.sum(attn_cot.astype(jnp.float32), axis=0)
    attended_grad = tail_dot(attn_cot, out_weight).astype(jnp.bfloat16)
    grad_blocks = attended_grad.reshape(blocks, block_rows, local_heads, HEAD_DIM)

    def backward_block(running, pieces):
        key_acc, value_acc = running
        query_part, seg_part, lse_part, grad_part = pieces
        scores = (
            jnp.einsum("qhd,khd->hqk", query_part, key_heads, preferred_element_type=jnp.float32)
            * score_scale
        )
        same_mol = (seg_part[:, None] == key_seg[None, :])[None]
        prob_full = jnp.where(same_mol, jnp.exp(scores - lse_part[..., None]), 0.0)
        prob_low = prob_full.astype(jnp.bfloat16)
        prob_grad = jnp.einsum(
            "qhd,khd->hqk", grad_part, value_heads, preferred_element_type=jnp.float32
        )
        row_delta = jnp.sum(prob_grad * prob_full, axis=-1, keepdims=True)
        score_grad = (prob_full * (prob_grad - row_delta)).astype(jnp.bfloat16)
        query_part_grad = (
            jnp.einsum("hqk,khd->qhd", score_grad, key_heads, preferred_element_type=jnp.float32)
            * score_scale
        )
        key_acc = (
            key_acc
            + jnp.einsum("hqk,qhd->khd", score_grad, query_part, preferred_element_type=jnp.float32)
            * score_scale
        )
        value_acc = value_acc + jnp.einsum(
            "hqk,qhd->khd", prob_low, grad_part, preferred_element_type=jnp.float32
        )
        return ((key_acc, value_acc), query_part_grad.astype(jnp.bfloat16))

    zero_keys = jnp.zeros((key_count, local_heads, HEAD_DIM), jnp.float32)
    (key_acc, value_acc), query_grads = lax.scan(
        backward_block, (zero_keys, zero_keys), (query_blocks, seg_blocks, lse_blocks, grad_blocks)
    )
    key_sum, value_sum = (
        lax.psum_scatter(
            key_acc.reshape(key_count, local_width), "stream", scatter_dimension=0, tiled=True
        ),
        lax.psum_scatter(
            value_acc.reshape(key_count, local_width), "stream", scatter_dimension=0, tiled=True
        ),
    )
    key_grad = key_sum.astype(jnp.bfloat16)
    value_grad = value_sum.astype(jnp.bfloat16)
    query_grad = query_grads.reshape(row_count, local_width)
    query_weight_grad = lead_dot(first_in, query_grad)
    query_bias_grad = jnp.sum(query_grad.astype(jnp.float32), axis=0)
    key_weight_grad = lead_dot(first_in, key_grad)
    value_weight_grad = lead_dot(first_in, value_grad)
    value_bias_grad = jnp.sum(value_grad.astype(jnp.float32), axis=0)
    first_part = (
        tail_dot(query_grad, query_weight)
        + tail_dot(key_grad, key_weight)
        + tail_dot(value_grad, value_weight)
    )
    first_grad = lax.psum(first_part.astype(jnp.bfloat16), "head").astype(jnp.float32)
    resid_part, attn_gain_full, attn_shift_full = norm_pull(first_grad)
    tokens_grad = mid_grad + resid_part
    attn_gain_grad = head_piece(attn_gain_full, head_rank, head_share)
    attn_shift_grad = head_piece(attn_shift_full, head_rank, head_share)
    out_bias_grad = head_piece(out_bias_full, head_rank, head_share)
    (
        attn_gain_grad,
        attn_shift_grad,
        query_weight_grad,
        query_bias_grad,
        key_weight_grad,
        value_weight_grad,
        value_bias_grad,
        out_weight_grad,
        out_bias_grad,
        ffn_gain_grad,
        ffn_shift_grad,
        up_weight_grad,
        up_bias_grad,
        down_weight_grad,
        down_bias_grad,
    ) = lax.psum(
        (
            attn_gain_grad,
            attn_shift_grad,
            query_weight_grad,
            query_bias_grad,
            key_weight_grad,
            value_weight_grad,
            value_bias_grad,
            out_weight_grad,
            out_bias_grad,
            ffn_gain_grad,
            ffn_shift_grad,
            up_weight_grad,
            up_bias_grad,
            down_weight_grad,
            down_bias_grad,
        ),
        ("mol", "stream"),
    )
    return (
        output,
        tokens_grad,
        attn_gain_grad,
        attn_shift_grad,
        query_weight_grad,
        query_bias_grad,
        key_weight_grad,
        value_weight_grad,
        value_bias_grad,
        out_weight_grad,
        out_bias_grad,
        ffn_gain_grad,
        ffn_shift_grad,
        up_weight_grad,
        up_bias_grad,
        down_weight_grad,
        down_bias_grad,
    )


def solution(mesh):
    in_specs = (
        P(("mol", "stream"), None),
        P(("mol", "stream"), None),
        P(),
        P(),
        P(None, "head"),
        P("head"),
        P(None, "head"),
        P(None, "head"),
        P("head"),
        P("head", None),
        P(),
        P(),
        P(),
        P(None, "head"),
        P("head"),
        P("head", None),
        P(),
        P("mol", None),
        P("mol", None),
    )
    out_specs = (
        P(("mol", "stream"), None),
        P(("mol", "stream"), None),
        P("head"),
        P("head"),
        P(None, "head"),
        P("head"),
        P(None, "head"),
        P(None, "head"),
        P("head"),
        P("head", None),
        P("head"),
        P("head"),
        P("head"),
        P(None, "head"),
        P("head"),
        P("head", None),
        P("head"),
    )
    one_chip_pair = (
        mesh.shape["head"] == 2 and mesh.shape["stream"] == 2 and mesh.shape["mol"] == 8
    )
    return jax.shard_map(
        fast_layer if one_chip_pair else on_device, mesh=mesh, in_specs=in_specs, out_specs=out_specs, check_vma=False
    )
```

```python
import functools
import math

import jax
import jax.numpy as jnp
from jax import lax
from jax.experimental import pallas as pl
from jax.experimental.pallas import tpu as pltpu
from jax.sharding import PartitionSpec as P

HEAD_DIM = 24
BF = jnp.bfloat16
F32 = jnp.float32
MESH = pl.DeviceIdType.MESH
EDGES = 512
NODES = 192
TOTAL = EDGES + NODES
PADDED = 768
HEADS_HERE = 8
SCALE = HEAD_DIM ** (-0.5)
SCALE2 = SCALE * math.log2(math.e)
BLOCKS = (
    (0, 128, ((0, 256), (512, 256))),
    (128, 128, ((64, 256), (512, 256))),
    (256, 128, ((192, 256), (512, 256))),
    (384, 128, ((256, 256), (512, 256))),
    (512, 192, ((0, 768),)),
)
OWNERS = (((0, 0), 512, 192), ((1, 0), 0, 256), ((1, 1), 256, 256))


def nn(a, b):
    return jnp.dot(a, b, preferred_element_type=F32)


def nt(a, b):
    return lax.dot_general(a, b, (((1,), (1,)), ((), ())), preferred_element_type=F32)


def tn(a, b):
    return lax.dot_general(a, b, (((0,), (0,)), ((), ())), preferred_element_type=F32)


def row_loop(count, step, fn, init):
    def body(i, carry):
        return fn(pl.ds(pl.multiple_of(i * step, step), step), carry)

    return lax.fori_loop(0, count // step, body, init)


def normed(x):
    mu = jnp.mean(x, axis=-1, keepdims=True)
    xc = x - mu
    var = jnp.mean(xc * xc, axis=-1, keepdims=True)
    r = lax.rsqrt(var + 1e-05)
    return xc * r, r


def col_sum(x):
    return jnp.sum(x, axis=0, keepdims=True)


SEM = {}


def sem_id(name, count=1):
    if name not in SEM:
        SEM[name] = sum(n for _, n in SEM.values()), count
    return SEM[name][0]


N_SEMS = 160
N_LOCAL = 24


def layer_kernel(
    tokens, cot, wq, wk, wv, wo, wu, wd,
    atoms, edges,
    a_gain_v, a_shift_v, q_bias_v, v_bias_v, o_bias_v, f_gain_v, f_shift_v, u_bias_v, d_bias_v,
    d_out, d_tok, f1, f2, vec,
    dov, dtv, zb, fz1, fz2, dxp, tok, res, cotv, ww, fwo, fwu, fwd, ub, fin1, qkv, dxw, qm, dam,
    p0, p1, p2, p3, p4, bias, segc, attf, att, ain, da, delta,
    t0, t1, n2s, r2s, mid, sec, hid, dc, ig, ac, ato, ago, mgd,
    ds, dkf, dvf,
    g1, gs1, xr, gx, yr, gq, zr1, g2, gs2, zr2, fp, fx, fs, fy,
    va, vq, vz, vc,
    ss, rs, ls,
):
    m, s, h = lax.axis_index("mol"), lax.axis_index("stream"), lax.axis_index("head")
    z, c = m // 2, lax.rem(m, 2)
    zc = lax.axis_size("mol") // 2
    me = 2 * s + h
    x_peer, y_peer, xy_peer = (m, s, 1 - h), (m, 1 - s, h), (m, 1 - s, 1 - h)
    quad = (x_peer, y_peer, xy_peer)
    twin = (2 * z + 1 - c, s, h)
    z_peers = [(2 * lax.rem(z + d, zc) + c, s, h) for d in range(1, zc)]

    def remote(name, src, dst, dev, k=0, count=1):
        i = sem_id(name, count) + k
        return pltpu.make_async_remote_copy(
            src_ref=src, dst_ref=dst, send_sem=ss.at[i], recv_sem=rs.at[i],
            device_id=dev, device_id_type=MESH,
        )

    def as_row(ref):
        return ref[...].astype(F32).reshape(1, -1)

    a_gain, a_shift, f_gain, f_shift = (as_row(r) for r in (a_gain_v, a_shift_v, f_gain_v, f_shift_v))
    o_bias, d_bias, q_bias, v_bias = (as_row(r) for r in (o_bias_v, d_bias_v, q_bias_v, v_bias_v))

    def local(k, src, dst):
        return pltpu.make_async_copy(src, dst, ls.at[k])

    own = pl.multiple_of(256 * h, 256)
    other = pl.multiple_of(256 * (1 - h), 256)
    window = pl.multiple_of(128 * s, 128)

    loads = [
        local(0, tokens.at[pl.ds(own, 256)], res),
        local(1, cot.at[pl.ds(own, 256)], cotv),
        local(2, wq.at[:, pl.ds(window, 256)], ww.at[:, 0:256]),
        local(3, wk.at[:, pl.ds(window, 256)], ww.at[:, 256:512]),
        local(4, wv.at[:, pl.ds(window, 256)], ww.at[:, 512:768]),
        local(5, wo, fwo.at[h]),
        local(6, wu, fwu.at[h]),
        local(7, wd, fwd.at[h]),
    ]
    edge_load = local(8, tokens, tok.at[0:EDGES])
    node_load = local(9, tokens.at[0:NODES], tok.at[EDGES:TOTAL])
    pl.when(s == 1)(edge_load.start)
    pl.when(s == 0)(node_load.start)
    for copy in loads:
        copy.start()
    ub[h] = jnp.broadcast_to(as_row(u_bias_v), (8, 384))

    barrier = pltpu.get_barrier_semaphore()
    greeted = [*quad, twin, *z_peers]
    for dev in greeted:
        pl.semaphore_signal(barrier, inc=1, device_id=dev, device_id_type=MESH)
    pl.semaphore_wait(barrier, len(greeted))

    def edge_part(k, half):
        rows = pl.ds(pl.multiple_of(256 * half + 64 * k, 64), 64)
        return rows

    tok_y = [
        remote("tok_y", tokens.at[edge_part(k, h)], tok.at[edge_part(k, h)], y_peer, k, 4)
        for k in range(4)
    ]
    tok_x = [
        remote("tok_x", tok.at[edge_part(k, h)], tok.at[edge_part(k, h)], x_peer, k, 4)
        for k in range(4)
    ]
    tok_x_in = [
        remote("tok_x", tok.at[edge_part(k, 1 - h)], tok.at[edge_part(k, 1 - h)], x_peer, k, 4)
        for k in range(4)
    ]
    tok_n = remote("tok_n", tokens.at[0:NODES], tok.at[EDGES:TOTAL], y_peer)

    @pl.when(s == 1)
    def _():
        for copy in tok_y:
            copy.start()

    pl.when(s == 0)(tok_n.start)
    u_send = remote("ub", ub.at[h], ub.at[h], x_peer)
    u_send.start()
    part_o = pl.ds(pl.multiple_of(192 * c, 192), 192)
    part_u = pl.ds(pl.multiple_of(384 * c, 384), 384)
    w_out = [
        remote("wo_x", wo.at[part_o], fwo.at[h, part_o], x_peer),
        remote("wu_x", wu.at[part_u], fwu.at[h, part_u], x_peer),
        remote("wd_x", wd.at[part_o], fwd.at[h, part_o], x_peer),
    ]

    @pl.when(s == 1)
    def _():
        for k in (0, 2, 1):
            w_out[k].start()

    w_in = [
        remote("wo_x", wo.at[part_o], fwo.at[1 - h, part_o], x_peer),
        remote("wu_x", wu.at[part_u], fwu.at[1 - h, part_u], x_peer),
        remote("wd_x", wd.at[part_o], fwd.at[1 - h, part_o], x_peer),
    ]
    w_twin = [
        remote("wo_c", fwo.at[1 - h, part_o], fwo.at[1 - h, part_o], twin),
        remote("wu_c", fwu.at[1 - h, part_u], fwu.at[1 - h, part_u], twin),
        remote("wd_c", fwd.at[1 - h, part_o], fwd.at[1 - h, part_o], twin),
    ]

    w_y = {
        0: remote("wo_y", fwo.at[1 - h, part_o], fwo.at[1 - h, part_o], y_peer),
        2: remote("wd_y", fwd.at[1 - h, part_o], fwd.at[1 - h, part_o], y_peer),
    }

    def pass_weight(k):
        w_in[k].wait_recv()
        w_y[k].start()
        w_twin[k].start()

    def share_weight(k):
        w_in[k].wait_recv()
        w_twin[k].start()

    def take_weight(k):
        w_y[k].wait_recv()
        w_twin[k].start()

    def ends_of(counts, added):
        total, ends = 0, []
        for j in range(counts.shape[1]):
            total = total + counts[0, j] + added
            ends.append(total)
        return ends

    node_ends, edge_ends = ends_of(atoms, 1), ends_of(edges, 0)
    live_count = jnp.where(s == 0, node_ends[-1], edge_ends[-1])

    def seg_of(position, ends):
        seg = jnp.zeros_like(position)
        for end in ends:
            seg = seg + jnp.where(position >= end, 1, 0)
        return seg

    segc[0:EDGES] = seg_of(lax.broadcasted_iota(jnp.int32, (EDGES, 1), 0), edge_ends)
    segc[EDGES:TOTAL] = seg_of(lax.broadcasted_iota(jnp.int32, (NODES, 1), 0), node_ends)
    at_row = lax.broadcasted_iota(jnp.int32, (1, PADDED), 1)
    seg_r = jnp.where(at_row < EDGES, seg_of(at_row, edge_ends), seg_of(at_row - EDGES, node_ends))
    seg_r = jnp.where(at_row < TOTAL, seg_r, -1)

    lane = lax.broadcasted_iota(jnp.int32, (1, 256), 1) - 64 * s
    head_of = jnp.where((lane >= 0) & (lane < 192), lane // HEAD_DIM, -1)
    zero = jnp.zeros((), BF)

    qkv[TOTAL:PADDED] = jnp.zeros((PADDED - TOTAL, 768), BF)
    bias_row = jnp.concatenate(
        [
            jnp.where(s == 0, q_bias[:, 0:256], q_bias[:, 128:384]),
            jnp.zeros((1, 256), F32),
            jnp.where(s == 0, v_bias[:, 0:256], v_bias[:, 128:384]),
        ],
        axis=1,
    )

    def project(first, count):
        def norm_rows(i, carry):
            rows = pl.ds(pl.multiple_of(first + i * 64, 64), 64)
            n1, _ = normed(tok[rows].astype(F32))
            fin1[rows] = (n1 * a_gain + a_shift).astype(BF)
            return carry

        lax.fori_loop(0, count // 64, norm_rows, 0)
        rows = pl.ds(pl.multiple_of(first, 64), count)
        qkv[rows] = (nn(fin1[rows], ww[...]) + bias_row).astype(BF)

    for copy in loads[2:5]:
        copy.wait()

    @pl.when(s == 1)
    def _():
        edge_load.wait()
        project(0, EDGES)
        tok_n.wait_recv()
        project(EDGES, NODES)
        pass_weight(0)

    @pl.when(s == 0)
    def _():
        node_load.wait()
        project(EDGES, NODES)
        for k in range(4):
            tok_y[k].wait_recv()
            tok_x[k].start()
        w_out[1].start()
        project(own, 256)
        for k in range(4):
            tok_x_in[k].wait_recv()
        project(other, 256)

    for j in range(HEADS_HERE):
        qm[j] = jnp.where(head_of == j, qkv[0:TOTAL, 0:256], zero)

    def send_rows(name, src, dst, k):
        dev_sh, first, count = OWNERS[k]
        target = (m, *dev_sh)
        mine = 2 * dev_sh[0] + dev_sh[1]

        @pl.when(me != mine)
        def _():
            i = sem_id(name + "_s", 3) + k
            j = sem_id(name, 4) + me
            pltpu.make_async_remote_copy(
                src_ref=src.at[first:first + count], dst_ref=dst.at[me, 0:count],
                send_sem=ss.at[i], recv_sem=rs.at[j], device_id=target, device_id_type=MESH,
            ).start()

        @pl.when(me == mine)
        def _():
            dst[mine, 0:count] = src[first:first + count]

    def wait_rows(name, src, dst):
        for k, (dev_sh, first, count) in enumerate(OWNERS):
            mine = 2 * dev_sh[0] + dev_sh[1]

            @pl.when(me == mine)
            def _():
                for r in range(4):
                    if r != mine:
                        j = sem_id(name, 4) + r
                        pltpu.make_async_remote_copy(
                            src_ref=src.at[first:first + count], dst_ref=dst.at[r, 0:count],
                            send_sem=ss.at[j], recv_sem=rs.at[j], device_id=x_peer, device_id_type=MESH,
                        ).wait_recv()

    def wait_sent(name, src, dst):
        for k, (dev_sh, first, count) in enumerate(OWNERS):
            mine = 2 * dev_sh[0] + dev_sh[1]

            @pl.when(me != mine)
            def _():
                i = sem_id(name + "_s", 3) + k
                pltpu.make_async_remote_copy(
                    src_ref=src.at[first:first + count], dst_ref=dst.at[me, 0:count],
                    send_sem=ss.at[i], recv_sem=rs.at[i], device_id=(m, *dev_sh), device_id_type=MESH,
                ).wait_send()

    def pick_heads(stacked, rows):
        total = None
        for j in range(HEADS_HERE):
            part = jnp.where(head_of == j, stacked[j * rows:(j + 1) * rows], 0.0)
            total = part if total is None else total + part
        return total

    probs = (p0, p1, p2, p3, p4)
    to_owner = (None, 1, None, 2, 0)
    group = 4

    @pl.when(s == 0)
    def _():
        ain[:, NODES:256] = jnp.zeros((4, 256 - NODES, 256), BF)

    @pl.when((s == 0) & (h == 1))
    def _():
        ain[:, 0:NODES] = jnp.zeros((4, NODES, 256), BF)

    for b, (q0, qn, segs) in enumerate(BLOCKS):
        o = 0
        for a, n in segs:
            bias[0:qn, o:o + n] = jnp.where(segc[q0:q0 + qn] == seg_r[:, a:a + n], 0.0, -1e30)
            o += n
        for j0 in range(0, HEADS_HERE, group):
            qb = qm[j0:j0 + group, q0:q0 + qn, :].reshape(group * qn, 256)
            raw = [nt(qb, qkv[a:a + n, 256:512]) for a, n in segs]
            for g in range(group):
                j, o, parts = j0 + g, 0, []
                for piece, (a, n) in zip(raw, segs):
                    parts.append(piece[g * qn:(g + 1) * qn] * SCALE2 + bias[0:qn, o:o + n])
                    o += n
                top = functools.reduce(
                    jnp.maximum, [jnp.max(x, axis=1, keepdims=True) for x in parts]
                )
                parts = [jnp.exp2(x - top) for x in parts]
                inv = 1.0 / sum(jnp.sum(x, axis=1, keepdims=True) for x in parts)
                o = 0
                for x, (a, n) in zip(parts, segs):
                    probs[b][j * qn:(j + 1) * qn, o:o + n] = (x * inv).astype(BF)
                    o += n
        o, acc = 0, None
        for a, n in segs:
            part = nn(probs[b][:, o:o + n], qkv[a:a + n, 512:768])
            acc = part if acc is None else acc + part
            o += n
        picked = pick_heads(acc, qn)
        attf[q0:q0 + qn] = picked
        att[q0:q0 + qn] = picked.astype(BF)
        if to_owner[b] is not None:
            send_rows("att", att, ain, to_owner[b])

    @pl.when(s == 1)
    def _():
        pass_weight(2)

    @pl.when(s == 0)
    def _():
        take_weight(0)

    share_weight(1)

    cut = [slice(0, 384), slice(384, 768)]
    g1_of = (
        lambda cc, xh: tn(hid[:, cut[xh]], dc[:, cut[cc]]),
        lambda cc, xh: tn(sec[:, cut[cc]], ig[:, cut[xh]]),
        lambda cc, xh: tn(ato[:, cut[xh]], ac[:, cut[cc]]),
    )
    g1_twin = [remote("g1_c", g1.at[p, 1 - c], gs1.at[p], twin, p, 3) for p in range(3)]

    def g1_compute(p):
        for cc in range(2):
            for xh in range(2):
                g1[p, cc, xh] = g1_of[p](cc, xh).astype(BF)
        g1_twin[p].start()

    rows_y = pl.ds(pl.multiple_of(192 * (1 - s), 192), 192)
    rows_s = pl.ds(pl.multiple_of(192 * s, 192), 192)
    y_first = (True, True, False)
    g1_x = [
        remote("g1_x", gx.at[p, 1 - h, 0:192], xr.at[p, 0:192], x_peer, p, 3)
        if y_first[p] else remote("g1_x", gs1.at[p, 1 - h], xr.at[p], x_peer, p, 3)
        for p in range(3)
    ]
    g1_y = [
        remote("g1_y", gs1.at[p, :, rows_y], yr.at[p], y_peer, p, 3)
        if y_first[p] else remote("g1_y", gx.at[p, 0, rows_y], yr.at[p, 0], y_peer, p, 3)
        for p in range(3)
    ]
    zn1, zn2 = 192 // zc, 384 // zc

    def chunk(t, n):
        return pl.ds(pl.multiple_of(n * t, n), n)

    g1_z = [
        [
            remote("g1_z", gq.at[p, chunk(lax.rem(z + d, zc), zn1)], zr1.at[p, d - 1], z_peers[d - 1],
                   p * (zc - 1) + d - 1, 3 * (zc - 1))
            for d in range(1, zc)
        ]
        for p in range(3)
    ]

    def add_into(dst, *terms):
        x = terms[0].astype(F32)
        for t in terms[1:]:
            x = x + t.astype(F32)
        dst[...] = x.astype(BF)

    def g1_after_twin(p):
        g1_twin[p].wait_recv()
        for xh in range(2):
            add_into(gs1.at[p, xh], g1[p, c, xh], gs1[p, xh])
        (g1_y if y_first[p] else g1_x)[p].start()

    def g1_after_x(p):
        g1_x[p].wait_recv()
        if y_first[p]:
            add_into(gq.at[p], gx[p, h, 0:192], xr[p, 0:192])
            for copy in g1_z[p]:
                copy.start()
        else:
            add_into(gx.at[p, 0], gs1[p, h], xr[p])
            g1_y[p].start()

    def g1_after_y(p):
        g1_y[p].wait_recv()
        if y_first[p]:
            for xh in range(2):
                add_into(gx.at[p, xh, 0:192], gs1[p, xh, rows_s], yr[p, xh])
            g1_x[p].start()
        else:
            add_into(gq.at[p], gx[p, 0, rows_s], yr[p, 0])
            for copy in g1_z[p]:
                copy.start()

    for copy in (loads[0], loads[1], *loads[5:8]):
        copy.wait()
    row_at = lax.broadcasted_iota(jnp.int32, (256, 1), 0) + own
    live_all = jnp.where(row_at < live_count, 1.0, 0.0)
    r2s[:, 1:2] = live_all
    wait_rows("att", att, ain)
    for x in range(2):
        ato[:, 384 * x:384 * x + 128] = ain[x, :, 0:128]
        ato[:, 384 * x + 128:384 * x + 256] = ain[x, :, 128:256] + ain[2 + x, :, 0:128]
        ato[:, 384 * x + 256:384 * x + 384] = ain[2 + x, :, 128:256]
    twin_o = pl.ds(pl.multiple_of(192 * (1 - c), 192), 192)
    twin_u = pl.ds(pl.multiple_of(384 * (1 - c), 384), 384)
    w_twin_in = [
        remote("wo_c", fwo.at[1 - h, twin_o], fwo.at[1 - h, twin_o], twin),
        remote("wu_c", fwu.at[1 - h, twin_u], fwu.at[1 - h, twin_u], twin),
        remote("wd_c", fwd.at[1 - h, twin_o], fwd.at[1 - h, twin_o], twin),
    ]
    w_twin_in[0].wait_recv()
    wo_all = fwo[...].reshape(768, 768)
    t0[...] = nn(ato[...], wo_all)
    pl.when(s == 0)(lambda: take_weight(2))
    live_of = lambda rows: r2s[rows, 1:2]

    def middle_rows(rows, carry):
        x = res[rows].astype(F32) + live_of(rows) * (t0[rows] + o_bias)
        mid[rows] = x
        n2, r2 = normed(x)
        n2s[rows] = n2
        r2s[rows, 0:1] = r2
        sec[rows] = (n2 * f_gain + f_shift).astype(BF)
        return carry

    row_loop(256, 64, middle_rows, 0)
    w_twin_in[1].wait_recv()
    u_recv = remote("ub", ub.at[1 - h], ub.at[1 - h], x_peer)
    u_recv.wait_recv()
    for x in range(2):
        t0[:, 384 * x:384 * (x + 1)] = nn(sec[...], fwu[x]) + ub[x, 0:1]

    def gelu_rows(rows, carry):
        u = t0[rows]
        cdf = 0.5 * (1.0 + lax.erf(u * math.sqrt(0.5)))
        hid[rows] = (u * cdf).astype(BF)
        t1[rows] = cdf + u * (jnp.exp(-0.5 * u * u) * (1.0 / math.sqrt(2.0 * math.pi)))
        return carry

    row_loop(256, 64, gelu_rows, 0)
    w_twin_in[2].wait_recv()
    wd_all = fwd[...].reshape(768, 768)
    t0[...] = nn(hid[...], wd_all)
    zero_row = jnp.zeros((1, 768), F32)

    def out_rows(rows, carry):
        live = live_of(rows)
        x = (mid[rows] + live * (t0[rows] + d_bias)) - res[rows].astype(F32)
        dov[rows] = x.astype(BF)
        down = (live * cotv[rows]).astype(BF)
        dc[rows] = down
        return carry + col_sum(down.astype(F32))

    down_bias_sum = row_loop(256, 64, out_rows, zero_row)
    own_rows = pl.ds(own, 256)
    other_rows = pl.ds(other, 256)
    out_send = remote("out", dov, d_out.at[own_rows], x_peer)
    out_node = remote("out", dov.at[0:NODES], d_out.at[0:NODES], x_peer)
    pl.when(s == 1)(out_send.start)
    pl.when(me == 0)(out_node.start)
    g1_compute(0)
    stores = [local(10, dov, d_out.at[own_rows])]
    stores[0].start()
    zb[...] = jnp.zeros_like(zb)
    far = [local(18 + k, zb, ref.at[256:512]) for k, ref in enumerate((d_out, d_tok))]
    near = [local(18 + k, zb.at[NODES:256], ref.at[NODES:256]) for k, ref in enumerate((d_out, d_tok))]

    @pl.when(me == 0)
    def _():
        for copy in far:
            copy.start()

    @pl.when(me == 1)
    def _():
        for copy in near:
            copy.start()

    t0[...] = nt(dc[...], wd_all)

    def inner_rows(rows, carry):
        x = (t0[rows] * t1[rows]).astype(BF)
        ig[rows] = x
        return carry + col_sum(x.astype(F32))

    up_bias_sum = row_loop(256, 64, inner_rows, zero_row)
    g1_after_twin(0)
    t0[...] = nt(ig[:, 0:384], fwu[0]) + nt(ig[:, 384:768], fwu[1])

    def second_rows(rows, carry):
        gain_sum, shift_sum, bias_sum = carry
        sg, n2 = t0[rows], n2s[rows]
        g = sg * f_gain
        back = r2s[rows, 0:1] * (
            g - jnp.mean(g, axis=-1, keepdims=True) - n2 * jnp.mean(g * n2, axis=-1, keepdims=True)
        )
        mgd[rows] = back
        x = (live_of(rows) * (cotv[rows] + back)).astype(BF)
        ac[rows] = x
        return gain_sum + col_sum(sg * n2), shift_sum + col_sum(sg), bias_sum + col_sum(x.astype(F32))

    f_gain_sum, f_shift_sum, out_bias_sum = row_loop(
        256, 64, second_rows, (zero_row, zero_row, zero_row)
    )
    ago[...] = nt(ac[...], wo_all).astype(BF)

    for k, (dev_sh, first, count) in enumerate(OWNERS):
        mine = 2 * dev_sh[0] + dev_sh[1]

        @pl.when(me == mine)
        def _():
            for r in range(4):
                cols = slice(384 * (r % 2) + 128 * (r // 2), 384 * (r % 2) + 128 * (r // 2) + 256)
                if r == mine:
                    da[first:first + count] = ago[0:count, cols]
                else:
                    i, j = sem_id("da_s", 4) + r, sem_id("da", 3) + k
                    pltpu.make_async_remote_copy(
                        src_ref=ago.at[0:count, cols], dst_ref=da.at[first:first + count],
                        send_sem=ss.at[i], recv_sem=rs.at[j],
                        device_id=(m, r // 2, r % 2), device_id_type=MESH,
                    ).start()

    g1_compute(1)
    g1_compute(2)
    g1_after_twin(1)
    g1_after_twin(2)

    for k, (dev_sh, first, count) in enumerate(OWNERS):
        mine = 2 * dev_sh[0] + dev_sh[1]

        @pl.when(me != mine)
        def _():
            j = sem_id("da", 3) + k
            pltpu.make_async_remote_copy(
                src_ref=ago.at[0:count, 0:256], dst_ref=da.at[first:first + count],
                send_sem=ss.at[j], recv_sem=rs.at[j], device_id=x_peer, device_id_type=MESH,
            ).wait_recv()

    head_col = lax.broadcasted_iota(jnp.int32, (256, 128), 1)
    lane_row = lax.broadcasted_iota(jnp.int32, (256, 128), 0) - 64 * s
    head_pick = jnp.where(
        (lane_row >= 0) & (lane_row < 192) & (lane_row // HEAD_DIM == head_col), 1.0, 0.0
    ).astype(BF)
    prod = da[0:TOTAL].astype(F32) * attf[...]
    prod_hi = prod.astype(BF)
    delta[...] = nn(prod_hi, head_pick) + nn((prod - prod_hi.astype(F32)).astype(BF), head_pick)
    for j in range(HEADS_HERE):
        dam[j] = jnp.where(head_of == j, da[0:TOTAL], zero)
    dkf[...] = jnp.zeros_like(dkf)
    dvf[...] = jnp.zeros_like(dvf)
    for (q0, qn, segs), pr in zip(BLOCKS, probs):
        o = 0
        for a, n in segs:
            dv = None
            for j in range(HEADS_HERE):
                pv = tn(pr[j * qn:(j + 1) * qn, o:o + n], dam[j, q0:q0 + qn])
                dv = pv if dv is None else dv + pv
            dvf[a:a + n] += dv
            o += n
    dxw[:, 512:768] = dvf[0:TOTAL].astype(BF)

    lanes2 = [slice(0, 256), slice(256, 512), slice(512, 640)]
    g2_twin = [
        remote("g2_c", g2.at[1 - c, :, lanes2[p]], gs2.at[:, lanes2[p]], twin, p, 3) for p in range(3)
    ]
    g2_z = [
        [
            remote("g2_z", gs2.at[chunk(lax.rem(z + d, zc), zn2), lanes2[p]], zr2.at[d - 1, :, lanes2[p]],
                   z_peers[d - 1], p * (zc - 1) + d - 1, 3 * (zc - 1))
            for d in range(1, zc)
        ]
        for p in range(3)
    ]

    def tiles_of(k):
        first = dxw[:, 256 * k:256 * k + 128]
        last = dxw[:, 256 * k + 128:256 * k + 256]
        return jnp.where(s == 0, first, last), jnp.where(s == 0, last, first)

    def g2_compute(p):
        for cc in range(2):
            g2[cc, :, lanes2[p]] = tn(fin1[0:TOTAL, cut[cc]], dxp[:, lanes2[p]]).astype(BF)
        g2_twin[p].start()

    def g2_after_twin(p):
        g2_twin[p].wait_recv()
        add_into(gs2.at[:, lanes2[p]], g2[c, :, lanes2[p]], gs2[:, lanes2[p]])
        for copy in g2_z[p]:
            copy.start()

    stores.append(local(11, dtv, d_tok.at[own_rows]))
    st1, st2 = [None] * 3, [None] * 3
    f1_z, f1_y, f1_c, f2_z, f2_y, f2_c = [], [], [], [], [], []

    def f1_at(p, cc, ss_, zz):
        return f1.at[p, cc, pl.ds(pl.multiple_of(192 * ss_ + zn1 * zz, 16), zn1)]

    def f1_half(p, ss_):
        return f1.at[p, c, pl.ds(pl.multiple_of(192 * ss_, 192), 192)]

    def f2_at(p, cc, ss_, zz):
        return f2.at[ss_, pl.ds(pl.multiple_of(384 * cc + zn2 * zz, 16), zn2), lanes2[p]]

    def f2_half(p, ss_):
        return f2.at[ss_, pl.ds(pl.multiple_of(384 * c, 384), 384), lanes2[p]]

    def g1_after_z(p):
        for copy in g1_z[p]:
            copy.wait_recv()
        add_into(fz1.at[p], gq[p, chunk(z, zn1)], *[zr1[p, d] for d in range(zc - 1)])
        f1_z.append([
            remote("f1_z", fz1.at[p], f1_at(p, c, s, z), z_peers[d], p * (zc - 1) + d, 3 * (zc - 1))
            for d in range(zc - 1)
        ])
        for copy in f1_z[p]:
            copy.start()
        stores.append(local(12 + p, fz1.at[p], f1_at(p, c, s, z)))
        stores[-1].start()
        return stores[-1]

    def f1_after_z(p, store):
        for copy in f1_z[p]:
            copy.wait_recv()
        store.wait()
        f1_y.append(remote("f1_y", f1_half(p, s), f1_half(p, s), y_peer, p, 3))
        f1_c.append(remote("f1_c", f1_half(p, s), f1_half(p, s), twin, 2 * p, 6))
        f1_y[p].start()
        f1_c[-1].start()

    def f1_after_y(p):
        f1_y[p].wait_recv()
        f1_c.append(remote("f1_c", f1_half(p, 1 - s), f1_half(p, 1 - s), twin, 2 * p + 1, 6))
        f1_c[-1].start()

    def g2_after_z(p):
        for copy in g2_z[p]:
            copy.wait_recv()
        add_into(
            fz2.at[:, lanes2[p]], gs2[chunk(z, zn2), lanes2[p]], *[zr2[d, :, lanes2[p]] for d in range(zc - 1)]
        )
        f2_z.append([
            remote("f2_z", fz2.at[:, lanes2[p]], f2_at(p, c, s, z), z_peers[d], p * (zc - 1) + d, 3 * (zc - 1))
            for d in range(zc - 1)
        ])
        for copy in f2_z[p]:
            copy.start()
        stores.append(local(15 + p, fz2.at[:, lanes2[p]], f2_at(p, c, s, z)))
        stores[-1].start()
        return stores[-1]

    def f2_after_z(p, store):
        for copy in f2_z[p]:
            copy.wait_recv()
        store.wait()
        f2_y.append(remote("f2_y", f2_half(p, s), f2_half(p, s), y_peer, p, 3))
        f2_c.append(remote("f2_c", f2_half(p, s), f2_half(p, s), twin, 2 * p, 6))
        f2_y[p].start()
        f2_c[-1].start()

    def f2_after_y(p):
        f2_y[p].wait_recv()
        f2_c.append(remote("f2_c", f2_half(p, 1 - s), f2_half(p, 1 - s), twin, 2 * p + 1, 6))
        f2_c[-1].start()


    dxp[:, 0:128], dxp[:, 128:256] = tiles_of(2)
    g2_compute(0)
    g1_after_y(0)
    for b, (q0, qn, segs) in enumerate(BLOCKS):
        pr = probs[b]
        for j0 in range(0, HEADS_HERE, group):
            ab = dam[j0:j0 + group, q0:q0 + qn, :].reshape(group * qn, 256)
            o = 0
            for a, n in segs:
                pg = nt(ab, qkv[a:a + n, 512:768])
                for g in range(group):
                    j = j0 + g
                    r = slice(j * qn, (j + 1) * qn)
                    ds[r, o:o + n] = (
                        pr[r, o:o + n].astype(F32)
                        * (pg[g * qn:(g + 1) * qn] - delta[q0:q0 + qn, j:j + 1])
                    ).astype(BF)
                o += n
        o, acc = 0, None
        for a, n in segs:
            part = nn(ds[0:HEADS_HERE * qn, o:o + n], qkv[a:a + n, 256:512])
            acc = part if acc is None else acc + part
            o += n
        dxw[q0:q0 + qn, 0:256] = (pick_heads(acc, qn) * SCALE).astype(BF)
        o = 0
        for a, n in segs:
            dk = None
            for j in range(HEADS_HERE):
                pk = tn(ds[j * qn:(j + 1) * qn, o:o + n], qm[j, q0:q0 + qn])
                dk = pk if dk is None else dk + pk
            dkf[a:a + n] += dk
            o += n
        if b == 0:
            g2_after_twin(0)
        if b == 1:
            g1_after_x(0)
            g1_after_y(1)
        if b == 2:
            g1_after_x(2)
        if b == 3:
            g1_after_x(1)
            st2[0] = g2_after_z(0)
    dxw[:, 256:512] = (dkf[0:TOTAL] * SCALE).astype(BF)
    q_full, q_half = tiles_of(0)
    k_full, k_half = tiles_of(1)
    dxp[:, 256:384], dxp[:, 384:512] = q_full, k_full
    dxp[:, 512:640] = (q_half.astype(F32) + pltpu.roll(k_half.astype(F32), 64, 1)).astype(BF)

    fp_x = [
        remote("fp_x", fp.at[chunk(2 * (1 - h) + k, 128)], fx.at[chunk(k, 128)], x_peer, k, 3)
        for k in range(2)
    ]
    fp_xn = [
        remote("fp_xn", fs.at[256 + 96 * k:256 + 96 * (k + 1)], fx.at[256 + 96 * k:256 + 96 * (k + 1)], x_peer, k, 2)
        for k in range(2)
    ]
    fp_y = [
        remote("fp_y", fs.at[chunk(k, 128)], fy.at[chunk(k, 128)], y_peer, k, 2) for k in range(2)
    ]
    fp_yn = [
        remote("fp_yn", fp.at[EDGES + 96 * k:EDGES + 96 * (k + 1)], fy.at[96 * k:96 * (k + 1)], y_peer, k, 2)
        for k in range(2)
    ]
    def fp_after_x(k):
        fp_x[k].wait_recv()
        add_into(fs.at[chunk(k, 128)], fp[chunk(2 * h + k, 128)], fx[chunk(k, 128)])
        pl.when(s == 0)(fp_y[k].start)

    g2_compute(1)
    g2_compute(2)
    for k in range(2):
        rows = chunk(2 * (1 - h) + k, 128)
        fp[rows] = nt(dxw[rows], ww[...]).astype(BF)
        fp_x[k].start()
    g2_after_twin(1)
    g2_after_twin(2)
    fp[EDGES:TOTAL] = nt(dxw[EDGES:TOTAL], ww[...]).astype(BF)

    @pl.when(s == 1)
    def _():
        for copy in fp_yn:
            copy.start()

    fp[pl.ds(own, 256)] = nt(dxw[pl.ds(own, 256)], ww[...]).astype(BF)
    fp_after_x(0)
    fp_after_x(1)

    @pl.when(s == 0)
    def _():
        for k in range(2):
            fp_yn[k].wait_recv()
            at = slice(256 + 96 * k, 256 + 96 * (k + 1))
            add_into(fs.at[at], fp[EDGES + 96 * k:EDGES + 96 * (k + 1)], fy[96 * k:96 * (k + 1)])
            pl.when(h == 1)(fp_xn[k].start)

    qkv_bias_sum = col_sum(dxw[...].astype(F32))

    g1_after_y(2)
    st1[0] = g1_after_z(0)

    def first_rows(rows, fg):
        n1, r1 = normed(res[rows].astype(F32))
        g = fg * a_gain
        back = r1 * (
            g - jnp.mean(g, axis=-1, keepdims=True) - n1 * jnp.mean(g * n1, axis=-1, keepdims=True)
        )
        dtv[rows] = (mgd[rows] + back).astype(BF)
        return jnp.concatenate([col_sum(fg * n1), col_sum(fg)], axis=0)

    def own_chunk(k, n):
        return pl.ds(pl.multiple_of(own + n * k, n), n)

    dt_e = [
        remote("dt", dtv.at[128 * k:128 * (k + 1)], d_tok.at[own_chunk(k, 128)], x_peer, k, 2)
        for k in range(2)
    ]
    dt_n = remote("dt", dtv.at[0:NODES], d_tok.at[0:NODES], x_peer, 0, 2)
    va[...] = jnp.zeros_like(va)

    @pl.when(s == 1)
    def _():
        for k in range(2):
            fp_y[k].wait_recv()

            def edge_rows(i, carry):
                rows = pl.ds(pl.multiple_of(128 * k + 64 * i, 64), 64)
                return carry + first_rows(rows, fs[rows].astype(F32) + fy[rows].astype(F32))

            got = lax.fori_loop(0, 2, edge_rows, jnp.zeros((2, 768), F32))
            va[0:2] += got
            dt_e[k].start()

    @pl.when((s == 0) & (h == 0))
    def _():
        for k in range(2):
            fp_xn[k].wait_recv()

            def node_rows(i, carry):
                rows = pl.ds(pl.multiple_of(96 * k + 32 * i, 32), 32)
                from_fs = pl.ds(pl.multiple_of(256 + 96 * k + 32 * i, 32), 32)
                return carry + first_rows(rows, fs[from_fs].astype(F32) + fx[from_fs].astype(F32))

            got = lax.fori_loop(0, 3, node_rows, jnp.zeros((2, 768), F32))
            va[0:2] += got
        dtv[NODES:256] = mgd[NODES:256].astype(BF)
        dt_n.start()

    @pl.when((s == 0) & (h == 1))
    def _():
        dtv[...] = mgd[...].astype(BF)

    stores[1].start()

    sums = [f_gain_sum, f_shift_sum, out_bias_sum, down_bias_sum, up_bias_sum, va[0:1], va[1:2], zero_row]
    sums += [jnp.where(me == r, qkv_bias_sum, 0.0) for r in range(4)] + [zero_row] * 4
    vq[me] = jnp.concatenate(sums, axis=0)
    v1 = [remote("v_q", vq.at[me], vq.at[me], dev, k, 3) for k, dev in enumerate(quad)]
    for copy in v1:
        copy.start()

    st1[1] = g1_after_z(1)
    st2[1] = g2_after_z(1)
    st2[2] = g2_after_z(2)
    f1_after_z(0, st1[0])
    f2_after_z(0, st2[0])
    st1[2] = g1_after_z(2)
    v1_in = [
        remote("v_q", vq.at[r], vq.at[r], dev, k, 3)
        for k, (dev, r) in enumerate(zip(quad, (2 * s + 1 - h, 2 - 2 * s + h, 3 - 2 * s - h)))
    ]
    for copy in v1_in:
        copy.wait_recv()
    vz[z] = vq[0] + vq[1] + vq[2] + vq[3]
    v2 = [remote("v_z", vz.at[z], vz.at[z], z_peers[d], d, zc - 1) for d in range(zc - 1)]
    for copy in v2:
        copy.start()
    f1_after_z(1, st1[1])
    f2_after_z(1, st2[1])
    f2_after_z(2, st2[2])
    f1_after_y(0)
    f2_after_y(0)
    for copy in v2:
        copy.wait_recv()
    vsum = vz[0]
    for d in range(1, zc):
        vsum = vsum + vz[d]
    vc[c] = vsum
    v3 = remote("v_c", vc.at[c], vc.at[c], twin)
    v3.start()
    f1_after_z(2, st1[2])
    f1_after_y(1)
    f2_after_y(1)
    f2_after_y(2)
    f1_after_y(2)
    v3.wait_recv()
    vec[...] = vc[0] + vc[1]
    for copy in (*f1_c, *f2_c):
        copy.wait_recv()
    for copy in stores[0:2]:
        copy.wait()

    @pl.when(s == 1)
    def _():
        for copy in (*dt_e, out_send):
            copy.wait()

    @pl.when(me == 0)
    def _():
        for copy in (dt_n, out_node):
            copy.wait_send()
        for copy in far:
            copy.wait()

    @pl.when(me == 1)
    def _():
        for copy in (dt_n, out_node):
            copy.wait_recv()
        for copy in near:
            copy.wait()

    @pl.when(s == 1)
    def _():
        for copy in tok_y:
            copy.wait_send()

    @pl.when(s == 0)
    def _():
        tok_n.wait_send()
        for copy in tok_x:
            copy.wait_send()

    wait_sent("att", att, ain)

    @pl.when(s == 0)
    def _():
        for copy in fp_y:
            copy.wait_send()

    @pl.when(me == 1)
    def _():
        for copy in fp_xn:
            copy.wait_send()

    @pl.when(s == 1)
    def _():
        for copy in fp_yn:
            copy.wait_send()

    @pl.when(s == 1)
    def _():
        w_out[0].wait_send()
        w_out[2].wait_send()
        w_y[0].wait_send()
        w_y[2].wait_send()

    for k, (dev_sh, first, count) in enumerate(OWNERS):
        mine = 2 * dev_sh[0] + dev_sh[1]

        @pl.when(me == mine)
        def _():
            for r in range(4):
                if r != mine:
                    i = sem_id("da_s", 4) + r
                    pltpu.make_async_remote_copy(
                        src_ref=ago.at[0:count, 0:256], dst_ref=da.at[first:first + count],
                        send_sem=ss.at[i], recv_sem=rs.at[i], device_id=x_peer, device_id_type=MESH,
                    ).wait_send()

    for copy in (
        u_send, w_out[1], *w_twin, *g1_twin, *g1_x, *g1_y, *sum(g1_z, []), *fp_x, *g2_twin,
        *sum(g2_z, []), *v1, *sum(f1_z, []), *f1_y, *f1_c, *sum(f2_z, []), *f2_y, *f2_c, *v2, v3,
    ):
        copy.wait_send()


def finish_kernel(
    tokens, cot, d_out, d_tok, f1, f2, vec,
    output, tokens_grad, a_gain, a_shift, wq, bq, wk, wv, bv, wo, bo, f_gain, f_shift, wu, bu, wd, bd,
):
    h = lax.axis_index("head")
    output[...] = tokens[...].astype(F32) + d_out[...].astype(F32)
    tokens_grad[...] = cot[...] + d_tok[...].astype(F32)
    for k in range(2):
        lanes = slice(384 * k, 384 * (k + 1))
        wd[:, lanes] = f1[0, k].astype(F32)
        wo[:, lanes] = f1[2, k].astype(F32)
        wu[k] = f1[1, k].astype(F32)
    low_half = lax.broadcasted_iota(jnp.int32, (1, 128), 1) < 64
    tile = lambda k, t: f2[k, :, 128 * t:128 * (t + 1)].astype(F32)
    for t, out in ((0, wv), (2, wq), (3, wk)):
        out[:, 0:128] = tile(0, t)
        out[:, 256:384] = tile(1, t)
    wq[:, 128:256] = jnp.where(low_half, tile(0, 4), tile(1, 4))
    wk[:, 128:256] = pltpu.roll(jnp.where(low_half, tile(1, 4), tile(0, 4)), 64, 1)
    wv[:, 128:256] = jnp.where(low_half, tile(0, 1), tile(1, 1))

    @pl.when(pl.program_id(0) == 0)
    def _():
        mine = pl.ds(pl.multiple_of(384 * h, 384), 384)
        for row, out in ((0, f_gain), (1, f_shift), (2, bo), (3, bd), (4, bu), (5, a_gain), (6, a_shift)):
            out[...] = vec[row:row + 1, mine].reshape(384)
        low = jnp.where(h == 0, vec[8:9], vec[9:10])
        high = jnp.where(h == 0, vec[10:11], vec[11:12])
        for first, out in ((0, bq), (512, bv)):
            a, b = low[:, first:first + 256], high[:, first:first + 256]
            parts = [a[:, 0:128], a[:, 128:256] + b[:, 0:128], b[:, 128:256]]
            out[...] = jnp.concatenate(parts, axis=1).reshape(384)


def fast_layer(
    tokens, cotangent, attn_gain, attn_shift, query_weight, query_bias, key_weight, value_weight,
    value_bias, out_weight, out_bias, ffn_gain, ffn_shift, up_weight, up_bias, down_weight,
    down_bias, atom_counts, edge_counts,
):
    zc = lax.axis_size("mol") // 2
    anywhere = pl.BlockSpec(memory_space=pl.ANY)
    vmem = pl.BlockSpec(memory_space=pltpu.VMEM)
    smem = pl.BlockSpec(memory_space=pltpu.SMEM)
    shape = jax.ShapeDtypeStruct
    SEM.clear()
    buf = lambda dtype, *dims: pltpu.VMEM(dims, dtype)
    scratch = [
        buf(BF, 256, 768), buf(BF, 256, 768), buf(BF, 256, 768), buf(BF, 3, 192 // zc, 384), buf(BF, 384 // zc, 640), buf(BF, TOTAL, 640),
        buf(BF, PADDED, 768), buf(BF, 256, 768), buf(F32, 256, 768), buf(BF, 768, 768),
        buf(BF, 2, 384, 768), buf(BF, 2, 768, 384), buf(BF, 2, 384, 768), buf(F32, 2, 8, 384),
        buf(BF, PADDED, 768), buf(BF, PADDED, 768), buf(BF, TOTAL, 768),
        buf(BF, HEADS_HERE, TOTAL, 256), buf(BF, HEADS_HERE, TOTAL, 256),
        buf(BF, 1024, 512), buf(BF, 1024, 512), buf(BF, 1024, 512), buf(BF, 1024, 512), buf(BF, 1536, 768),
        buf(F32, 256, 768), buf(jnp.int32, TOTAL, 1),
        buf(F32, TOTAL, 256), buf(BF, TOTAL, 256), buf(BF, 4, 256, 256), buf(BF, TOTAL, 256), buf(F32, TOTAL, 128),
        buf(F32, 256, 768), buf(F32, 256, 768), buf(F32, 256, 768), buf(F32, 256, 128), buf(F32, 256, 768),
        buf(BF, 256, 768), buf(BF, 256, 768), buf(BF, 256, 768), buf(BF, 256, 768), buf(BF, 256, 768),
        buf(BF, 256, 768), buf(BF, 256, 768), buf(F32, 256, 768),
        buf(BF, 1536, 768), buf(F32, PADDED, 256), buf(F32, PADDED, 256),
        buf(BF, 3, 2, 2, 384, 384), buf(BF, 3, 2, 384, 384), buf(BF, 3, 384, 384), buf(BF, 3, 2, 384, 384),
        buf(BF, 3, 2, 192, 384), buf(BF, 3, 192, 384), buf(BF, 3, zc - 1, 192 // zc, 384),
        buf(BF, 2, 384, 640), buf(BF, 384, 640), buf(BF, zc - 1, 384 // zc, 640),
        buf(BF, TOTAL, 768), buf(BF, 256 + NODES, 768), buf(BF, 256 + NODES, 768), buf(BF, 256, 768),
        buf(F32, 8, 768), buf(F32, 4, 16, 768), buf(F32, zc, 16, 768), buf(F32, 2, 16, 768),
        pltpu.SemaphoreType.DMA((N_SEMS,)), pltpu.SemaphoreType.DMA((N_SEMS,)), pltpu.SemaphoreType.DMA((N_LOCAL,)),
    ]
    d_out, d_tok, f1, f2, vec = pl.pallas_call(
        layer_kernel,
        out_shape=[
            shape((512, 768), BF), shape((512, 768), BF), shape((3, 2, 384, 384), BF),
            shape((2, 768, 640), BF), shape((16, 768), F32),
        ],
        in_specs=[anywhere] * 8 + [smem] * 2 + [vmem] * 9,
        out_specs=[anywhere] * 4 + [vmem],
        scratch_shapes=scratch,
        compiler_params=pltpu.CompilerParams(
            collective_id=0, has_side_effects=True, vmem_limit_bytes=61 * 2**20
        ),
        name="layer",
    )(
        tokens, cotangent, query_weight, key_weight, value_weight, out_weight, up_weight, down_weight,
        atom_counts, edge_counts, attn_gain, attn_shift, query_bias, value_bias, out_bias,
        ffn_gain, ffn_shift, up_bias, down_bias,
    )
    assert sum(n for _, n in SEM.values()) <= N_SEMS
    steps = 4
    mat, tall, line = shape((384, 768), F32), shape((768, 384), F32), shape((384,), F32)
    big, pair = shape((512, 768), F32), shape((2, 384, 384), F32)
    by_rows = lambda rows, cols: pl.BlockSpec((rows // steps, cols), lambda i: (i, 0))
    big_spec, mat_spec, tall_spec = by_rows(512, 768), by_rows(384, 768), by_rows(768, 384)
    line_spec = pl.BlockSpec((384,), lambda i: (0,))
    pair_spec = pl.BlockSpec((2, 384 // steps, 384), lambda i: (0, i, 0))
    outs = pl.pallas_call(
        finish_kernel,
        grid=(steps,),
        out_shape=[big, big, line, line, tall, line, tall, tall, line, mat, line, line, line, pair, line, mat, line],
        in_specs=[
            big_spec, big_spec, big_spec, big_spec,
            pl.BlockSpec((3, 2, 384 // steps, 384), lambda i: (0, 0, i, 0)),
            pl.BlockSpec((2, 768 // steps, 640), lambda i: (0, i, 0)),
            pl.BlockSpec((16, 768), lambda i: (0, 0)),
        ],
        out_specs=[
            big_spec, big_spec, line_spec, line_spec, tall_spec, line_spec, tall_spec, tall_spec, line_spec,
            mat_spec, line_spec, line_spec, line_spec, pair_spec, line_spec, mat_spec, line_spec,
        ],
        compiler_params=pltpu.CompilerParams(vmem_limit_bytes=60 * 2**20),
        name="finish",
    )(tokens, cotangent, d_out, d_tok, f1, f2, vec)
    return tuple(o.reshape(768, 384) if o.ndim == 3 else o for o in outs)


def plain_dot(operand, partner):
    return jnp.dot(operand, partner, preferred_element_type=jnp.float32)


def lead_dot(operand, partner):
    return lax.dot_general(
        operand, partner, (((0,), (0,)), ((), ())), preferred_element_type=jnp.float32
    )


def tail_dot(operand, partner):
    return lax.dot_general(
        operand, partner, (((1,), (1,)), ((), ())), preferred_element_type=jnp.float32
    )


def norm_apply(values, gain_vec, shift_vec):
    row_mean = jnp.mean(values, axis=-1, keepdims=True)
    centered = values - row_mean
    variance = jnp.mean(centered * centered, axis=-1, keepdims=True)
    return centered * lax.rsqrt(variance + 1e-05) * gain_vec + shift_vec


def gelu_exact(values):
    return jax.nn.gelu(values, approximate=False)


def segment_ids(counts, added, slot_count):
    members = jnp.arange(counts.shape[0])
    earlier = members[:, None] <= members[None, :]
    seg_ends = jnp.sum(jnp.where(earlier, (counts + added)[:, None], 0), axis=0)
    positions = jnp.arange(slot_count, dtype=jnp.int32)
    return jnp.sum((positions[:, None] >= seg_ends[None, :]).astype(jnp.int32), axis=1)


def head_piece(vector, head_rank, head_share):
    return lax.dynamic_slice_in_dim(vector, head_rank * head_share, head_share)


def on_device(
    tokens,
    cotangent,
    attn_gain,
    attn_shift,
    query_weight,
    query_bias,
    key_weight,
    value_weight,
    value_bias,
    out_weight,
    out_bias,
    ffn_gain,
    ffn_shift,
    up_weight,
    up_bias,
    down_weight,
    down_bias,
    atom_counts,
    edge_counts,
):
    row_count = tokens.shape[0]
    model_width = tokens.shape[1]
    local_width = query_weight.shape[1]
    local_heads = local_width // HEAD_DIM
    head_count = lax.axis_size("head")
    head_rank = lax.axis_index("head")
    stream_rank = lax.axis_index("stream")
    molecules = atom_counts.shape[1]
    head_share = model_width // head_count
    score_scale = HEAD_DIM ** (-0.5)
    seg_node = segment_ids(atom_counts[0], 1, row_count)
    seg_edge = segment_ids(edge_counts[0], 0, row_count)
    key_seg = jnp.concatenate([seg_node, seg_edge])
    own_seg = jnp.where(stream_rank == 0, seg_node, seg_edge)
    live_rows = (own_seg < molecules).astype(jnp.float32)[:, None]
    residual = tokens.astype(jnp.float32)
    normed, norm_pull = jax.vjp(norm_apply, residual, attn_gain, attn_shift)
    first_in = normed.astype(jnp.bfloat16)
    queries = (plain_dot(first_in, query_weight) + query_bias).astype(jnp.bfloat16)
    keys_local = plain_dot(first_in, key_weight).astype(jnp.bfloat16)
    values_local = (plain_dot(first_in, value_weight) + value_bias).astype(jnp.bfloat16)
    all_keys, all_values = (
        lax.all_gather(keys_local, "stream", axis=0, tiled=True),
        lax.all_gather(values_local, "stream", axis=0, tiled=True),
    )
    key_count = all_keys.shape[0]
    key_heads = all_keys.reshape(key_count, local_heads, HEAD_DIM)
    value_heads = all_values.reshape(key_count, local_heads, HEAD_DIM)
    blocks = row_count // 512
    block_rows = row_count // blocks
    query_blocks = queries.reshape(blocks, block_rows, local_heads, HEAD_DIM)
    seg_blocks = own_seg.reshape(blocks, block_rows)

    def forward_block(pieces):
        query_part, seg_part = pieces
        scores = (
            jnp.einsum("qhd,khd->hqk", query_part, key_heads, preferred_element_type=jnp.float32)
            * score_scale
        )
        same_mol = (seg_part[:, None] == key_seg[None, :])[None]
        scores = jnp.where(same_mol, scores, -1e30)
        row_top = jnp.max(scores, axis=-1, keepdims=True)
        shifted = jnp.exp(scores - row_top)
        row_total = jnp.sum(shifted, axis=-1, keepdims=True)
        prob_low = (shifted / row_total).astype(jnp.bfloat16)
        attended_part = jnp.einsum(
            "hqk,khd->qhd", prob_low, value_heads, preferred_element_type=jnp.float32
        )
        return (attended_part.astype(jnp.bfloat16), (row_top + jnp.log(row_total))[..., 0])

    attended_blocks, lse_blocks = lax.map(forward_block, (query_blocks, seg_blocks))
    attended = attended_blocks.reshape(row_count, local_width)
    attn_sum = lax.psum(plain_dot(attended, out_weight), "head")
    middle = residual + live_rows * (attn_sum + out_bias)
    second, second_pull = jax.vjp(norm_apply, middle, ffn_gain, ffn_shift)
    second_in = second.astype(jnp.bfloat16)
    inner_pre = plain_dot(second_in, up_weight) + up_bias.astype(jnp.float32)
    activated, gelu_pull = jax.vjp(gelu_exact, inner_pre)
    hidden = activated.astype(jnp.bfloat16)
    ffn_sum = lax.psum(plain_dot(hidden, down_weight).astype(jnp.bfloat16), "head").astype(
        jnp.float32
    )
    output = middle + live_rows * (ffn_sum + down_bias)
    down_cot = (live_rows * cotangent).astype(jnp.bfloat16)
    down_weight_grad = lead_dot(hidden, down_cot)
    down_bias_full = jnp.sum(down_cot.astype(jnp.float32), axis=0)
    inner_grad = gelu_pull(tail_dot(down_cot, down_weight))[0].astype(jnp.bfloat16)
    up_weight_grad = lead_dot(second_in, inner_grad)
    up_bias_grad = jnp.sum(inner_grad.astype(jnp.float32), axis=0)
    second_grad = lax.psum(tail_dot(inner_grad, up_weight), "head")
    middle_part, ffn_gain_full, ffn_shift_full = second_pull(second_grad)
    mid_grad = cotangent + middle_part
    ffn_gain_grad = head_piece(ffn_gain_full, head_rank, head_share)
    ffn_shift_grad = head_piece(ffn_shift_full, head_rank, head_share)
    down_bias_grad = head_piece(down_bias_full, head_rank, head_share)
    attn_cot = (live_rows * mid_grad).astype(jnp.bfloat16)
    out_weight_grad = lead_dot(attended, attn_cot)
    out_bias_full = jnp.sum(attn_cot.astype(jnp.float32), axis=0)
    attended_grad = tail_dot(attn_cot, out_weight).astype(jnp.bfloat16)
    grad_blocks = attended_grad.reshape(blocks, block_rows, local_heads, HEAD_DIM)

    def backward_block(running, pieces):
        key_acc, value_acc = running
        query_part, seg_part, lse_part, grad_part = pieces
        scores = (
            jnp.einsum("qhd,khd->hqk", query_part, key_heads, preferred_element_type=jnp.float32)
            * score_scale
        )
        same_mol = (seg_part[:, None] == key_seg[None, :])[None]
        prob_full = jnp.where(same_mol, jnp.exp(scores - lse_part[..., None]), 0.0)
        prob_low = prob_full.astype(jnp.bfloat16)
        prob_grad = jnp.einsum(
            "qhd,khd->hqk", grad_part, value_heads, preferred_element_type=jnp.float32
        )
        row_delta = jnp.sum(prob_grad * prob_full, axis=-1, keepdims=True)
        score_grad = (prob_full * (prob_grad - row_delta)).astype(jnp.bfloat16)
        query_part_grad = (
            jnp.einsum("hqk,khd->qhd", score_grad, key_heads, preferred_element_type=jnp.float32)
            * score_scale
        )
        key_acc = (
            key_acc
            + jnp.einsum("hqk,qhd->khd", score_grad, query_part, preferred_element_type=jnp.float32)
            * score_scale
        )
        value_acc = value_acc + jnp.einsum(
            "hqk,qhd->khd", prob_low, grad_part, preferred_element_type=jnp.float32
        )
        return ((key_acc, value_acc), query_part_grad.astype(jnp.bfloat16))

    zero_keys = jnp.zeros((key_count, local_heads, HEAD_DIM), jnp.float32)
    (key_acc, value_acc), query_grads = lax.scan(
        backward_block, (zero_keys, zero_keys), (query_blocks, seg_blocks, lse_blocks, grad_blocks)
    )
    key_sum, value_sum = (
        lax.psum_scatter(
            key_acc.reshape(key_count, local_width), "stream", scatter_dimension=0, tiled=True
        ),
        lax.psum_scatter(
            value_acc.reshape(key_count, local_width), "stream", scatter_dimension=0, tiled=True
        ),
    )
    key_grad = key_sum.astype(jnp.bfloat16)
    value_grad = value_sum.astype(jnp.bfloat16)
    query_grad = query_grads.reshape(row_count, local_width)
    query_weight_grad = lead_dot(first_in, query_grad)
    query_bias_grad = jnp.sum(query_grad.astype(jnp.float32), axis=0)
    key_weight_grad = lead_dot(first_in, key_grad)
    value_weight_grad = lead_dot(first_in, value_grad)
    value_bias_grad = jnp.sum(value_grad.astype(jnp.float32), axis=0)
    first_part = (
        tail_dot(query_grad, query_weight)
        + tail_dot(key_grad, key_weight)
        + tail_dot(value_grad, value_weight)
    )
    first_grad = lax.psum(first_part.astype(jnp.bfloat16), "head").astype(jnp.float32)
    resid_part, attn_gain_full, attn_shift_full = norm_pull(first_grad)
    tokens_grad = mid_grad + resid_part
    attn_gain_grad = head_piece(attn_gain_full, head_rank, head_share)
    attn_shift_grad = head_piece(attn_shift_full, head_rank, head_share)
    out_bias_grad = head_piece(out_bias_full, head_rank, head_share)
    (
        attn_gain_grad,
        attn_shift_grad,
        query_weight_grad,
        query_bias_grad,
        key_weight_grad,
        value_weight_grad,
        value_bias_grad,
        out_weight_grad,
        out_bias_grad,
        ffn_gain_grad,
        ffn_shift_grad,
        up_weight_grad,
        up_bias_grad,
        down_weight_grad,
        down_bias_grad,
    ) = lax.psum(
        (
            attn_gain_grad,
            attn_shift_grad,
            query_weight_grad,
            query_bias_grad,
            key_weight_grad,
            value_weight_grad,
            value_bias_grad,
            out_weight_grad,
            out_bias_grad,
            ffn_gain_grad,
            ffn_shift_grad,
            up_weight_grad,
            up_bias_grad,
            down_weight_grad,
            down_bias_grad,
        ),
        ("mol", "stream"),
    )
    return (
        output,
        tokens_grad,
        attn_gain_grad,
        attn_shift_grad,
        query_weight_grad,
        query_bias_grad,
        key_weight_grad,
        value_weight_grad,
        value_bias_grad,
        out_weight_grad,
        out_bias_grad,
        ffn_gain_grad,
        ffn_shift_grad,
        up_weight_grad,
        up_bias_grad,
        down_weight_grad,
        down_bias_grad,
    )


def solution(mesh):
    in_specs = (
        P(("mol", "stream"), None),
        P(("mol", "stream"), None),
        P(),
        P(),
        P(None, "head"),
        P("head"),
        P(None, "head"),
        P(None, "head"),
        P("head"),
        P("head", None),
        P(),
        P(),
        P(),
        P(None, "head"),
        P("head"),
        P("head", None),
        P(),
        P("mol", None),
        P("mol", None),
    )
    out_specs = (
        P(("mol", "stream"), None),
        P(("mol", "stream"), None),
        P("head"),
        P("head"),
        P(None, "head"),
        P("head"),
        P(None, "head"),
        P(None, "head"),
        P("head"),
        P("head", None),
        P("head"),
        P("head"),
        P("head"),
        P(None, "head"),
        P("head"),
        P("head", None),
        P("head"),
    )
    one_chip_pair = (
        mesh.shape["head"] == 2 and mesh.shape["stream"] == 2 and mesh.shape["mol"] == 8
    )
    return jax.shard_map(
        fast_layer if one_chip_pair else on_device, mesh=mesh, in_specs=in_specs, out_specs=out_specs, check_vma=False
    )
```

```python
import functools
import math

import jax
import jax.numpy as jnp
from jax import lax
from jax.experimental import pallas as pl
from jax.experimental.pallas import tpu as pltpu
from jax.sharding import PartitionSpec as P

HEAD_DIM = 24
BF = jnp.bfloat16
F32 = jnp.float32
MESH = pl.DeviceIdType.MESH
EDGES = 512
NODES = 192
TOTAL = EDGES + NODES
PADDED = 768
HEADS_HERE = 8
SCALE = HEAD_DIM ** (-0.5)
SCALE2 = SCALE * math.log2(math.e)
BLOCKS = (
    (0, 128, ((0, 256), (512, 256))),
    (128, 128, ((64, 256), (512, 256))),
    (256, 128, ((192, 256), (512, 256))),
    (384, 128, ((256, 256), (512, 256))),
    (512, 192, ((0, 768),)),
)
OWNERS = (((0, 0), 512, 192), ((1, 0), 0, 256), ((1, 1), 256, 256))


def nn(a, b):
    return jnp.dot(a, b, preferred_element_type=F32)


def nt(a, b):
    return lax.dot_general(a, b, (((1,), (1,)), ((), ())), preferred_element_type=F32)


def tn(a, b):
    return lax.dot_general(a, b, (((0,), (0,)), ((), ())), preferred_element_type=F32)


def row_loop(count, step, fn, init):
    def body(i, carry):
        return fn(pl.ds(pl.multiple_of(i * step, step), step), carry)

    return lax.fori_loop(0, count // step, body, init)


def normed(x):
    mu = jnp.mean(x, axis=-1, keepdims=True)
    xc = x - mu
    var = jnp.mean(xc * xc, axis=-1, keepdims=True)
    r = lax.rsqrt(var + 1e-05)
    return xc * r, r


def col_sum(x):
    return jnp.sum(x, axis=0, keepdims=True)


SEM = {}


def sem_id(name, count=1):
    if name not in SEM:
        SEM[name] = sum(n for _, n in SEM.values()), count
    return SEM[name][0]


N_SEMS = 160
N_LOCAL = 24


def layer_kernel(
    tokens, cot, wq, wk, wv, wo, wu, wd,
    atoms, edges,
    a_gain_v, a_shift_v, q_bias_v, v_bias_v, o_bias_v, f_gain_v, f_shift_v, u_bias_v, d_bias_v,
    d_out, d_tok, f1, f2, vec,
    dov, dtv, zb, fz1, fz2, dxp, tok, res, cotv, ww, fwo, fwu, fwd, ub, fin1, qkv, dxw, qm, dam,
    p0, p1, p2, p3, p4, bias, segc, attf, att, ain, da, delta,
    t0, t1, n2s, r2s, mid, sec, hid, dc, ig, ac, ato, ago, mgd,
    ds, dkf, dvf,
    g1, gs1, qr, xr, gx, yr, gq, zr1, g2, gs2, zr2, fp, fx, fs, fy,
    va, vq, vz, vc,
    ss, rs, ls,
):
    m, s, h = lax.axis_index("mol"), lax.axis_index("stream"), lax.axis_index("head")
    z, c = m // 2, lax.rem(m, 2)
    zc = lax.axis_size("mol") // 2
    me = 2 * s + h
    x_peer, y_peer, xy_peer = (m, s, 1 - h), (m, 1 - s, h), (m, 1 - s, 1 - h)
    quad = (x_peer, y_peer, xy_peer)
    twin = (2 * z + 1 - c, s, h)
    z_peers = [(2 * lax.rem(z + d, zc) + c, s, h) for d in range(1, zc)]

    def remote(name, src, dst, dev, k=0, count=1):
        i = sem_id(name, count) + k
        return pltpu.make_async_remote_copy(
            src_ref=src, dst_ref=dst, send_sem=ss.at[i], recv_sem=rs.at[i],
            device_id=dev, device_id_type=MESH,
        )

    def as_row(ref):
        return ref[...].astype(F32).reshape(1, -1)

    a_gain, a_shift, f_gain, f_shift = (as_row(r) for r in (a_gain_v, a_shift_v, f_gain_v, f_shift_v))
    o_bias, d_bias, q_bias, v_bias = (as_row(r) for r in (o_bias_v, d_bias_v, q_bias_v, v_bias_v))

    def local(k, src, dst):
        return pltpu.make_async_copy(src, dst, ls.at[k])

    own = pl.multiple_of(256 * h, 256)
    other = pl.multiple_of(256 * (1 - h), 256)
    window = pl.multiple_of(128 * s, 128)

    loads = [
        local(0, tokens.at[pl.ds(own, 256)], res),
        local(1, cot.at[pl.ds(own, 256)], cotv),
        local(2, wq.at[:, pl.ds(window, 256)], ww.at[:, 0:256]),
        local(3, wk.at[:, pl.ds(window, 256)], ww.at[:, 256:512]),
        local(4, wv.at[:, pl.ds(window, 256)], ww.at[:, 512:768]),
        local(5, wo, fwo.at[h]),
        local(6, wu, fwu.at[h]),
        local(7, wd, fwd.at[h]),
    ]
    edge_load = local(8, tokens, tok.at[0:EDGES])
    node_load = local(9, tokens.at[0:NODES], tok.at[EDGES:TOTAL])
    pl.when(s == 1)(edge_load.start)
    pl.when(s == 0)(node_load.start)
    for copy in loads:
        copy.start()
    ub[h] = jnp.broadcast_to(as_row(u_bias_v), (8, 384))

    barrier = pltpu.get_barrier_semaphore()
    greeted = [*quad, twin, *z_peers]
    for dev in greeted:
        pl.semaphore_signal(barrier, inc=1, device_id=dev, device_id_type=MESH)
    pl.semaphore_wait(barrier, len(greeted))

    def edge_part(k, half):
        rows = pl.ds(pl.multiple_of(256 * half + 64 * k, 64), 64)
        return rows

    tok_y = [
        remote("tok_y", tokens.at[edge_part(k, h)], tok.at[edge_part(k, h)], y_peer, k, 4)
        for k in range(4)
    ]
    tok_x = [
        remote("tok_x", tok.at[edge_part(k, h)], tok.at[edge_part(k, h)], x_peer, k, 4)
        for k in range(4)
    ]
    tok_x_in = [
        remote("tok_x", tok.at[edge_part(k, 1 - h)], tok.at[edge_part(k, 1 - h)], x_peer, k, 4)
        for k in range(4)
    ]
    tok_n = remote("tok_n", tokens.at[0:NODES], tok.at[EDGES:TOTAL], y_peer)

    @pl.when(s == 1)
    def _():
        for copy in tok_y:
            copy.start()

    pl.when(s == 0)(tok_n.start)
    u_send = remote("ub", ub.at[h], ub.at[h], x_peer)
    u_send.start()
    part_o = pl.ds(pl.multiple_of(192 * c, 192), 192)
    part_u = pl.ds(pl.multiple_of(384 * c, 384), 384)
    w_out = [
        remote("wo_x", wo.at[part_o], fwo.at[h, part_o], x_peer),
        remote("wu_x", wu.at[part_u], fwu.at[h, part_u], x_peer),
        remote("wd_x", wd.at[part_o], fwd.at[h, part_o], x_peer),
    ]

    @pl.when(s == 1)
    def _():
        for k in (0, 2, 1):
            w_out[k].start()

    w_in = [
        remote("wo_x", wo.at[part_o], fwo.at[1 - h, part_o], x_peer),
        remote("wu_x", wu.at[part_u], fwu.at[1 - h, part_u], x_peer),
        remote("wd_x", wd.at[part_o], fwd.at[1 - h, part_o], x_peer),
    ]
    w_twin = [
        remote("wo_c", fwo.at[1 - h, part_o], fwo.at[1 - h, part_o], twin),
        remote("wu_c", fwu.at[1 - h, part_u], fwu.at[1 - h, part_u], twin),
        remote("wd_c", fwd.at[1 - h, part_o], fwd.at[1 - h, part_o], twin),
    ]

    w_y = {
        0: remote("wo_y", fwo.at[1 - h, part_o], fwo.at[1 - h, part_o], y_peer),
        2: remote("wd_y", fwd.at[1 - h, part_o], fwd.at[1 - h, part_o], y_peer),
    }

    def pass_weight(k):
        w_in[k].wait_recv()
        w_y[k].start()
        w_twin[k].start()

    def share_weight(k):
        w_in[k].wait_recv()
        w_twin[k].start()

    def take_weight(k):
        w_y[k].wait_recv()
        w_twin[k].start()

    def ends_of(counts, added):
        total, ends = 0, []
        for j in range(counts.shape[1]):
            total = total + counts[0, j] + added
            ends.append(total)
        return ends

    node_ends, edge_ends = ends_of(atoms, 1), ends_of(edges, 0)
    live_count = jnp.where(s == 0, node_ends[-1], edge_ends[-1])

    def seg_of(position, ends):
        seg = jnp.zeros_like(position)
        for end in ends:
            seg = seg + jnp.where(position >= end, 1, 0)
        return seg

    segc[0:EDGES] = seg_of(lax.broadcasted_iota(jnp.int32, (EDGES, 1), 0), edge_ends)
    segc[EDGES:TOTAL] = seg_of(lax.broadcasted_iota(jnp.int32, (NODES, 1), 0), node_ends)
    at_row = lax.broadcasted_iota(jnp.int32, (1, PADDED), 1)
    seg_r = jnp.where(at_row < EDGES, seg_of(at_row, edge_ends), seg_of(at_row - EDGES, node_ends))
    seg_r = jnp.where(at_row < TOTAL, seg_r, -1)

    lane = lax.broadcasted_iota(jnp.int32, (1, 256), 1) - 64 * s
    head_of = jnp.where((lane >= 0) & (lane < 192), lane // HEAD_DIM, -1)
    zero = jnp.zeros((), BF)

    qkv[TOTAL:PADDED] = jnp.zeros((PADDED - TOTAL, 768), BF)
    bias_row = jnp.concatenate(
        [
            jnp.where(s == 0, q_bias[:, 0:256], q_bias[:, 128:384]),
            jnp.zeros((1, 256), F32),
            jnp.where(s == 0, v_bias[:, 0:256], v_bias[:, 128:384]),
        ],
        axis=1,
    )

    def project(first, count):
        def norm_rows(i, carry):
            rows = pl.ds(pl.multiple_of(first + i * 64, 64), 64)
            n1, _ = normed(tok[rows].astype(F32))
            fin1[rows] = (n1 * a_gain + a_shift).astype(BF)
            return carry

        lax.fori_loop(0, count // 64, norm_rows, 0)
        rows = pl.ds(pl.multiple_of(first, 64), count)
        qkv[rows] = (nn(fin1[rows], ww[...]) + bias_row).astype(BF)

    for copy in loads[2:5]:
        copy.wait()

    @pl.when(s == 1)
    def _():
        edge_load.wait()
        project(0, EDGES)
        tok_n.wait_recv()
        project(EDGES, NODES)
        pass_weight(0)

    @pl.when(s == 0)
    def _():
        node_load.wait()
        project(EDGES, NODES)
        for k in range(4):
            tok_y[k].wait_recv()
            tok_x[k].start()
        w_out[1].start()
        project(own, 256)
        for k in range(4):
            tok_x_in[k].wait_recv()
        project(other, 256)

    for j in range(HEADS_HERE):
        qm[j] = jnp.where(head_of == j, qkv[0:TOTAL, 0:256], zero)

    def send_rows(name, src, dst, k):
        dev_sh, first, count = OWNERS[k]
        target = (m, *dev_sh)
        mine = 2 * dev_sh[0] + dev_sh[1]

        @pl.when(me != mine)
        def _():
            i = sem_id(name + "_s", 3) + k
            j = sem_id(name, 4) + me
            pltpu.make_async_remote_copy(
                src_ref=src.at[first:first + count], dst_ref=dst.at[me, 0:count],
                send_sem=ss.at[i], recv_sem=rs.at[j], device_id=target, device_id_type=MESH,
            ).start()

        @pl.when(me == mine)
        def _():
            dst[mine, 0:count] = src[first:first + count]

    def wait_rows(name, src, dst):
        for k, (dev_sh, first, count) in enumerate(OWNERS):
            mine = 2 * dev_sh[0] + dev_sh[1]

            @pl.when(me == mine)
            def _():
                for r in range(4):
                    if r != mine:
                        j = sem_id(name, 4) + r
                        pltpu.make_async_remote_copy(
                            src_ref=src.at[first:first + count], dst_ref=dst.at[r, 0:count],
                            send_sem=ss.at[j], recv_sem=rs.at[j], device_id=x_peer, device_id_type=MESH,
                        ).wait_recv()

    def wait_sent(name, src, dst):
        for k, (dev_sh, first, count) in enumerate(OWNERS):
            mine = 2 * dev_sh[0] + dev_sh[1]

            @pl.when(me != mine)
            def _():
                i = sem_id(name + "_s", 3) + k
                pltpu.make_async_remote_copy(
                    src_ref=src.at[first:first + count], dst_ref=dst.at[me, 0:count],
                    send_sem=ss.at[i], recv_sem=rs.at[i], device_id=(m, *dev_sh), device_id_type=MESH,
                ).wait_send()

    def pick_heads(stacked, rows):
        total = None
        for j in range(HEADS_HERE):
            part = jnp.where(head_of == j, stacked[j * rows:(j + 1) * rows], 0.0)
            total = part if total is None else total + part
        return total

    probs = (p0, p1, p2, p3, p4)
    to_owner = (None, 1, None, 2, 0)
    group = 4

    @pl.when(s == 0)
    def _():
        ain[:, NODES:256] = jnp.zeros((4, 256 - NODES, 256), BF)

    @pl.when((s == 0) & (h == 1))
    def _():
        ain[:, 0:NODES] = jnp.zeros((4, NODES, 256), BF)

    for b, (q0, qn, segs) in enumerate(BLOCKS):
        o = 0
        for a, n in segs:
            bias[0:qn, o:o + n] = jnp.where(segc[q0:q0 + qn] == seg_r[:, a:a + n], 0.0, -1e30)
            o += n
        for j0 in range(0, HEADS_HERE, group):
            qb = qm[j0:j0 + group, q0:q0 + qn, :].reshape(group * qn, 256)
            raw = [nt(qb, qkv[a:a + n, 256:512]) for a, n in segs]
            for g in range(group):
                j, o, parts = j0 + g, 0, []
                for piece, (a, n) in zip(raw, segs):
                    parts.append(piece[g * qn:(g + 1) * qn] * SCALE2 + bias[0:qn, o:o + n])
                    o += n
                top = functools.reduce(
                    jnp.maximum, [jnp.max(x, axis=1, keepdims=True) for x in parts]
                )
                parts = [jnp.exp2(x - top) for x in parts]
                inv = 1.0 / sum(jnp.sum(x, axis=1, keepdims=True) for x in parts)
                o = 0
                for x, (a, n) in zip(parts, segs):
                    probs[b][j * qn:(j + 1) * qn, o:o + n] = (x * inv).astype(BF)
                    o += n
        o, acc = 0, None
        for a, n in segs:
            part = nn(probs[b][:, o:o + n], qkv[a:a + n, 512:768])
            acc = part if acc is None else acc + part
            o += n
        picked = pick_heads(acc, qn)
        attf[q0:q0 + qn] = picked
        att[q0:q0 + qn] = picked.astype(BF)
        if to_owner[b] is not None:
            send_rows("att", att, ain, to_owner[b])

    @pl.when(s == 1)
    def _():
        pass_weight(2)

    @pl.when(s == 0)
    def _():
        take_weight(0)

    share_weight(1)

    cut = [slice(0, 384), slice(384, 768)]
    g1_of = (
        lambda cc, xh: tn(hid[:, cut[xh]], dc[:, cut[cc]]),
        lambda cc, xh: tn(sec[:, cut[cc]], ig[:, cut[xh]]),
        lambda cc, xh: tn(ato[:, cut[xh]], ac[:, cut[cc]]),
    )
    g1_twin = [remote("g1_c", g1.at[p, 1 - c], gs1.at[p], twin, p, 3) for p in range(3)]

    def g1_compute(p):
        for cc in range(2):
            for xh in range(2):
                g1[p, cc, xh] = g1_of[p](cc, xh).astype(BF)
        g1_twin[p].start()

    rows_y = pl.ds(pl.multiple_of(192 * (1 - s), 192), 192)
    rows_s = pl.ds(pl.multiple_of(192 * s, 192), 192)
    y_first = (None, True, False)
    g1_q = [
        remote("g1_q", gs1.at[0, 1 - h, rows_s], qr.at[0], x_peer, 0, 3),
        remote("g1_q", gs1.at[0, h, rows_y], qr.at[1], y_peer, 1, 3),
        remote("g1_q", gs1.at[0, 1 - h, rows_y], qr.at[2], xy_peer, 2, 3),
    ]
    g1_x = [
        remote("g1_x", gx.at[p, 1 - h, 0:192], xr.at[p, 0:192], x_peer, p, 3)
        if y_first[p] else remote("g1_x", gs1.at[p, 1 - h], xr.at[p], x_peer, p, 3)
        for p in range(3)
    ]
    g1_y = [
        remote("g1_y", gs1.at[p, :, rows_y], yr.at[p], y_peer, p, 3)
        if y_first[p] else remote("g1_y", gx.at[p, 0, rows_y], yr.at[p, 0], y_peer, p, 3)
        for p in range(3)
    ]
    zn1, zn2 = 192 // zc, 384 // zc

    def chunk(t, n):
        return pl.ds(pl.multiple_of(n * t, n), n)

    g1_z = [
        [
            remote("g1_z", gq.at[p, chunk(lax.rem(z + d, zc), zn1)], zr1.at[p, d - 1], z_peers[d - 1],
                   p * (zc - 1) + d - 1, 3 * (zc - 1))
            for d in range(1, zc)
        ]
        for p in range(3)
    ]

    def add_into(dst, *terms):
        x = terms[0].astype(F32)
        for t in terms[1:]:
            x = x + t.astype(F32)
        dst[...] = x.astype(BF)

    def g1_after_twin(p):
        g1_twin[p].wait_recv()
        for xh in range(2):
            add_into(gs1.at[p, xh], g1[p, c, xh], gs1[p, xh])

    def g1_after_quad():
        for copy in g1_q:
            copy.wait_recv()
        add_into(gq.at[0], gs1[0, h, rows_s], qr[0], qr[1], qr[2])
        for copy in g1_z[0]:
            copy.start()

    def g1_after_x(p):
        g1_x[p].wait_recv()
        if y_first[p]:
            add_into(gq.at[p], gx[p, h, 0:192], xr[p, 0:192])
            for copy in g1_z[p]:
                copy.start()
        else:
            add_into(gx.at[p, 0], gs1[p, h], xr[p])
            g1_y[p].start()

    def g1_after_y(p):
        g1_y[p].wait_recv()
        if y_first[p]:
            for xh in range(2):
                add_into(gx.at[p, xh, 0:192], gs1[p, xh, rows_s], yr[p, xh])
            g1_x[p].start()
        else:
            add_into(gq.at[p], gx[p, 0, rows_s], yr[p, 0])
            for copy in g1_z[p]:
                copy.start()

    for copy in (loads[0], loads[1], *loads[5:8]):
        copy.wait()
    row_at = lax.broadcasted_iota(jnp.int32, (256, 1), 0) + own
    live_all = jnp.where(row_at < live_count, 1.0, 0.0)
    r2s[:, 1:2] = live_all
    wait_rows("att", att, ain)
    for x in range(2):
        ato[:, 384 * x:384 * x + 128] = ain[x, :, 0:128]
        ato[:, 384 * x + 128:384 * x + 256] = ain[x, :, 128:256] + ain[2 + x, :, 0:128]
        ato[:, 384 * x + 256:384 * x + 384] = ain[2 + x, :, 128:256]
    twin_o = pl.ds(pl.multiple_of(192 * (1 - c), 192), 192)
    twin_u = pl.ds(pl.multiple_of(384 * (1 - c), 384), 384)
    w_twin_in = [
        remote("wo_c", fwo.at[1 - h, twin_o], fwo.at[1 - h, twin_o], twin),
        remote("wu_c", fwu.at[1 - h, twin_u], fwu.at[1 - h, twin_u], twin),
        remote("wd_c", fwd.at[1 - h, twin_o], fwd.at[1 - h, twin_o], twin),
    ]
    w_twin_in[0].wait_recv()
    wo_all = fwo[...].reshape(768, 768)
    t0[...] = nn(ato[...], wo_all)
    pl.when(s == 0)(lambda: take_weight(2))
    live_of = lambda rows: r2s[rows, 1:2]

    def middle_rows(rows, carry):
        x = res[rows].astype(F32) + live_of(rows) * (t0[rows] + o_bias)
        mid[rows] = x
        n2, r2 = normed(x)
        n2s[rows] = n2
        r2s[rows, 0:1] = r2
        sec[rows] = (n2 * f_gain + f_shift).astype(BF)
        return carry

    row_loop(256, 64, middle_rows, 0)
    w_twin_in[1].wait_recv()
    u_recv = remote("ub", ub.at[1 - h], ub.at[1 - h], x_peer)
    u_recv.wait_recv()
    for x in range(2):
        t0[:, 384 * x:384 * (x + 1)] = nn(sec[...], fwu[x]) + ub[x, 0:1]

    def gelu_rows(rows, carry):
        u = t0[rows]
        cdf = 0.5 * (1.0 + lax.erf(u * math.sqrt(0.5)))
        hid[rows] = (u * cdf).astype(BF)
        t1[rows] = cdf + u * (jnp.exp(-0.5 * u * u) * (1.0 / math.sqrt(2.0 * math.pi)))
        return carry

    row_loop(256, 64, gelu_rows, 0)
    w_twin_in[2].wait_recv()
    wd_all = fwd[...].reshape(768, 768)
    t0[...] = nn(hid[...], wd_all)
    zero_row = jnp.zeros((1, 768), F32)

    def out_rows(rows, carry):
        live = live_of(rows)
        x = (mid[rows] + live * (t0[rows] + d_bias)) - res[rows].astype(F32)
        dov[rows] = x.astype(BF)
        down = (live * cotv[rows]).astype(BF)
        dc[rows] = down
        return carry + col_sum(down.astype(F32))

    down_bias_sum = row_loop(256, 64, out_rows, zero_row)
    own_rows = pl.ds(own, 256)
    other_rows = pl.ds(other, 256)
    out_send = remote("out", dov, d_out.at[own_rows], x_peer)
    out_node = remote("out", dov.at[0:NODES], d_out.at[0:NODES], x_peer)
    g1_compute(0)
    stores = [local(10, dov, d_out.at[own_rows])]
    stores[0].start()
    zb[...] = jnp.zeros_like(zb)
    far = [local(18 + k, zb, ref.at[256:512]) for k, ref in enumerate((d_out, d_tok))]
    near = [local(18 + k, zb.at[NODES:256], ref.at[NODES:256]) for k, ref in enumerate((d_out, d_tok))]

    @pl.when(me == 0)
    def _():
        for copy in far:
            copy.start()

    @pl.when(me == 1)
    def _():
        for copy in near:
            copy.start()

    t0[...] = nt(dc[...], wd_all)

    def inner_rows(rows, carry):
        x = (t0[rows] * t1[rows]).astype(BF)
        ig[rows] = x
        return carry + col_sum(x.astype(F32))

    up_bias_sum = row_loop(256, 64, inner_rows, zero_row)
    t0[...] = nt(ig[:, 0:384], fwu[0]) + nt(ig[:, 384:768], fwu[1])

    def second_rows(rows, carry):
        gain_sum, shift_sum, bias_sum = carry
        sg, n2 = t0[rows], n2s[rows]
        g = sg * f_gain
        back = r2s[rows, 0:1] * (
            g - jnp.mean(g, axis=-1, keepdims=True) - n2 * jnp.mean(g * n2, axis=-1, keepdims=True)
        )
        mgd[rows] = back
        x = (live_of(rows) * (cotv[rows] + back)).astype(BF)
        ac[rows] = x
        return gain_sum + col_sum(sg * n2), shift_sum + col_sum(sg), bias_sum + col_sum(x.astype(F32))

    f_gain_sum, f_shift_sum, out_bias_sum = row_loop(
        256, 64, second_rows, (zero_row, zero_row, zero_row)
    )
    ago[...] = nt(ac[...], wo_all).astype(BF)

    for k, (dev_sh, first, count) in enumerate(OWNERS):
        mine = 2 * dev_sh[0] + dev_sh[1]

        @pl.when(me == mine)
        def _():
            for r in range(4):
                cols = slice(384 * (r % 2) + 128 * (r // 2), 384 * (r % 2) + 128 * (r // 2) + 256)
                if r == mine:
                    da[first:first + count] = ago[0:count, cols]
                else:
                    i, j = sem_id("da_s", 4) + r, sem_id("da", 3) + k
                    pltpu.make_async_remote_copy(
                        src_ref=ago.at[0:count, cols], dst_ref=da.at[first:first + count],
                        send_sem=ss.at[i], recv_sem=rs.at[j],
                        device_id=(m, r // 2, r % 2), device_id_type=MESH,
                    ).start()

    g1_compute(1)
    g1_compute(2)
    for p in range(3):
        g1_after_twin(p)

    for k, (dev_sh, first, count) in enumerate(OWNERS):
        mine = 2 * dev_sh[0] + dev_sh[1]

        @pl.when(me != mine)
        def _():
            j = sem_id("da", 3) + k
            pltpu.make_async_remote_copy(
                src_ref=ago.at[0:count, 0:256], dst_ref=da.at[first:first + count],
                send_sem=ss.at[j], recv_sem=rs.at[j], device_id=x_peer, device_id_type=MESH,
            ).wait_recv()

    for copy in (*g1_q, g1_y[1], g1_x[2]):
        copy.start()
    head_col = lax.broadcasted_iota(jnp.int32, (256, 128), 1)
    lane_row = lax.broadcasted_iota(jnp.int32, (256, 128), 0) - 64 * s
    head_pick = jnp.where(
        (lane_row >= 0) & (lane_row < 192) & (lane_row // HEAD_DIM == head_col), 1.0, 0.0
    ).astype(BF)
    prod = da[0:TOTAL].astype(F32) * attf[...]
    prod_hi = prod.astype(BF)
    delta[...] = nn(prod_hi, head_pick) + nn((prod - prod_hi.astype(F32)).astype(BF), head_pick)
    for j in range(HEADS_HERE):
        dam[j] = jnp.where(head_of == j, da[0:TOTAL], zero)
    dkf[...] = jnp.zeros_like(dkf)
    dvf[...] = jnp.zeros_like(dvf)
    for (q0, qn, segs), pr in zip(BLOCKS, probs):
        o = 0
        for a, n in segs:
            dv = None
            for j in range(HEADS_HERE):
                pv = tn(pr[j * qn:(j + 1) * qn, o:o + n], dam[j, q0:q0 + qn])
                dv = pv if dv is None else dv + pv
            dvf[a:a + n] += dv
            o += n
    dxw[:, 512:768] = dvf[0:TOTAL].astype(BF)

    lanes2 = [slice(0, 256), slice(256, 512), slice(512, 640)]
    g2_twin = [
        remote("g2_c", g2.at[1 - c, :, lanes2[p]], gs2.at[:, lanes2[p]], twin, p, 3) for p in range(3)
    ]
    g2_z = [
        [
            remote("g2_z", gs2.at[chunk(lax.rem(z + d, zc), zn2), lanes2[p]], zr2.at[d - 1, :, lanes2[p]],
                   z_peers[d - 1], p * (zc - 1) + d - 1, 3 * (zc - 1))
            for d in range(1, zc)
        ]
        for p in range(3)
    ]

    def tiles_of(k):
        first = dxw[:, 256 * k:256 * k + 128]
        last = dxw[:, 256 * k + 128:256 * k + 256]
        return jnp.where(s == 0, first, last), jnp.where(s == 0, last, first)

    def g2_compute(p):
        for cc in range(2):
            g2[cc, :, lanes2[p]] = tn(fin1[0:TOTAL, cut[cc]], dxp[:, lanes2[p]]).astype(BF)
        g2_twin[p].start()

    def g2_after_twin(p):
        g2_twin[p].wait_recv()
        add_into(gs2.at[:, lanes2[p]], g2[c, :, lanes2[p]], gs2[:, lanes2[p]])
        for copy in g2_z[p]:
            copy.start()

    stores.append(local(11, dtv, d_tok.at[own_rows]))
    st1, st2 = [None] * 3, [None] * 3
    f1_z, f1_y, f1_c, f2_z, f2_y, f2_c = [], [], [], [], [], []

    def f1_at(p, cc, ss_, zz):
        return f1.at[p, cc, pl.ds(pl.multiple_of(192 * ss_ + zn1 * zz, 16), zn1)]

    def f1_half(p, ss_):
        return f1.at[p, c, pl.ds(pl.multiple_of(192 * ss_, 192), 192)]

    def f2_at(p, cc, ss_, zz):
        return f2.at[ss_, pl.ds(pl.multiple_of(384 * cc + zn2 * zz, 16), zn2), lanes2[p]]

    def f2_half(p, ss_):
        return f2.at[ss_, pl.ds(pl.multiple_of(384 * c, 384), 384), lanes2[p]]

    def g1_after_z(p):
        for copy in g1_z[p]:
            copy.wait_recv()
        add_into(fz1.at[p], gq[p, chunk(z, zn1)], *[zr1[p, d] for d in range(zc - 1)])
        f1_z.append([
            remote("f1_z", fz1.at[p], f1_at(p, c, s, z), z_peers[d], p * (zc - 1) + d, 3 * (zc - 1))
            for d in range(zc - 1)
        ])
        for copy in f1_z[p]:
            copy.start()
        stores.append(local(12 + p, fz1.at[p], f1_at(p, c, s, z)))
        stores[-1].start()
        return stores[-1]

    def f1_after_z(p, store):
        for copy in f1_z[p]:
            copy.wait_recv()
        store.wait()
        f1_y.append(remote("f1_y", f1_half(p, s), f1_half(p, s), y_peer, p, 3))
        f1_c.append(remote("f1_c", f1_half(p, s), f1_half(p, s), twin, 2 * p, 6))
        f1_y[p].start()
        f1_c[-1].start()

    def f1_after_y(p):
        f1_y[p].wait_recv()
        f1_c.append(remote("f1_c", f1_half(p, 1 - s), f1_half(p, 1 - s), twin, 2 * p + 1, 6))
        f1_c[-1].start()

    def g2_after_z(p):
        for copy in g2_z[p]:
            copy.wait_recv()
        add_into(
            fz2.at[:, lanes2[p]], gs2[chunk(z, zn2), lanes2[p]], *[zr2[d, :, lanes2[p]] for d in range(zc - 1)]
        )
        f2_z.append([
            remote("f2_z", fz2.at[:, lanes2[p]], f2_at(p, c, s, z), z_peers[d], p * (zc - 1) + d, 3 * (zc - 1))
            for d in range(zc - 1)
        ])
        for copy in f2_z[p]:
            copy.start()
        stores.append(local(15 + p, fz2.at[:, lanes2[p]], f2_at(p, c, s, z)))
        stores[-1].start()
        return stores[-1]

    def f2_after_z(p, store):
        for copy in f2_z[p]:
            copy.wait_recv()
        store.wait()
        f2_y.append(remote("f2_y", f2_half(p, s), f2_half(p, s), y_peer, p, 3))
        f2_c.append(remote("f2_c", f2_half(p, s), f2_half(p, s), twin, 2 * p, 6))
        f2_y[p].start()
        f2_c[-1].start()

    def f2_after_y(p):
        f2_y[p].wait_recv()
        f2_c.append(remote("f2_c", f2_half(p, 1 - s), f2_half(p, 1 - s), twin, 2 * p + 1, 6))
        f2_c[-1].start()


    dxp[:, 0:128], dxp[:, 128:256] = tiles_of(2)
    g2_compute(0)
    g1_after_quad()
    for b, (q0, qn, segs) in enumerate(BLOCKS):
        pr = probs[b]
        for j0 in range(0, HEADS_HERE, group):
            ab = dam[j0:j0 + group, q0:q0 + qn, :].reshape(group * qn, 256)
            o = 0
            for a, n in segs:
                pg = nt(ab, qkv[a:a + n, 512:768])
                for g in range(group):
                    j = j0 + g
                    r = slice(j * qn, (j + 1) * qn)
                    ds[r, o:o + n] = (
                        pr[r, o:o + n].astype(F32)
                        * (pg[g * qn:(g + 1) * qn] - delta[q0:q0 + qn, j:j + 1])
                    ).astype(BF)
                o += n
        o, acc = 0, None
        for a, n in segs:
            part = nn(ds[0:HEADS_HERE * qn, o:o + n], qkv[a:a + n, 256:512])
            acc = part if acc is None else acc + part
            o += n
        dxw[q0:q0 + qn, 0:256] = (pick_heads(acc, qn) * SCALE).astype(BF)
        o = 0
        for a, n in segs:
            dk = None
            for j in range(HEADS_HERE):
                pk = tn(ds[j * qn:(j + 1) * qn, o:o + n], qm[j, q0:q0 + qn])
                dk = pk if dk is None else dk + pk
            dkf[a:a + n] += dk
            o += n
        if b == 0:
            g2_after_twin(0)
        if b == 1:
            g1_after_y(1)
        if b == 2:
            g1_after_x(2)
        if b == 3:
            st1[0] = g1_after_z(0)
        if b == 4:
            g1_after_x(1)
            st2[0] = g2_after_z(0)
    dxw[:, 256:512] = (dkf[0:TOTAL] * SCALE).astype(BF)
    q_full, q_half = tiles_of(0)
    k_full, k_half = tiles_of(1)
    dxp[:, 256:384], dxp[:, 384:512] = q_full, k_full
    dxp[:, 512:640] = (q_half.astype(F32) + pltpu.roll(k_half.astype(F32), 64, 1)).astype(BF)

    fp_x = [
        remote("fp_x", fp.at[chunk(2 * (1 - h) + k, 128)], fx.at[chunk(k, 128)], x_peer, k, 3)
        for k in range(2)
    ]
    fp_xn = [
        remote("fp_xn", fs.at[256 + 96 * k:256 + 96 * (k + 1)], fx.at[256 + 96 * k:256 + 96 * (k + 1)], x_peer, k, 2)
        for k in range(2)
    ]
    fp_y = [
        remote("fp_y", fs.at[chunk(k, 128)], fy.at[chunk(k, 128)], y_peer, k, 2) for k in range(2)
    ]
    fp_yn = [
        remote("fp_yn", fp.at[EDGES + 96 * k:EDGES + 96 * (k + 1)], fy.at[96 * k:96 * (k + 1)], y_peer, k, 2)
        for k in range(2)
    ]
    def fp_after_x(k):
        fp_x[k].wait_recv()
        add_into(fs.at[chunk(k, 128)], fp[chunk(2 * h + k, 128)], fx[chunk(k, 128)])
        pl.when(s == 0)(fp_y[k].start)

    g2_compute(1)
    g2_compute(2)
    for k in range(2):
        rows = chunk(2 * (1 - h) + k, 128)
        fp[rows] = nt(dxw[rows], ww[...]).astype(BF)
        fp_x[k].start()
    g2_after_twin(1)
    g2_after_twin(2)
    fp[EDGES:TOTAL] = nt(dxw[EDGES:TOTAL], ww[...]).astype(BF)

    @pl.when(s == 1)
    def _():
        for copy in fp_yn:
            copy.start()

    fp[pl.ds(own, 256)] = nt(dxw[pl.ds(own, 256)], ww[...]).astype(BF)
    g1_after_y(2)
    fp_after_x(0)
    st1[1] = g1_after_z(1)
    fp_after_x(1)
    pl.when(s == 1)(out_send.start)
    pl.when(me == 0)(out_node.start)
    f1_after_z(0, st1[0])
    f2_after_z(0, st2[0])

    @pl.when(s == 0)
    def _():
        for k in range(2):
            fp_yn[k].wait_recv()
            at = slice(256 + 96 * k, 256 + 96 * (k + 1))
            add_into(fs.at[at], fp[EDGES + 96 * k:EDGES + 96 * (k + 1)], fy[96 * k:96 * (k + 1)])
            pl.when(h == 1)(fp_xn[k].start)

    qkv_bias_sum = col_sum(dxw[...].astype(F32))

    st2[1] = g2_after_z(1)
    st2[2] = g2_after_z(2)

    def first_rows(rows, fg):
        n1, r1 = normed(res[rows].astype(F32))
        g = fg * a_gain
        back = r1 * (
            g - jnp.mean(g, axis=-1, keepdims=True) - n1 * jnp.mean(g * n1, axis=-1, keepdims=True)
        )
        dtv[rows] = (mgd[rows] + back).astype(BF)
        return jnp.concatenate([col_sum(fg * n1), col_sum(fg)], axis=0)

    def own_chunk(k, n):
        return pl.ds(pl.multiple_of(own + n * k, n), n)

    dt_e = [
        remote("dt", dtv.at[128 * k:128 * (k + 1)], d_tok.at[own_chunk(k, 128)], x_peer, k, 2)
        for k in range(2)
    ]
    dt_n = remote("dt", dtv.at[0:NODES], d_tok.at[0:NODES], x_peer, 0, 2)
    va[...] = jnp.zeros_like(va)

    @pl.when(s == 1)
    def _():
        for k in range(2):
            fp_y[k].wait_recv()

            def edge_rows(i, carry):
                rows = pl.ds(pl.multiple_of(128 * k + 64 * i, 64), 64)
                return carry + first_rows(rows, fs[rows].astype(F32) + fy[rows].astype(F32))

            got = lax.fori_loop(0, 2, edge_rows, jnp.zeros((2, 768), F32))
            va[0:2] += got
            dt_e[k].start()

    @pl.when((s == 0) & (h == 0))
    def _():
        for k in range(2):
            fp_xn[k].wait_recv()

            def node_rows(i, carry):
                rows = pl.ds(pl.multiple_of(96 * k + 32 * i, 32), 32)
                from_fs = pl.ds(pl.multiple_of(256 + 96 * k + 32 * i, 32), 32)
                return carry + first_rows(rows, fs[from_fs].astype(F32) + fx[from_fs].astype(F32))

            got = lax.fori_loop(0, 3, node_rows, jnp.zeros((2, 768), F32))
            va[0:2] += got
        dtv[NODES:256] = mgd[NODES:256].astype(BF)
        dt_n.start()

    @pl.when((s == 0) & (h == 1))
    def _():
        dtv[...] = mgd[...].astype(BF)

    stores[1].start()

    sums = [f_gain_sum, f_shift_sum, out_bias_sum, down_bias_sum, up_bias_sum, va[0:1], va[1:2], zero_row]
    sums += [jnp.where(me == r, qkv_bias_sum, 0.0) for r in range(4)] + [zero_row] * 4
    vq[me] = jnp.concatenate(sums, axis=0)
    v1 = [remote("v_q", vq.at[me], vq.at[me], dev, k, 3) for k, dev in enumerate(quad)]
    for copy in v1:
        copy.start()

    st1[2] = g1_after_z(2)
    f1_after_z(1, st1[1])
    f1_after_y(0)
    v1_in = [
        remote("v_q", vq.at[r], vq.at[r], dev, k, 3)
        for k, (dev, r) in enumerate(zip(quad, (2 * s + 1 - h, 2 - 2 * s + h, 3 - 2 * s - h)))
    ]
    for copy in v1_in:
        copy.wait_recv()
    vz[z] = vq[0] + vq[1] + vq[2] + vq[3]
    v2 = [remote("v_z", vz.at[z], vz.at[z], z_peers[d], d, zc - 1) for d in range(zc - 1)]
    for copy in v2:
        copy.start()
    f2_after_z(1, st2[1])
    f2_after_z(2, st2[2])
    f1_after_z(2, st1[2])
    f2_after_y(0)
    f1_after_y(1)
    for copy in v2:
        copy.wait_recv()
    vsum = vz[0]
    for d in range(1, zc):
        vsum = vsum + vz[d]
    vc[c] = vsum
    v3 = remote("v_c", vc.at[c], vc.at[c], twin)
    v3.start()
    f2_after_y(1)
    f2_after_y(2)
    f1_after_y(2)
    v3.wait_recv()
    vec[...] = vc[0] + vc[1]
    for copy in (*f1_c, *f2_c):
        copy.wait_recv()
    for copy in stores[0:2]:
        copy.wait()

    @pl.when(s == 1)
    def _():
        for copy in (*dt_e, out_send):
            copy.wait()

    @pl.when(me == 0)
    def _():
        for copy in (dt_n, out_node):
            copy.wait_send()
        for copy in far:
            copy.wait()

    @pl.when(me == 1)
    def _():
        for copy in (dt_n, out_node):
            copy.wait_recv()
        for copy in near:
            copy.wait()

    @pl.when(s == 1)
    def _():
        for copy in tok_y:
            copy.wait_send()

    @pl.when(s == 0)
    def _():
        tok_n.wait_send()
        for copy in tok_x:
            copy.wait_send()

    wait_sent("att", att, ain)

    @pl.when(s == 0)
    def _():
        for copy in fp_y:
            copy.wait_send()

    @pl.when(me == 1)
    def _():
        for copy in fp_xn:
            copy.wait_send()

    @pl.when(s == 1)
    def _():
        for copy in fp_yn:
            copy.wait_send()

    @pl.when(s == 1)
    def _():
        w_out[0].wait_send()
        w_out[2].wait_send()
        w_y[0].wait_send()
        w_y[2].wait_send()

    for k, (dev_sh, first, count) in enumerate(OWNERS):
        mine = 2 * dev_sh[0] + dev_sh[1]

        @pl.when(me == mine)
        def _():
            for r in range(4):
                if r != mine:
                    i = sem_id("da_s", 4) + r
                    pltpu.make_async_remote_copy(
                        src_ref=ago.at[0:count, 0:256], dst_ref=da.at[first:first + count],
                        send_sem=ss.at[i], recv_sem=rs.at[i], device_id=x_peer, device_id_type=MESH,
                    ).wait_send()

    for copy in (
        u_send, w_out[1], *w_twin, *g1_twin, *g1_q, *g1_x[1:], *g1_y[1:], *sum(g1_z, []), *fp_x, *g2_twin,
        *sum(g2_z, []), *v1, *sum(f1_z, []), *f1_y, *f1_c, *sum(f2_z, []), *f2_y, *f2_c, *v2, v3,
    ):
        copy.wait_send()


def finish_kernel(
    tokens, cot, d_out, d_tok, f1, f2, vec,
    output, tokens_grad, a_gain, a_shift, wq, bq, wk, wv, bv, wo, bo, f_gain, f_shift, wu, bu, wd, bd,
):
    h = lax.axis_index("head")
    output[...] = tokens[...].astype(F32) + d_out[...].astype(F32)
    tokens_grad[...] = cot[...] + d_tok[...].astype(F32)
    for k in range(2):
        lanes = slice(384 * k, 384 * (k + 1))
        wd[:, lanes] = f1[0, k].astype(F32)
        wo[:, lanes] = f1[2, k].astype(F32)
        wu[k] = f1[1, k].astype(F32)
    low_half = lax.broadcasted_iota(jnp.int32, (1, 128), 1) < 64
    tile = lambda k, t: f2[k, :, 128 * t:128 * (t + 1)].astype(F32)
    for t, out in ((0, wv), (2, wq), (3, wk)):
        out[:, 0:128] = tile(0, t)
        out[:, 256:384] = tile(1, t)
    wq[:, 128:256] = jnp.where(low_half, tile(0, 4), tile(1, 4))
    wk[:, 128:256] = pltpu.roll(jnp.where(low_half, tile(1, 4), tile(0, 4)), 64, 1)
    wv[:, 128:256] = jnp.where(low_half, tile(0, 1), tile(1, 1))

    @pl.when(pl.program_id(0) == 0)
    def _():
        mine = pl.ds(pl.multiple_of(384 * h, 384), 384)
        for row, out in ((0, f_gain), (1, f_shift), (2, bo), (3, bd), (4, bu), (5, a_gain), (6, a_shift)):
            out[...] = vec[row:row + 1, mine].reshape(384)
        low = jnp.where(h == 0, vec[8:9], vec[9:10])
        high = jnp.where(h == 0, vec[10:11], vec[11:12])
        for first, out in ((0, bq), (512, bv)):
            a, b = low[:, first:first + 256], high[:, first:first + 256]
            parts = [a[:, 0:128], a[:, 128:256] + b[:, 0:128], b[:, 128:256]]
            out[...] = jnp.concatenate(parts, axis=1).reshape(384)


def fast_layer(
    tokens, cotangent, attn_gain, attn_shift, query_weight, query_bias, key_weight, value_weight,
    value_bias, out_weight, out_bias, ffn_gain, ffn_shift, up_weight, up_bias, down_weight,
    down_bias, atom_counts, edge_counts,
):
    zc = lax.axis_size("mol") // 2
    anywhere = pl.BlockSpec(memory_space=pl.ANY)
    vmem = pl.BlockSpec(memory_space=pltpu.VMEM)
    smem = pl.BlockSpec(memory_space=pltpu.SMEM)
    shape = jax.ShapeDtypeStruct
    SEM.clear()
    buf = lambda dtype, *dims: pltpu.VMEM(dims, dtype)
    scratch = [
        buf(BF, 256, 768), buf(BF, 256, 768), buf(BF, 256, 768), buf(BF, 3, 192 // zc, 384), buf(BF, 384 // zc, 640), buf(BF, TOTAL, 640),
        buf(BF, PADDED, 768), buf(BF, 256, 768), buf(F32, 256, 768), buf(BF, 768, 768),
        buf(BF, 2, 384, 768), buf(BF, 2, 768, 384), buf(BF, 2, 384, 768), buf(F32, 2, 8, 384),
        buf(BF, PADDED, 768), buf(BF, PADDED, 768), buf(BF, TOTAL, 768),
        buf(BF, HEADS_HERE, TOTAL, 256), buf(BF, HEADS_HERE, TOTAL, 256),
        buf(BF, 1024, 512), buf(BF, 1024, 512), buf(BF, 1024, 512), buf(BF, 1024, 512), buf(BF, 1536, 768),
        buf(F32, 256, 768), buf(jnp.int32, TOTAL, 1),
        buf(F32, TOTAL, 256), buf(BF, TOTAL, 256), buf(BF, 4, 256, 256), buf(BF, TOTAL, 256), buf(F32, TOTAL, 128),
        buf(F32, 256, 768), buf(F32, 256, 768), buf(F32, 256, 768), buf(F32, 256, 128), buf(F32, 256, 768),
        buf(BF, 256, 768), buf(BF, 256, 768), buf(BF, 256, 768), buf(BF, 256, 768), buf(BF, 256, 768),
        buf(BF, 256, 768), buf(BF, 256, 768), buf(F32, 256, 768),
        buf(BF, 1536, 768), buf(F32, PADDED, 256), buf(F32, PADDED, 256),
        buf(BF, 3, 2, 2, 384, 384), buf(BF, 3, 2, 384, 384), buf(BF, 3, 192, 384), buf(BF, 3, 384, 384), buf(BF, 3, 2, 384, 384),
        buf(BF, 3, 2, 192, 384), buf(BF, 3, 192, 384), buf(BF, 3, zc - 1, 192 // zc, 384),
        buf(BF, 2, 384, 640), buf(BF, 384, 640), buf(BF, zc - 1, 384 // zc, 640),
        buf(BF, TOTAL, 768), buf(BF, 256 + NODES, 768), buf(BF, 256 + NODES, 768), buf(BF, 256, 768),
        buf(F32, 8, 768), buf(F32, 4, 16, 768), buf(F32, zc, 16, 768), buf(F32, 2, 16, 768),
        pltpu.SemaphoreType.DMA((N_SEMS,)), pltpu.SemaphoreType.DMA((N_SEMS,)), pltpu.SemaphoreType.DMA((N_LOCAL,)),
    ]
    d_out, d_tok, f1, f2, vec = pl.pallas_call(
        layer_kernel,
        out_shape=[
            shape((512, 768), BF), shape((512, 768), BF), shape((3, 2, 384, 384), BF),
            shape((2, 768, 640), BF), shape((16, 768), F32),
        ],
        in_specs=[anywhere] * 8 + [smem] * 2 + [vmem] * 9,
        out_specs=[anywhere] * 4 + [vmem],
        scratch_shapes=scratch,
        compiler_params=pltpu.CompilerParams(
            collective_id=0, has_side_effects=True, vmem_limit_bytes=61 * 2**20
        ),
        name="layer",
    )(
        tokens, cotangent, query_weight, key_weight, value_weight, out_weight, up_weight, down_weight,
        atom_counts, edge_counts, attn_gain, attn_shift, query_bias, value_bias, out_bias,
        ffn_gain, ffn_shift, up_bias, down_bias,
    )
    assert sum(n for _, n in SEM.values()) <= N_SEMS
    steps = 4
    mat, tall, line = shape((384, 768), F32), shape((768, 384), F32), shape((384,), F32)
    big, pair = shape((512, 768), F32), shape((2, 384, 384), F32)
    by_rows = lambda rows, cols: pl.BlockSpec((rows // steps, cols), lambda i: (i, 0))
    big_spec, mat_spec, tall_spec = by_rows(512, 768), by_rows(384, 768), by_rows(768, 384)
    line_spec = pl.BlockSpec((384,), lambda i: (0,))
    pair_spec = pl.BlockSpec((2, 384 // steps, 384), lambda i: (0, i, 0))
    outs = pl.pallas_call(
        finish_kernel,
        grid=(steps,),
        out_shape=[big, big, line, line, tall, line, tall, tall, line, mat, line, line, line, pair, line, mat, line],
        in_specs=[
            big_spec, big_spec, big_spec, big_spec,
            pl.BlockSpec((3, 2, 384 // steps, 384), lambda i: (0, 0, i, 0)),
            pl.BlockSpec((2, 768 // steps, 640), lambda i: (0, i, 0)),
            pl.BlockSpec((16, 768), lambda i: (0, 0)),
        ],
        out_specs=[
            big_spec, big_spec, line_spec, line_spec, tall_spec, line_spec, tall_spec, tall_spec, line_spec,
            mat_spec, line_spec, line_spec, line_spec, pair_spec, line_spec, mat_spec, line_spec,
        ],
        compiler_params=pltpu.CompilerParams(vmem_limit_bytes=60 * 2**20),
        name="finish",
    )(tokens, cotangent, d_out, d_tok, f1, f2, vec)
    return tuple(o.reshape(768, 384) if o.ndim == 3 else o for o in outs)


def plain_dot(operand, partner):
    return jnp.dot(operand, partner, preferred_element_type=jnp.float32)


def lead_dot(operand, partner):
    return lax.dot_general(
        operand, partner, (((0,), (0,)), ((), ())), preferred_element_type=jnp.float32
    )


def tail_dot(operand, partner):
    return lax.dot_general(
        operand, partner, (((1,), (1,)), ((), ())), preferred_element_type=jnp.float32
    )


def norm_apply(values, gain_vec, shift_vec):
    row_mean = jnp.mean(values, axis=-1, keepdims=True)
    centered = values - row_mean
    variance = jnp.mean(centered * centered, axis=-1, keepdims=True)
    return centered * lax.rsqrt(variance + 1e-05) * gain_vec + shift_vec


def gelu_exact(values):
    return jax.nn.gelu(values, approximate=False)


def segment_ids(counts, added, slot_count):
    members = jnp.arange(counts.shape[0])
    earlier = members[:, None] <= members[None, :]
    seg_ends = jnp.sum(jnp.where(earlier, (counts + added)[:, None], 0), axis=0)
    positions = jnp.arange(slot_count, dtype=jnp.int32)
    return jnp.sum((positions[:, None] >= seg_ends[None, :]).astype(jnp.int32), axis=1)


def head_piece(vector, head_rank, head_share):
    return lax.dynamic_slice_in_dim(vector, head_rank * head_share, head_share)


def on_device(
    tokens,
    cotangent,
    attn_gain,
    attn_shift,
    query_weight,
    query_bias,
    key_weight,
    value_weight,
    value_bias,
    out_weight,
    out_bias,
    ffn_gain,
    ffn_shift,
    up_weight,
    up_bias,
    down_weight,
    down_bias,
    atom_counts,
    edge_counts,
):
    row_count = tokens.shape[0]
    model_width = tokens.shape[1]
    local_width = query_weight.shape[1]
    local_heads = local_width // HEAD_DIM
    head_count = lax.axis_size("head")
    head_rank = lax.axis_index("head")
    stream_rank = lax.axis_index("stream")
    molecules = atom_counts.shape[1]
    head_share = model_width // head_count
    score_scale = HEAD_DIM ** (-0.5)
    seg_node = segment_ids(atom_counts[0], 1, row_count)
    seg_edge = segment_ids(edge_counts[0], 0, row_count)
    key_seg = jnp.concatenate([seg_node, seg_edge])
    own_seg = jnp.where(stream_rank == 0, seg_node, seg_edge)
    live_rows = (own_seg < molecules).astype(jnp.float32)[:, None]
    residual = tokens.astype(jnp.float32)
    normed, norm_pull = jax.vjp(norm_apply, residual, attn_gain, attn_shift)
    first_in = normed.astype(jnp.bfloat16)
    queries = (plain_dot(first_in, query_weight) + query_bias).astype(jnp.bfloat16)
    keys_local = plain_dot(first_in, key_weight).astype(jnp.bfloat16)
    values_local = (plain_dot(first_in, value_weight) + value_bias).astype(jnp.bfloat16)
    all_keys, all_values = (
        lax.all_gather(keys_local, "stream", axis=0, tiled=True),
        lax.all_gather(values_local, "stream", axis=0, tiled=True),
    )
    key_count = all_keys.shape[0]
    key_heads = all_keys.reshape(key_count, local_heads, HEAD_DIM)
    value_heads = all_values.reshape(key_count, local_heads, HEAD_DIM)
    blocks = row_count // 512
    block_rows = row_count // blocks
    query_blocks = queries.reshape(blocks, block_rows, local_heads, HEAD_DIM)
    seg_blocks = own_seg.reshape(blocks, block_rows)

    def forward_block(pieces):
        query_part, seg_part = pieces
        scores = (
            jnp.einsum("qhd,khd->hqk", query_part, key_heads, preferred_element_type=jnp.float32)
            * score_scale
        )
        same_mol = (seg_part[:, None] == key_seg[None, :])[None]
        scores = jnp.where(same_mol, scores, -1e30)
        row_top = jnp.max(scores, axis=-1, keepdims=True)
        shifted = jnp.exp(scores - row_top)
        row_total = jnp.sum(shifted, axis=-1, keepdims=True)
        prob_low = (shifted / row_total).astype(jnp.bfloat16)
        attended_part = jnp.einsum(
            "hqk,khd->qhd", prob_low, value_heads, preferred_element_type=jnp.float32
        )
        return (attended_part.astype(jnp.bfloat16), (row_top + jnp.log(row_total))[..., 0])

    attended_blocks, lse_blocks = lax.map(forward_block, (query_blocks, seg_blocks))
    attended = attended_blocks.reshape(row_count, local_width)
    attn_sum = lax.psum(plain_dot(attended, out_weight), "head")
    middle = residual + live_rows * (attn_sum + out_bias)
    second, second_pull = jax.vjp(norm_apply, middle, ffn_gain, ffn_shift)
    second_in = second.astype(jnp.bfloat16)
    inner_pre = plain_dot(second_in, up_weight) + up_bias.astype(jnp.float32)
    activated, gelu_pull = jax.vjp(gelu_exact, inner_pre)
    hidden = activated.astype(jnp.bfloat16)
    ffn_sum = lax.psum(plain_dot(hidden, down_weight).astype(jnp.bfloat16), "head").astype(
        jnp.float32
    )
    output = middle + live_rows * (ffn_sum + down_bias)
    down_cot = (live_rows * cotangent).astype(jnp.bfloat16)
    down_weight_grad = lead_dot(hidden, down_cot)
    down_bias_full = jnp.sum(down_cot.astype(jnp.float32), axis=0)
    inner_grad = gelu_pull(tail_dot(down_cot, down_weight))[0].astype(jnp.bfloat16)
    up_weight_grad = lead_dot(second_in, inner_grad)
    up_bias_grad = jnp.sum(inner_grad.astype(jnp.float32), axis=0)
    second_grad = lax.psum(tail_dot(inner_grad, up_weight), "head")
    middle_part, ffn_gain_full, ffn_shift_full = second_pull(second_grad)
    mid_grad = cotangent + middle_part
    ffn_gain_grad = head_piece(ffn_gain_full, head_rank, head_share)
    ffn_shift_grad = head_piece(ffn_shift_full, head_rank, head_share)
    down_bias_grad = head_piece(down_bias_full, head_rank, head_share)
    attn_cot = (live_rows * mid_grad).astype(jnp.bfloat16)
    out_weight_grad = lead_dot(attended, attn_cot)
    out_bias_full = jnp.sum(attn_cot.astype(jnp.float32), axis=0)
    attended_grad = tail_dot(attn_cot, out_weight).astype(jnp.bfloat16)
    grad_blocks = attended_grad.reshape(blocks, block_rows, local_heads, HEAD_DIM)

    def backward_block(running, pieces):
        key_acc, value_acc = running
        query_part, seg_part, lse_part, grad_part = pieces
        scores = (
            jnp.einsum("qhd,khd->hqk", query_part, key_heads, preferred_element_type=jnp.float32)
            * score_scale
        )
        same_mol = (seg_part[:, None] == key_seg[None, :])[None]
        prob_full = jnp.where(same_mol, jnp.exp(scores - lse_part[..., None]), 0.0)
        prob_low = prob_full.astype(jnp.bfloat16)
        prob_grad = jnp.einsum(
            "qhd,khd->hqk", grad_part, value_heads, preferred_element_type=jnp.float32
        )
        row_delta = jnp.sum(prob_grad * prob_full, axis=-1, keepdims=True)
        score_grad = (prob_full * (prob_grad - row_delta)).astype(jnp.bfloat16)
        query_part_grad = (
            jnp.einsum("hqk,khd->qhd", score_grad, key_heads, preferred_element_type=jnp.float32)
            * score_scale
        )
        key_acc = (
            key_acc
            + jnp.einsum("hqk,qhd->khd", score_grad, query_part, preferred_element_type=jnp.float32)
            * score_scale
        )
        value_acc = value_acc + jnp.einsum(
            "hqk,qhd->khd", prob_low, grad_part, preferred_element_type=jnp.float32
        )
        return ((key_acc, value_acc), query_part_grad.astype(jnp.bfloat16))

    zero_keys = jnp.zeros((key_count, local_heads, HEAD_DIM), jnp.float32)
    (key_acc, value_acc), query_grads = lax.scan(
        backward_block, (zero_keys, zero_keys), (query_blocks, seg_blocks, lse_blocks, grad_blocks)
    )
    key_sum, value_sum = (
        lax.psum_scatter(
            key_acc.reshape(key_count, local_width), "stream", scatter_dimension=0, tiled=True
        ),
        lax.psum_scatter(
            value_acc.reshape(key_count, local_width), "stream", scatter_dimension=0, tiled=True
        ),
    )
    key_grad = key_sum.astype(jnp.bfloat16)
    value_grad = value_sum.astype(jnp.bfloat16)
    query_grad = query_grads.reshape(row_count, local_width)
    query_weight_grad = lead_dot(first_in, query_grad)
    query_bias_grad = jnp.sum(query_grad.astype(jnp.float32), axis=0)
    key_weight_grad = lead_dot(first_in, key_grad)
    value_weight_grad = lead_dot(first_in, value_grad)
    value_bias_grad = jnp.sum(value_grad.astype(jnp.float32), axis=0)
    first_part = (
        tail_dot(query_grad, query_weight)
        + tail_dot(key_grad, key_weight)
        + tail_dot(value_grad, value_weight)
    )
    first_grad = lax.psum(first_part.astype(jnp.bfloat16), "head").astype(jnp.float32)
    resid_part, attn_gain_full, attn_shift_full = norm_pull(first_grad)
    tokens_grad = mid_grad + resid_part
    attn_gain_grad = head_piece(attn_gain_full, head_rank, head_share)
    attn_shift_grad = head_piece(attn_shift_full, head_rank, head_share)
    out_bias_grad = head_piece(out_bias_full, head_rank, head_share)
    (
        attn_gain_grad,
        attn_shift_grad,
        query_weight_grad,
        query_bias_grad,
        key_weight_grad,
        value_weight_grad,
        value_bias_grad,
        out_weight_grad,
        out_bias_grad,
        ffn_gain_grad,
        ffn_shift_grad,
        up_weight_grad,
        up_bias_grad,
        down_weight_grad,
        down_bias_grad,
    ) = lax.psum(
        (
            attn_gain_grad,
            attn_shift_grad,
            query_weight_grad,
            query_bias_grad,
            key_weight_grad,
            value_weight_grad,
            value_bias_grad,
            out_weight_grad,
            out_bias_grad,
            ffn_gain_grad,
            ffn_shift_grad,
            up_weight_grad,
            up_bias_grad,
            down_weight_grad,
            down_bias_grad,
        ),
        ("mol", "stream"),
    )
    return (
        output,
        tokens_grad,
        attn_gain_grad,
        attn_shift_grad,
        query_weight_grad,
        query_bias_grad,
        key_weight_grad,
        value_weight_grad,
        value_bias_grad,
        out_weight_grad,
        out_bias_grad,
        ffn_gain_grad,
        ffn_shift_grad,
        up_weight_grad,
        up_bias_grad,
        down_weight_grad,
        down_bias_grad,
    )


def solution(mesh):
    in_specs = (
        P(("mol", "stream"), None),
        P(("mol", "stream"), None),
        P(),
        P(),
        P(None, "head"),
        P("head"),
        P(None, "head"),
        P(None, "head"),
        P("head"),
        P("head", None),
        P(),
        P(),
        P(),
        P(None, "head"),
        P("head"),
        P("head", None),
        P(),
        P("mol", None),
        P("mol", None),
    )
    out_specs = (
        P(("mol", "stream"), None),
        P(("mol", "stream"), None),
        P("head"),
        P("head"),
        P(None, "head"),
        P("head"),
        P(None, "head"),
        P(None, "head"),
        P("head"),
        P("head", None),
        P("head"),
        P("head"),
        P("head"),
        P(None, "head"),
        P("head"),
        P("head", None),
        P("head"),
    )
    one_chip_pair = (
        mesh.shape["head"] == 2 and mesh.shape["stream"] == 2 and mesh.shape["mol"] == 8
    )
    return jax.shard_map(
        fast_layer if one_chip_pair else on_device, mesh=mesh, in_specs=in_specs, out_specs=out_specs, check_vma=False
    )
```

```python
import functools
import math

import jax
import jax.numpy as jnp
from jax import lax
from jax.experimental import pallas as pl
from jax.experimental.pallas import tpu as pltpu
from jax.sharding import PartitionSpec as P

HEAD_DIM = 24
BF = jnp.bfloat16
F32 = jnp.float32
MESH = pl.DeviceIdType.MESH
EDGES = 512
NODES = 192
TOTAL = EDGES + NODES
PADDED = 768
HEADS_HERE = 8
SCALE = HEAD_DIM ** (-0.5)
SCALE2 = SCALE * math.log2(math.e)
BLOCKS = (
    (0, 128, ((0, 256), (512, 256))),
    (128, 128, ((64, 256), (512, 256))),
    (256, 128, ((192, 256), (512, 256))),
    (384, 128, ((256, 256), (512, 256))),
    (512, 192, ((0, 768),)),
)
OWNERS = (((0, 0), 512, 192), ((1, 0), 0, 256), ((1, 1), 256, 256))


def nn(a, b):
    return jnp.dot(a, b, preferred_element_type=F32)


def nt(a, b):
    return lax.dot_general(a, b, (((1,), (1,)), ((), ())), preferred_element_type=F32)


def tn(a, b):
    return lax.dot_general(a, b, (((0,), (0,)), ((), ())), preferred_element_type=F32)


def row_loop(count, step, fn, init):
    def body(i, carry):
        return fn(pl.ds(pl.multiple_of(i * step, step), step), carry)

    return lax.fori_loop(0, count // step, body, init)


def normed(x):
    mu = jnp.mean(x, axis=-1, keepdims=True)
    xc = x - mu
    var = jnp.mean(xc * xc, axis=-1, keepdims=True)
    r = lax.rsqrt(var + 1e-05)
    return xc * r, r


def col_sum(x):
    return jnp.sum(x, axis=0, keepdims=True)


SEM = {}


def sem_id(name, count=1):
    if name not in SEM:
        SEM[name] = sum(n for _, n in SEM.values()), count
    return SEM[name][0]


N_SEMS = 160
N_LOCAL = 24


def layer_kernel(
    tokens, cot, wq, wk, wv, wo, wu, wd,
    atoms, edges,
    a_gain_v, a_shift_v, q_bias_v, v_bias_v, o_bias_v, f_gain_v, f_shift_v, u_bias_v, d_bias_v,
    d_out, d_tok, f1, f2, vec,
    dov, dtv, zb, fz1, fz2, dxp, tok, res, cotv, ww, fwo, fwu, fwd, ub, fin1, qkv, dxw, qm, dam,
    p0, p1, p2, p3, p4, bias, segc, attf, att, ain, da, delta,
    t0, t1, n2s, r2s, mid, sec, hid, dc, ig, ac, ato, ago, mgd,
    ds, dkf, dvf,
    g1, gs1, qr, xr, gx, yr, gq, zr1, g2, gs2, zr2, fp, fx, fs, fy,
    va, vq, vz, vc,
    ss, rs, ls,
):
    m, s, h = lax.axis_index("mol"), lax.axis_index("stream"), lax.axis_index("head")
    z, c = m // 2, lax.rem(m, 2)
    zc = lax.axis_size("mol") // 2
    me = 2 * s + h
    x_peer, y_peer, xy_peer = (m, s, 1 - h), (m, 1 - s, h), (m, 1 - s, 1 - h)
    quad = (x_peer, y_peer, xy_peer)
    twin = (2 * z + 1 - c, s, h)
    z_peers = [(2 * lax.rem(z + d, zc) + c, s, h) for d in range(1, zc)]

    def remote(name, src, dst, dev, k=0, count=1):
        i = sem_id(name, count) + k
        return pltpu.make_async_remote_copy(
            src_ref=src, dst_ref=dst, send_sem=ss.at[i], recv_sem=rs.at[i],
            device_id=dev, device_id_type=MESH,
        )

    def as_row(ref):
        return ref[...].astype(F32).reshape(1, -1)

    a_gain, a_shift, f_gain, f_shift = (as_row(r) for r in (a_gain_v, a_shift_v, f_gain_v, f_shift_v))
    o_bias, d_bias, q_bias, v_bias = (as_row(r) for r in (o_bias_v, d_bias_v, q_bias_v, v_bias_v))

    def local(k, src, dst):
        return pltpu.make_async_copy(src, dst, ls.at[k])

    own = pl.multiple_of(256 * h, 256)
    other = pl.multiple_of(256 * (1 - h), 256)
    window = pl.multiple_of(128 * s, 128)

    loads = [
        local(0, tokens.at[pl.ds(own, 256)], res),
        local(1, cot.at[pl.ds(own, 256)], cotv),
        local(2, wq.at[:, pl.ds(window, 256)], ww.at[:, 0:256]),
        local(3, wk.at[:, pl.ds(window, 256)], ww.at[:, 256:512]),
        local(4, wv.at[:, pl.ds(window, 256)], ww.at[:, 512:768]),
        local(5, wo, fwo.at[h]),
        local(6, wu, fwu.at[h]),
        local(7, wd, fwd.at[h]),
    ]
    edge_load = local(8, tokens, tok.at[0:EDGES])
    node_load = local(9, tokens.at[0:NODES], tok.at[EDGES:TOTAL])
    pl.when(s == 1)(edge_load.start)
    pl.when(s == 0)(node_load.start)
    for copy in loads:
        copy.start()
    ub[h] = jnp.broadcast_to(as_row(u_bias_v), (8, 384))

    barrier = pltpu.get_barrier_semaphore()
    greeted = [*quad, twin, *z_peers]
    for dev in greeted:
        pl.semaphore_signal(barrier, inc=1, device_id=dev, device_id_type=MESH)
    pl.semaphore_wait(barrier, len(greeted))

    def edge_part(k, half):
        rows = pl.ds(pl.multiple_of(256 * half + 64 * k, 64), 64)
        return rows

    tok_y = [
        remote("tok_y", tokens.at[edge_part(k, h)], tok.at[edge_part(k, h)], y_peer, k, 4)
        for k in range(4)
    ]
    tok_x = [
        remote("tok_x", tok.at[edge_part(k, h)], tok.at[edge_part(k, h)], x_peer, k, 4)
        for k in range(4)
    ]
    tok_x_in = [
        remote("tok_x", tok.at[edge_part(k, 1 - h)], tok.at[edge_part(k, 1 - h)], x_peer, k, 4)
        for k in range(4)
    ]
    tok_n = remote("tok_n", tokens.at[0:NODES], tok.at[EDGES:TOTAL], y_peer)

    @pl.when(s == 1)
    def _():
        for copy in tok_y:
            copy.start()

    pl.when(s == 0)(tok_n.start)
    u_send = remote("ub", ub.at[h], ub.at[h], x_peer)
    u_send.start()
    part_o = pl.ds(pl.multiple_of(192 * c, 192), 192)
    part_u = pl.ds(pl.multiple_of(384 * c, 384), 384)
    w_out = [
        remote("wo_x", wo.at[part_o], fwo.at[h, part_o], x_peer),
        remote("wu_x", wu.at[part_u], fwu.at[h, part_u], x_peer),
        remote("wd_x", wd.at[part_o], fwd.at[h, part_o], x_peer),
    ]

    @pl.when(s == 1)
    def _():
        for k in (0, 2, 1):
            w_out[k].start()

    w_in = [
        remote("wo_x", wo.at[part_o], fwo.at[1 - h, part_o], x_peer),
        remote("wu_x", wu.at[part_u], fwu.at[1 - h, part_u], x_peer),
        remote("wd_x", wd.at[part_o], fwd.at[1 - h, part_o], x_peer),
    ]
    w_twin = [
        remote("wo_c", fwo.at[1 - h, part_o], fwo.at[1 - h, part_o], twin),
        remote("wu_c", fwu.at[1 - h, part_u], fwu.at[1 - h, part_u], twin),
        remote("wd_c", fwd.at[1 - h, part_o], fwd.at[1 - h, part_o], twin),
    ]

    w_y = {
        0: remote("wo_y", fwo.at[1 - h, part_o], fwo.at[1 - h, part_o], y_peer),
        2: remote("wd_y", fwd.at[1 - h, part_o], fwd.at[1 - h, part_o], y_peer),
    }

    def pass_weight(k):
        w_in[k].wait_recv()
        w_y[k].start()
        w_twin[k].start()

    def share_weight(k):
        w_in[k].wait_recv()
        w_twin[k].start()

    def take_weight(k):
        w_y[k].wait_recv()
        w_twin[k].start()

    def ends_of(counts, added):
        total, ends = 0, []
        for j in range(counts.shape[1]):
            total = total + counts[0, j] + added
            ends.append(total)
        return ends

    node_ends, edge_ends = ends_of(atoms, 1), ends_of(edges, 0)
    live_count = jnp.where(s == 0, node_ends[-1], edge_ends[-1])

    def seg_of(position, ends):
        seg = jnp.zeros_like(position)
        for end in ends:
            seg = seg + jnp.where(position >= end, 1, 0)
        return seg

    segc[0:EDGES] = seg_of(lax.broadcasted_iota(jnp.int32, (EDGES, 1), 0), edge_ends)
    segc[EDGES:TOTAL] = seg_of(lax.broadcasted_iota(jnp.int32, (NODES, 1), 0), node_ends)
    at_row = lax.broadcasted_iota(jnp.int32, (1, PADDED), 1)
    seg_r = jnp.where(at_row < EDGES, seg_of(at_row, edge_ends), seg_of(at_row - EDGES, node_ends))
    seg_r = jnp.where(at_row < TOTAL, seg_r, -1)

    lane = lax.broadcasted_iota(jnp.int32, (1, 256), 1) - 64 * s
    head_of = jnp.where((lane >= 0) & (lane < 192), lane // HEAD_DIM, -1)
    zero = jnp.zeros((), BF)

    qkv[TOTAL:PADDED] = jnp.zeros((PADDED - TOTAL, 768), BF)
    bias_row = jnp.concatenate(
        [
            jnp.where(s == 0, q_bias[:, 0:256], q_bias[:, 128:384]),
            jnp.zeros((1, 256), F32),
            jnp.where(s == 0, v_bias[:, 0:256], v_bias[:, 128:384]),
        ],
        axis=1,
    )

    for who, slot in ((0, qr.at[0]), (3, qr.at[1]), (2, qr.at[2]), (3, yr.at[1, 0]), (3, yr.at[1, 1]), (0, xr.at[2])):

        @pl.when(me == who)
        def _():
            slot[...] = jnp.zeros_like(slot)

    def project(first, count):
        def norm_rows(i, carry):
            rows = pl.ds(pl.multiple_of(first + i * 64, 64), 64)
            n1, _ = normed(tok[rows].astype(F32))
            fin1[rows] = (n1 * a_gain + a_shift).astype(BF)
            return carry

        lax.fori_loop(0, count // 64, norm_rows, 0)
        rows = pl.ds(pl.multiple_of(first, 64), count)
        qkv[rows] = (nn(fin1[rows], ww[...]) + bias_row).astype(BF)

    for copy in loads[2:5]:
        copy.wait()

    @pl.when(s == 1)
    def _():
        edge_load.wait()
        project(0, EDGES)
        tok_n.wait_recv()
        project(EDGES, NODES)
        pass_weight(0)

    @pl.when(s == 0)
    def _():
        node_load.wait()
        project(EDGES, NODES)
        for k in range(4):
            tok_y[k].wait_recv()
            tok_x[k].start()
        w_out[1].start()
        project(own, 256)
        for k in range(4):
            tok_x_in[k].wait_recv()
        project(other, 256)

    for j in range(HEADS_HERE):
        qm[j] = jnp.where(head_of == j, qkv[0:TOTAL, 0:256], zero)

    def send_rows(name, src, dst, k):
        dev_sh, first, count = OWNERS[k]
        target = (m, *dev_sh)
        mine = 2 * dev_sh[0] + dev_sh[1]

        @pl.when(me != mine)
        def _():
            i = sem_id(name + "_s", 3) + k
            j = sem_id(name, 4) + me
            pltpu.make_async_remote_copy(
                src_ref=src.at[first:first + count], dst_ref=dst.at[me, 0:count],
                send_sem=ss.at[i], recv_sem=rs.at[j], device_id=target, device_id_type=MESH,
            ).start()

        @pl.when(me == mine)
        def _():
            dst[mine, 0:count] = src[first:first + count]

    def wait_rows(name, src, dst):
        for k, (dev_sh, first, count) in enumerate(OWNERS):
            mine = 2 * dev_sh[0] + dev_sh[1]

            @pl.when(me == mine)
            def _():
                for r in range(4):
                    if r != mine:
                        j = sem_id(name, 4) + r
                        pltpu.make_async_remote_copy(
                            src_ref=src.at[first:first + count], dst_ref=dst.at[r, 0:count],
                            send_sem=ss.at[j], recv_sem=rs.at[j], device_id=x_peer, device_id_type=MESH,
                        ).wait_recv()

    def wait_sent(name, src, dst):
        for k, (dev_sh, first, count) in enumerate(OWNERS):
            mine = 2 * dev_sh[0] + dev_sh[1]

            @pl.when(me != mine)
            def _():
                i = sem_id(name + "_s", 3) + k
                pltpu.make_async_remote_copy(
                    src_ref=src.at[first:first + count], dst_ref=dst.at[me, 0:count],
                    send_sem=ss.at[i], recv_sem=rs.at[i], device_id=(m, *dev_sh), device_id_type=MESH,
                ).wait_send()

    def pick_heads(stacked, rows):
        total = None
        for j in range(HEADS_HERE):
            part = jnp.where(head_of == j, stacked[j * rows:(j + 1) * rows], 0.0)
            total = part if total is None else total + part
        return total

    probs = (p0, p1, p2, p3, p4)
    to_owner = (None, 1, None, 2, 0)
    group = 4

    @pl.when(s == 0)
    def _():
        ain[:, NODES:256] = jnp.zeros((4, 256 - NODES, 256), BF)

    @pl.when((s == 0) & (h == 1))
    def _():
        ain[:, 0:NODES] = jnp.zeros((4, NODES, 256), BF)

    for b, (q0, qn, segs) in enumerate(BLOCKS):
        o = 0
        for a, n in segs:
            bias[0:qn, o:o + n] = jnp.where(segc[q0:q0 + qn] == seg_r[:, a:a + n], 0.0, -1e30)
            o += n
        for j0 in range(0, HEADS_HERE, group):
            qb = qm[j0:j0 + group, q0:q0 + qn, :].reshape(group * qn, 256)
            raw = [nt(qb, qkv[a:a + n, 256:512]) for a, n in segs]
            for g in range(group):
                j, o, parts = j0 + g, 0, []
                for piece, (a, n) in zip(raw, segs):
                    parts.append(piece[g * qn:(g + 1) * qn] * SCALE2 + bias[0:qn, o:o + n])
                    o += n
                top = functools.reduce(
                    jnp.maximum, [jnp.max(x, axis=1, keepdims=True) for x in parts]
                )
                parts = [jnp.exp2(x - top) for x in parts]
                inv = 1.0 / sum(jnp.sum(x, axis=1, keepdims=True) for x in parts)
                o = 0
                for x, (a, n) in zip(parts, segs):
                    probs[b][j * qn:(j + 1) * qn, o:o + n] = (x * inv).astype(BF)
                    o += n
        o, acc = 0, None
        for a, n in segs:
            part = nn(probs[b][:, o:o + n], qkv[a:a + n, 512:768])
            acc = part if acc is None else acc + part
            o += n
        picked = pick_heads(acc, qn)
        attf[q0:q0 + qn] = picked
        att[q0:q0 + qn] = picked.astype(BF)
        if to_owner[b] is not None:
            send_rows("att", att, ain, to_owner[b])

    @pl.when(s == 1)
    def _():
        pass_weight(2)

    @pl.when(s == 0)
    def _():
        take_weight(0)

    share_weight(1)

    cut = [slice(0, 384), slice(384, 768)]
    g1_of = (
        lambda cc, xh: tn(hid[:, cut[xh]], dc[:, cut[cc]]),
        lambda cc, xh: tn(sec[:, cut[cc]], ig[:, cut[xh]]),
        lambda cc, xh: tn(ato[:, cut[xh]], ac[:, cut[cc]]),
    )
    g1_twin = [remote("g1_c", g1.at[p, 1 - c], gs1.at[p], twin, p, 3) for p in range(3)]

    def g1_compute(p):
        for cc in range(2):
            for xh in range(2):
                g1[p, cc, xh] = g1_of[p](cc, xh).astype(BF)
        g1_twin[p].start()

    rows_y = pl.ds(pl.multiple_of(192 * (1 - s), 192), 192)
    rows_s = pl.ds(pl.multiple_of(192 * s, 192), 192)
    y_first = (None, True, False)
    g1_q = [
        remote("g1_q", gs1.at[0, 1 - h, rows_s], qr.at[0], x_peer, 0, 3),
        remote("g1_q", gs1.at[0, h, rows_y], qr.at[1], y_peer, 1, 3),
        remote("g1_q", gs1.at[0, 1 - h, rows_y], qr.at[2], xy_peer, 2, 3),
    ]
    g1_x = [
        remote("g1_x", gx.at[p, 1 - h, 0:192], xr.at[p, 0:192], x_peer, p, 3)
        if y_first[p] else remote("g1_x", gs1.at[p, 1 - h], xr.at[p], x_peer, p, 3)
        for p in range(3)
    ]
    g1_y = [
        remote("g1_y", gs1.at[p, :, rows_y], yr.at[p], y_peer, p, 3)
        if y_first[p] else remote("g1_y", gx.at[p, 0, rows_y], yr.at[p, 0], y_peer, p, 3)
        for p in range(3)
    ]
    zn1, zn2 = 192 // zc, 384 // zc

    def chunk(t, n):
        return pl.ds(pl.multiple_of(n * t, n), n)

    g1_z = [
        [
            remote("g1_z", gq.at[p, chunk(lax.rem(z + d, zc), zn1)], zr1.at[p, d - 1], z_peers[d - 1],
                   p * (zc - 1) + d - 1, 3 * (zc - 1))
            for d in range(1, zc)
        ]
        for p in range(3)
    ]

    def add_into(dst, *terms):
        x = terms[0].astype(F32)
        for t in terms[1:]:
            x = x + t.astype(F32)
        dst[...] = x.astype(BF)

    def g1_after_twin(p):
        g1_twin[p].wait_recv()
        for xh in range(2):
            add_into(gs1.at[p, xh], g1[p, c, xh], gs1[p, xh])

    def g1_after_quad():
        for copy, without in zip(g1_q, (0, 3, 2)):
            pl.when(me != without)(copy.wait_recv)
        add_into(gq.at[0], gs1[0, h, rows_s], qr[0], qr[1], qr[2])
        for copy in g1_z[0]:
            copy.start()

    def g1_after_x(p):
        if y_first[p]:
            g1_x[p].wait_recv()
        else:
            pl.when(me != 0)(g1_x[p].wait_recv)
        if y_first[p]:
            add_into(gq.at[p], gx[p, h, 0:192], xr[p, 0:192])
            for copy in g1_z[p]:
                copy.start()
        else:
            add_into(gx.at[p, 0], gs1[p, h], xr[p])
            g1_y[p].start()

    def g1_after_y(p):
        if y_first[p]:
            pl.when(me != 3)(g1_y[p].wait_recv)
        else:
            g1_y[p].wait_recv()
        if y_first[p]:
            for xh in range(2):
                add_into(gx.at[p, xh, 0:192], gs1[p, xh, rows_s], yr[p, xh])
            g1_x[p].start()
        else:
            add_into(gq.at[p], gx[p, 0, rows_s], yr[p, 0])
            for copy in g1_z[p]:
                copy.start()

    for copy in (loads[0], loads[1], *loads[5:8]):
        copy.wait()
    row_at = lax.broadcasted_iota(jnp.int32, (256, 1), 0) + own
    live_all = jnp.where(row_at < live_count, 1.0, 0.0)
    r2s[:, 1:2] = live_all
    wait_rows("att", att, ain)
    for x in range(2):
        ato[:, 384 * x:384 * x + 128] = ain[x, :, 0:128]
        ato[:, 384 * x + 128:384 * x + 256] = ain[x, :, 128:256] + ain[2 + x, :, 0:128]
        ato[:, 384 * x + 256:384 * x + 384] = ain[2 + x, :, 128:256]
    twin_o = pl.ds(pl.multiple_of(192 * (1 - c), 192), 192)
    twin_u = pl.ds(pl.multiple_of(384 * (1 - c), 384), 384)
    w_twin_in = [
        remote("wo_c", fwo.at[1 - h, twin_o], fwo.at[1 - h, twin_o], twin),
        remote("wu_c", fwu.at[1 - h, twin_u], fwu.at[1 - h, twin_u], twin),
        remote("wd_c", fwd.at[1 - h, twin_o], fwd.at[1 - h, twin_o], twin),
    ]
    w_twin_in[0].wait_recv()
    wo_all = fwo[...].reshape(768, 768)
    t0[...] = nn(ato[...], wo_all)
    pl.when(s == 0)(lambda: take_weight(2))
    live_of = lambda rows: r2s[rows, 1:2]

    def middle_rows(rows, carry):
        x = res[rows].astype(F32) + live_of(rows) * (t0[rows] + o_bias)
        mid[rows] = x
        n2, r2 = normed(x)
        n2s[rows] = n2
        r2s[rows, 0:1] = r2
        sec[rows] = (n2 * f_gain + f_shift).astype(BF)
        return carry

    row_loop(256, 64, middle_rows, 0)
    w_twin_in[1].wait_recv()
    u_recv = remote("ub", ub.at[1 - h], ub.at[1 - h], x_peer)
    u_recv.wait_recv()
    for x in range(2):
        t0[:, 384 * x:384 * (x + 1)] = nn(sec[...], fwu[x]) + ub[x, 0:1]

    def gelu_rows(rows, carry):
        u = t0[rows]
        cdf = 0.5 * (1.0 + lax.erf(u * math.sqrt(0.5)))
        hid[rows] = (u * cdf).astype(BF)
        t1[rows] = cdf + u * (jnp.exp(-0.5 * u * u) * (1.0 / math.sqrt(2.0 * math.pi)))
        return carry

    row_loop(256, 64, gelu_rows, 0)
    w_twin_in[2].wait_recv()
    wd_all = fwd[...].reshape(768, 768)
    t0[...] = nn(hid[...], wd_all)
    zero_row = jnp.zeros((1, 768), F32)

    def out_rows(rows, carry):
        live = live_of(rows)
        x = (mid[rows] + live * (t0[rows] + d_bias)) - res[rows].astype(F32)
        dov[rows] = x.astype(BF)
        down = (live * cotv[rows]).astype(BF)
        dc[rows] = down
        return carry + col_sum(down.astype(F32))

    down_bias_sum = row_loop(256, 64, out_rows, zero_row)
    own_rows = pl.ds(own, 256)
    other_rows = pl.ds(other, 256)
    out_send = remote("out", dov, d_out.at[own_rows], x_peer)
    out_node = remote("out", dov.at[0:NODES], d_out.at[0:NODES], x_peer)
    g1_compute(0)
    stores = [local(10, dov, d_out.at[own_rows])]
    stores[0].start()
    zb[...] = jnp.zeros_like(zb)
    far = [local(18 + k, zb, ref.at[256:512]) for k, ref in enumerate((d_out, d_tok))]
    near = [local(18 + k, zb.at[NODES:256], ref.at[NODES:256]) for k, ref in enumerate((d_out, d_tok))]

    @pl.when(me == 0)
    def _():
        for copy in far:
            copy.start()

    @pl.when(me == 1)
    def _():
        for copy in near:
            copy.start()

    t0[...] = nt(dc[...], wd_all)

    def inner_rows(rows, carry):
        x = (t0[rows] * t1[rows]).astype(BF)
        ig[rows] = x
        return carry + col_sum(x.astype(F32))

    up_bias_sum = row_loop(256, 64, inner_rows, zero_row)
    t0[...] = nt(ig[:, 0:384], fwu[0]) + nt(ig[:, 384:768], fwu[1])

    def second_rows(rows, carry):
        gain_sum, shift_sum, bias_sum = carry
        sg, n2 = t0[rows], n2s[rows]
        g = sg * f_gain
        back = r2s[rows, 0:1] * (
            g - jnp.mean(g, axis=-1, keepdims=True) - n2 * jnp.mean(g * n2, axis=-1, keepdims=True)
        )
        mgd[rows] = back
        x = (live_of(rows) * (cotv[rows] + back)).astype(BF)
        ac[rows] = x
        return gain_sum + col_sum(sg * n2), shift_sum + col_sum(sg), bias_sum + col_sum(x.astype(F32))

    f_gain_sum, f_shift_sum, out_bias_sum = row_loop(
        256, 64, second_rows, (zero_row, zero_row, zero_row)
    )
    ago[...] = nt(ac[...], wo_all).astype(BF)

    for k, (dev_sh, first, count) in enumerate(OWNERS):
        mine = 2 * dev_sh[0] + dev_sh[1]

        @pl.when(me == mine)
        def _():
            for r in range(4):
                cols = slice(384 * (r % 2) + 128 * (r // 2), 384 * (r % 2) + 128 * (r // 2) + 256)
                if r == mine:
                    da[first:first + count] = ago[0:count, cols]
                else:
                    i, j = sem_id("da_s", 4) + r, sem_id("da", 3) + k
                    pltpu.make_async_remote_copy(
                        src_ref=ago.at[0:count, cols], dst_ref=da.at[first:first + count],
                        send_sem=ss.at[i], recv_sem=rs.at[j],
                        device_id=(m, r // 2, r % 2), device_id_type=MESH,
                    ).start()

    g1_compute(1)
    g1_compute(2)
    for p in range(3):
        g1_after_twin(p)

    for k, (dev_sh, first, count) in enumerate(OWNERS):
        mine = 2 * dev_sh[0] + dev_sh[1]

        @pl.when(me != mine)
        def _():
            j = sem_id("da", 3) + k
            pltpu.make_async_remote_copy(
                src_ref=ago.at[0:count, 0:256], dst_ref=da.at[first:first + count],
                send_sem=ss.at[j], recv_sem=rs.at[j], device_id=x_peer, device_id_type=MESH,
            ).wait_recv()

    @pl.when(me != 1)
    def _():
        for copy in (*g1_q, g1_y[1], g1_x[2]):
            copy.start()

    head_col = lax.broadcasted_iota(jnp.int32, (256, 128), 1)
    lane_row = lax.broadcasted_iota(jnp.int32, (256, 128), 0) - 64 * s
    head_pick = jnp.where(
        (lane_row >= 0) & (lane_row < 192) & (lane_row // HEAD_DIM == head_col), 1.0, 0.0
    ).astype(BF)
    prod = da[0:TOTAL].astype(F32) * attf[...]
    prod_hi = prod.astype(BF)
    delta[...] = nn(prod_hi, head_pick) + nn((prod - prod_hi.astype(F32)).astype(BF), head_pick)
    for j in range(HEADS_HERE):
        dam[j] = jnp.where(head_of == j, da[0:TOTAL], zero)
    dkf[...] = jnp.zeros_like(dkf)
    dvf[...] = jnp.zeros_like(dvf)
    for (q0, qn, segs), pr in zip(BLOCKS, probs):
        o = 0
        for a, n in segs:
            dv = None
            for j in range(HEADS_HERE):
                pv = tn(pr[j * qn:(j + 1) * qn, o:o + n], dam[j, q0:q0 + qn])
                dv = pv if dv is None else dv + pv
            dvf[a:a + n] += dv
            o += n
    dxw[:, 512:768] = dvf[0:TOTAL].astype(BF)

    lanes2 = [slice(0, 256), slice(256, 512), slice(512, 640)]
    g2_twin = [
        remote("g2_c", g2.at[1 - c, :, lanes2[p]], gs2.at[:, lanes2[p]], twin, p, 3) for p in range(3)
    ]
    g2_z = [
        [
            remote("g2_z", gs2.at[chunk(lax.rem(z + d, zc), zn2), lanes2[p]], zr2.at[d - 1, :, lanes2[p]],
                   z_peers[d - 1], p * (zc - 1) + d - 1, 3 * (zc - 1))
            for d in range(1, zc)
        ]
        for p in range(3)
    ]

    def tiles_of(k):
        first = dxw[:, 256 * k:256 * k + 128]
        last = dxw[:, 256 * k + 128:256 * k + 256]
        return jnp.where(s == 0, first, last), jnp.where(s == 0, last, first)

    def g2_compute(p):
        for cc in range(2):
            g2[cc, :, lanes2[p]] = tn(fin1[0:TOTAL, cut[cc]], dxp[:, lanes2[p]]).astype(BF)
        g2_twin[p].start()

    def g2_after_twin(p):
        g2_twin[p].wait_recv()
        add_into(gs2.at[:, lanes2[p]], g2[c, :, lanes2[p]], gs2[:, lanes2[p]])
        for copy in g2_z[p]:
            copy.start()

    stores.append(local(11, dtv, d_tok.at[own_rows]))
    st1, st2 = [None] * 3, [None] * 3
    f1_z, f1_y, f1_c, f2_z, f2_y, f2_c = [], [], [], [], [], []

    def f1_at(p, cc, ss_, zz):
        return f1.at[p, cc, pl.ds(pl.multiple_of(192 * ss_ + zn1 * zz, 16), zn1)]

    def f1_half(p, ss_):
        return f1.at[p, c, pl.ds(pl.multiple_of(192 * ss_, 192), 192)]

    def f2_at(p, cc, ss_, zz):
        return f2.at[ss_, pl.ds(pl.multiple_of(384 * cc + zn2 * zz, 16), zn2), lanes2[p]]

    def f2_half(p, ss_):
        return f2.at[ss_, pl.ds(pl.multiple_of(384 * c, 384), 384), lanes2[p]]

    def g1_after_z(p):
        for copy in g1_z[p]:
            copy.wait_recv()
        add_into(fz1.at[p], gq[p, chunk(z, zn1)], *[zr1[p, d] for d in range(zc - 1)])
        f1_z.append([
            remote("f1_z", fz1.at[p], f1_at(p, c, s, z), z_peers[d], p * (zc - 1) + d, 3 * (zc - 1))
            for d in range(zc - 1)
        ])
        for copy in f1_z[p]:
            copy.start()
        stores.append(local(12 + p, fz1.at[p], f1_at(p, c, s, z)))
        stores[-1].start()
        return stores[-1]

    def f1_after_z(p, store):
        for copy in f1_z[p]:
            copy.wait_recv()
        store.wait()
        f1_y.append(remote("f1_y", f1_half(p, s), f1_half(p, s), y_peer, p, 3))
        f1_c.append(remote("f1_c", f1_half(p, s), f1_half(p, s), twin, 2 * p, 6))
        f1_y[p].start()
        f1_c[-1].start()

    def f1_after_y(p):
        f1_y[p].wait_recv()
        f1_c.append(remote("f1_c", f1_half(p, 1 - s), f1_half(p, 1 - s), twin, 2 * p + 1, 6))
        f1_c[-1].start()

    def g2_after_z(p):
        for copy in g2_z[p]:
            copy.wait_recv()
        add_into(
            fz2.at[:, lanes2[p]], gs2[chunk(z, zn2), lanes2[p]], *[zr2[d, :, lanes2[p]] for d in range(zc - 1)]
        )
        f2_z.append([
            remote("f2_z", fz2.at[:, lanes2[p]], f2_at(p, c, s, z), z_peers[d], p * (zc - 1) + d, 3 * (zc - 1))
            for d in range(zc - 1)
        ])
        for copy in f2_z[p]:
            copy.start()
        stores.append(local(15 + p, fz2.at[:, lanes2[p]], f2_at(p, c, s, z)))
        stores[-1].start()
        return stores[-1]

    def f2_after_z(p, store):
        for copy in f2_z[p]:
            copy.wait_recv()
        store.wait()
        f2_y.append(remote("f2_y", f2_half(p, s), f2_half(p, s), y_peer, p, 3))
        f2_c.append(remote("f2_c", f2_half(p, s), f2_half(p, s), twin, 2 * p, 6))
        f2_y[p].start()
        f2_c[-1].start()

    def f2_after_y(p):
        f2_y[p].wait_recv()
        f2_c.append(remote("f2_c", f2_half(p, 1 - s), f2_half(p, 1 - s), twin, 2 * p + 1, 6))
        f2_c[-1].start()


    dxp[:, 0:128], dxp[:, 128:256] = tiles_of(2)
    g2_compute(0)
    g1_after_quad()
    for b, (q0, qn, segs) in enumerate(BLOCKS):
        pr = probs[b]
        for j0 in range(0, HEADS_HERE, group):
            ab = dam[j0:j0 + group, q0:q0 + qn, :].reshape(group * qn, 256)
            o = 0
            for a, n in segs:
                pg = nt(ab, qkv[a:a + n, 512:768])
                for g in range(group):
                    j = j0 + g
                    r = slice(j * qn, (j + 1) * qn)
                    ds[r, o:o + n] = (
                        pr[r, o:o + n].astype(F32)
                        * (pg[g * qn:(g + 1) * qn] - delta[q0:q0 + qn, j:j + 1])
                    ).astype(BF)
                o += n
        o, acc = 0, None
        for a, n in segs:
            part = nn(ds[0:HEADS_HERE * qn, o:o + n], qkv[a:a + n, 256:512])
            acc = part if acc is None else acc + part
            o += n
        dxw[q0:q0 + qn, 0:256] = (pick_heads(acc, qn) * SCALE).astype(BF)
        o = 0
        for a, n in segs:
            dk = None
            for j in range(HEADS_HERE):
                pk = tn(ds[j * qn:(j + 1) * qn, o:o + n], qm[j, q0:q0 + qn])
                dk = pk if dk is None else dk + pk
            dkf[a:a + n] += dk
            o += n
        if b == 0:
            g2_after_twin(0)
        if b == 1:
            g1_after_y(1)
        if b == 2:
            g1_after_x(2)
        if b == 3:
            st1[0] = g1_after_z(0)
        if b == 4:
            g1_after_x(1)
            st2[0] = g2_after_z(0)
    g1_after_y(2)
    dxw[:, 256:512] = (dkf[0:TOTAL] * SCALE).astype(BF)
    q_full, q_half = tiles_of(0)
    k_full, k_half = tiles_of(1)
    dxp[:, 256:384], dxp[:, 384:512] = q_full, k_full
    dxp[:, 512:640] = (q_half.astype(F32) + pltpu.roll(k_half.astype(F32), 64, 1)).astype(BF)

    fp_x = [
        remote("fp_x", fp.at[chunk(2 * (1 - h) + k, 128)], fx.at[chunk(k, 128)], x_peer, k, 3)
        for k in range(2)
    ]
    fp_xn = [
        remote("fp_xn", fs.at[256 + 96 * k:256 + 96 * (k + 1)], fx.at[256 + 96 * k:256 + 96 * (k + 1)], x_peer, k, 2)
        for k in range(2)
    ]
    fp_y = [
        remote("fp_y", fs.at[chunk(k, 128)], fy.at[chunk(k, 128)], y_peer, k, 2) for k in range(2)
    ]
    fp_yn = [
        remote("fp_yn", fp.at[EDGES + 96 * k:EDGES + 96 * (k + 1)], fy.at[96 * k:96 * (k + 1)], y_peer, k, 2)
        for k in range(2)
    ]
    def fp_after_x(k):
        fp_x[k].wait_recv()
        add_into(fs.at[chunk(k, 128)], fp[chunk(2 * h + k, 128)], fx[chunk(k, 128)])
        pl.when(s == 0)(fp_y[k].start)

    g2_compute(1)
    g2_compute(2)
    for k in range(2):
        rows = chunk(2 * (1 - h) + k, 128)
        fp[rows] = nt(dxw[rows], ww[...]).astype(BF)
        fp_x[k].start()
    g2_after_twin(1)
    g2_after_twin(2)
    fp[EDGES:TOTAL] = nt(dxw[EDGES:TOTAL], ww[...]).astype(BF)

    @pl.when(s == 1)
    def _():
        for copy in fp_yn:
            copy.start()

    fp[pl.ds(own, 256)] = nt(dxw[pl.ds(own, 256)], ww[...]).astype(BF)
    st1[1] = g1_after_z(1)
    f1_after_z(0, st1[0])
    fp_after_x(0)
    fp_after_x(1)
    pl.when(s == 1)(out_send.start)
    pl.when(me == 0)(out_node.start)
    f2_after_z(0, st2[0])

    @pl.when(s == 0)
    def _():
        for k in range(2):
            fp_yn[k].wait_recv()
            at = slice(256 + 96 * k, 256 + 96 * (k + 1))
            add_into(fs.at[at], fp[EDGES + 96 * k:EDGES + 96 * (k + 1)], fy[96 * k:96 * (k + 1)])
            pl.when(h == 1)(fp_xn[k].start)

    qkv_bias_sum = col_sum(dxw[...].astype(F32))

    st2[1] = g2_after_z(1)
    st2[2] = g2_after_z(2)

    def first_rows(rows, fg):
        n1, r1 = normed(res[rows].astype(F32))
        g = fg * a_gain
        back = r1 * (
            g - jnp.mean(g, axis=-1, keepdims=True) - n1 * jnp.mean(g * n1, axis=-1, keepdims=True)
        )
        dtv[rows] = (mgd[rows] + back).astype(BF)
        return jnp.concatenate([col_sum(fg * n1), col_sum(fg)], axis=0)

    def own_chunk(k, n):
        return pl.ds(pl.multiple_of(own + n * k, n), n)

    dt_e = [
        remote("dt", dtv.at[128 * k:128 * (k + 1)], d_tok.at[own_chunk(k, 128)], x_peer, k, 2)
        for k in range(2)
    ]
    dt_n = remote("dt", dtv.at[0:NODES], d_tok.at[0:NODES], x_peer, 0, 2)
    va[...] = jnp.zeros_like(va)

    @pl.when(s == 1)
    def _():
        for k in range(2):
            fp_y[k].wait_recv()

            def edge_rows(i, carry):
                rows = pl.ds(pl.multiple_of(128 * k + 64 * i, 64), 64)
                return carry + first_rows(rows, fs[rows].astype(F32) + fy[rows].astype(F32))

            got = lax.fori_loop(0, 2, edge_rows, jnp.zeros((2, 768), F32))
            va[0:2] += got
            dt_e[k].start()

    @pl.when((s == 0) & (h == 0))
    def _():
        for k in range(2):
            fp_xn[k].wait_recv()

            def node_rows(i, carry):
                rows = pl.ds(pl.multiple_of(96 * k + 32 * i, 32), 32)
                from_fs = pl.ds(pl.multiple_of(256 + 96 * k + 32 * i, 32), 32)
                return carry + first_rows(rows, fs[from_fs].astype(F32) + fx[from_fs].astype(F32))

            got = lax.fori_loop(0, 3, node_rows, jnp.zeros((2, 768), F32))
            va[0:2] += got
        dtv[NODES:256] = mgd[NODES:256].astype(BF)
        dt_n.start()

    @pl.when((s == 0) & (h == 1))
    def _():
        dtv[...] = mgd[...].astype(BF)

    stores[1].start()

    sums = [f_gain_sum, f_shift_sum, out_bias_sum, down_bias_sum, up_bias_sum, va[0:1], va[1:2], zero_row]
    sums += [jnp.where(me == r, qkv_bias_sum, 0.0) for r in range(4)] + [zero_row] * 4
    vq[me] = jnp.concatenate(sums, axis=0)
    v1 = [remote("v_q", vq.at[me], vq.at[me], dev, k, 3) for k, dev in enumerate(quad)]
    for copy in v1:
        copy.start()

    st1[2] = g1_after_z(2)
    f2_after_z(1, st2[1])
    f2_after_z(2, st2[2])
    f1_after_z(1, st1[1])
    f1_after_y(0)
    f2_after_y(0)
    v1_in = [
        remote("v_q", vq.at[r], vq.at[r], dev, k, 3)
        for k, (dev, r) in enumerate(zip(quad, (2 * s + 1 - h, 2 - 2 * s + h, 3 - 2 * s - h)))
    ]
    for copy in v1_in:
        copy.wait_recv()
    vz[z] = vq[0] + vq[1] + vq[2] + vq[3]
    v2 = [remote("v_z", vz.at[z], vz.at[z], z_peers[d], d, zc - 1) for d in range(zc - 1)]
    for copy in v2:
        copy.start()
    f1_after_z(2, st1[2])
    f1_after_y(1)
    f2_after_y(1)
    f2_after_y(2)
    for copy in v2:
        copy.wait_recv()
    vsum = vz[0]
    for d in range(1, zc):
        vsum = vsum + vz[d]
    vc[c] = vsum
    v3 = remote("v_c", vc.at[c], vc.at[c], twin)
    v3.start()
    f1_after_y(2)
    v3.wait_recv()
    vec[...] = vc[0] + vc[1]
    for copy in (*f1_c, *f2_c):
        copy.wait_recv()
    for copy in stores[0:2]:
        copy.wait()

    @pl.when(s == 1)
    def _():
        for copy in (*dt_e, out_send):
            copy.wait()

    @pl.when(me == 0)
    def _():
        for copy in (dt_n, out_node):
            copy.wait_send()
        for copy in far:
            copy.wait()

    @pl.when(me == 1)
    def _():
        for copy in (dt_n, out_node):
            copy.wait_recv()
        for copy in near:
            copy.wait()

    @pl.when(s == 1)
    def _():
        for copy in tok_y:
            copy.wait_send()

    @pl.when(s == 0)
    def _():
        tok_n.wait_send()
        for copy in tok_x:
            copy.wait_send()

    @pl.when(me != 1)
    def _():
        for copy in (*g1_q, g1_y[1], g1_x[2]):
            copy.wait_send()

    wait_sent("att", att, ain)

    @pl.when(s == 0)
    def _():
        for copy in fp_y:
            copy.wait_send()

    @pl.when(me == 1)
    def _():
        for copy in fp_xn:
            copy.wait_send()

    @pl.when(s == 1)
    def _():
        for copy in fp_yn:
            copy.wait_send()

    @pl.when(s == 1)
    def _():
        w_out[0].wait_send()
        w_out[2].wait_send()
        w_y[0].wait_send()
        w_y[2].wait_send()

    for k, (dev_sh, first, count) in enumerate(OWNERS):
        mine = 2 * dev_sh[0] + dev_sh[1]

        @pl.when(me == mine)
        def _():
            for r in range(4):
                if r != mine:
                    i = sem_id("da_s", 4) + r
                    pltpu.make_async_remote_copy(
                        src_ref=ago.at[0:count, 0:256], dst_ref=da.at[first:first + count],
                        send_sem=ss.at[i], recv_sem=rs.at[i], device_id=x_peer, device_id_type=MESH,
                    ).wait_send()

    for copy in (
        u_send, w_out[1], *w_twin, *g1_twin, g1_x[1], g1_y[2], *sum(g1_z, []), *fp_x, *g2_twin,
        *sum(g2_z, []), *v1, *sum(f1_z, []), *f1_y, *f1_c, *sum(f2_z, []), *f2_y, *f2_c, *v2, v3,
    ):
        copy.wait_send()


def finish_kernel(
    tokens, cot, d_out, d_tok, f1, f2, vec,
    output, tokens_grad, a_gain, a_shift, wq, bq, wk, wv, bv, wo, bo, f_gain, f_shift, wu, bu, wd, bd,
):
    h = lax.axis_index("head")
    output[...] = tokens[...].astype(F32) + d_out[...].astype(F32)
    tokens_grad[...] = cot[...] + d_tok[...].astype(F32)
    for k in range(2):
        lanes = slice(384 * k, 384 * (k + 1))
        wd[:, lanes] = f1[0, k].astype(F32)
        wo[:, lanes] = f1[2, k].astype(F32)
        wu[k] = f1[1, k].astype(F32)
    low_half = lax.broadcasted_iota(jnp.int32, (1, 128), 1) < 64
    tile = lambda k, t: f2[k, :, 128 * t:128 * (t + 1)].astype(F32)
    for t, out in ((0, wv), (2, wq), (3, wk)):
        out[:, 0:128] = tile(0, t)
        out[:, 256:384] = tile(1, t)
    wq[:, 128:256] = jnp.where(low_half, tile(0, 4), tile(1, 4))
    wk[:, 128:256] = pltpu.roll(jnp.where(low_half, tile(1, 4), tile(0, 4)), 64, 1)
    wv[:, 128:256] = jnp.where(low_half, tile(0, 1), tile(1, 1))

    @pl.when(pl.program_id(0) == 0)
    def _():
        mine = pl.ds(pl.multiple_of(384 * h, 384), 384)
        for row, out in ((0, f_gain), (1, f_shift), (2, bo), (3, bd), (4, bu), (5, a_gain), (6, a_shift)):
            out[...] = vec[row:row + 1, mine].reshape(384)
        low = jnp.where(h == 0, vec[8:9], vec[9:10])
        high = jnp.where(h == 0, vec[10:11], vec[11:12])
        for first, out in ((0, bq), (512, bv)):
            a, b = low[:, first:first + 256], high[:, first:first + 256]
            parts = [a[:, 0:128], a[:, 128:256] + b[:, 0:128], b[:, 128:256]]
            out[...] = jnp.concatenate(parts, axis=1).reshape(384)


def fast_layer(
    tokens, cotangent, attn_gain, attn_shift, query_weight, query_bias, key_weight, value_weight,
    value_bias, out_weight, out_bias, ffn_gain, ffn_shift, up_weight, up_bias, down_weight,
    down_bias, atom_counts, edge_counts,
):
    zc = lax.axis_size("mol") // 2
    anywhere = pl.BlockSpec(memory_space=pl.ANY)
    vmem = pl.BlockSpec(memory_space=pltpu.VMEM)
    smem = pl.BlockSpec(memory_space=pltpu.SMEM)
    shape = jax.ShapeDtypeStruct
    SEM.clear()
    buf = lambda dtype, *dims: pltpu.VMEM(dims, dtype)
    scratch = [
        buf(BF, 256, 768), buf(BF, 256, 768), buf(BF, 256, 768), buf(BF, 3, 192 // zc, 384), buf(BF, 384 // zc, 640), buf(BF, TOTAL, 640),
        buf(BF, PADDED, 768), buf(BF, 256, 768), buf(F32, 256, 768), buf(BF, 768, 768),
        buf(BF, 2, 384, 768), buf(BF, 2, 768, 384), buf(BF, 2, 384, 768), buf(F32, 2, 8, 384),
        buf(BF, PADDED, 768), buf(BF, PADDED, 768), buf(BF, TOTAL, 768),
        buf(BF, HEADS_HERE, TOTAL, 256), buf(BF, HEADS_HERE, TOTAL, 256),
        buf(BF, 1024, 512), buf(BF, 1024, 512), buf(BF, 1024, 512), buf(BF, 1024, 512), buf(BF, 1536, 768),
        buf(F32, 256, 768), buf(jnp.int32, TOTAL, 1),
        buf(F32, TOTAL, 256), buf(BF, TOTAL, 256), buf(BF, 4, 256, 256), buf(BF, TOTAL, 256), buf(F32, TOTAL, 128),
        buf(F32, 256, 768), buf(F32, 256, 768), buf(F32, 256, 768), buf(F32, 256, 128), buf(F32, 256, 768),
        buf(BF, 256, 768), buf(BF, 256, 768), buf(BF, 256, 768), buf(BF, 256, 768), buf(BF, 256, 768),
        buf(BF, 256, 768), buf(BF, 256, 768), buf(F32, 256, 768),
        buf(BF, 1536, 768), buf(F32, PADDED, 256), buf(F32, PADDED, 256),
        buf(BF, 3, 2, 2, 384, 384), buf(BF, 3, 2, 384, 384), buf(BF, 3, 192, 384), buf(BF, 3, 384, 384), buf(BF, 3, 2, 384, 384),
        buf(BF, 3, 2, 192, 384), buf(BF, 3, 192, 384), buf(BF, 3, zc - 1, 192 // zc, 384),
        buf(BF, 2, 384, 640), buf(BF, 384, 640), buf(BF, zc - 1, 384 // zc, 640),
        buf(BF, TOTAL, 768), buf(BF, 256 + NODES, 768), buf(BF, 256 + NODES, 768), buf(BF, 256, 768),
        buf(F32, 8, 768), buf(F32, 4, 16, 768), buf(F32, zc, 16, 768), buf(F32, 2, 16, 768),
        pltpu.SemaphoreType.DMA((N_SEMS,)), pltpu.SemaphoreType.DMA((N_SEMS,)), pltpu.SemaphoreType.DMA((N_LOCAL,)),
    ]
    d_out, d_tok, f1, f2, vec = pl.pallas_call(
        layer_kernel,
        out_shape=[
            shape((512, 768), BF), shape((512, 768), BF), shape((3, 2, 384, 384), BF),
            shape((2, 768, 640), BF), shape((16, 768), F32),
        ],
        in_specs=[anywhere] * 8 + [smem] * 2 + [vmem] * 9,
        out_specs=[anywhere] * 4 + [vmem],
        scratch_shapes=scratch,
        compiler_params=pltpu.CompilerParams(
            collective_id=0, has_side_effects=True, vmem_limit_bytes=61 * 2**20
        ),
        name="layer",
    )(
        tokens, cotangent, query_weight, key_weight, value_weight, out_weight, up_weight, down_weight,
        atom_counts, edge_counts, attn_gain, attn_shift, query_bias, value_bias, out_bias,
        ffn_gain, ffn_shift, up_bias, down_bias,
    )
    assert sum(n for _, n in SEM.values()) <= N_SEMS
    steps = 4
    mat, tall, line = shape((384, 768), F32), shape((768, 384), F32), shape((384,), F32)
    big, pair = shape((512, 768), F32), shape((2, 384, 384), F32)
    by_rows = lambda rows, cols: pl.BlockSpec((rows // steps, cols), lambda i: (i, 0))
    big_spec, mat_spec, tall_spec = by_rows(512, 768), by_rows(384, 768), by_rows(768, 384)
    line_spec = pl.BlockSpec((384,), lambda i: (0,))
    pair_spec = pl.BlockSpec((2, 384 // steps, 384), lambda i: (0, i, 0))
    outs = pl.pallas_call(
        finish_kernel,
        grid=(steps,),
        out_shape=[big, big, line, line, tall, line, tall, tall, line, mat, line, line, line, pair, line, mat, line],
        in_specs=[
            big_spec, big_spec, big_spec, big_spec,
            pl.BlockSpec((3, 2, 384 // steps, 384), lambda i: (0, 0, i, 0)),
            pl.BlockSpec((2, 768 // steps, 640), lambda i: (0, i, 0)),
            pl.BlockSpec((16, 768), lambda i: (0, 0)),
        ],
        out_specs=[
            big_spec, big_spec, line_spec, line_spec, tall_spec, line_spec, tall_spec, tall_spec, line_spec,
            mat_spec, line_spec, line_spec, line_spec, pair_spec, line_spec, mat_spec, line_spec,
        ],
        compiler_params=pltpu.CompilerParams(vmem_limit_bytes=60 * 2**20),
        name="finish",
    )(tokens, cotangent, d_out, d_tok, f1, f2, vec)
    return tuple(o.reshape(768, 384) if o.ndim == 3 else o for o in outs)


def plain_dot(operand, partner):
    return jnp.dot(operand, partner, preferred_element_type=jnp.float32)


def lead_dot(operand, partner):
    return lax.dot_general(
        operand, partner, (((0,), (0,)), ((), ())), preferred_element_type=jnp.float32
    )


def tail_dot(operand, partner):
    return lax.dot_general(
        operand, partner, (((1,), (1,)), ((), ())), preferred_element_type=jnp.float32
    )


def norm_apply(values, gain_vec, shift_vec):
    row_mean = jnp.mean(values, axis=-1, keepdims=True)
    centered = values - row_mean
    variance = jnp.mean(centered * centered, axis=-1, keepdims=True)
    return centered * lax.rsqrt(variance + 1e-05) * gain_vec + shift_vec


def gelu_exact(values):
    return jax.nn.gelu(values, approximate=False)


def segment_ids(counts, added, slot_count):
    members = jnp.arange(counts.shape[0])
    earlier = members[:, None] <= members[None, :]
    seg_ends = jnp.sum(jnp.where(earlier, (counts + added)[:, None], 0), axis=0)
    positions = jnp.arange(slot_count, dtype=jnp.int32)
    return jnp.sum((positions[:, None] >= seg_ends[None, :]).astype(jnp.int32), axis=1)


def head_piece(vector, head_rank, head_share):
    return lax.dynamic_slice_in_dim(vector, head_rank * head_share, head_share)


def on_device(
    tokens,
    cotangent,
    attn_gain,
    attn_shift,
    query_weight,
    query_bias,
    key_weight,
    value_weight,
    value_bias,
    out_weight,
    out_bias,
    ffn_gain,
    ffn_shift,
    up_weight,
    up_bias,
    down_weight,
    down_bias,
    atom_counts,
    edge_counts,
):
    row_count = tokens.shape[0]
    model_width = tokens.shape[1]
    local_width = query_weight.shape[1]
    local_heads = local_width // HEAD_DIM
    head_count = lax.axis_size("head")
    head_rank = lax.axis_index("head")
    stream_rank = lax.axis_index("stream")
    molecules = atom_counts.shape[1]
    head_share = model_width // head_count
    score_scale = HEAD_DIM ** (-0.5)
    seg_node = segment_ids(atom_counts[0], 1, row_count)
    seg_edge = segment_ids(edge_counts[0], 0, row_count)
    key_seg = jnp.concatenate([seg_node, seg_edge])
    own_seg = jnp.where(stream_rank == 0, seg_node, seg_edge)
    live_rows = (own_seg < molecules).astype(jnp.float32)[:, None]
    residual = tokens.astype(jnp.float32)
    normed, norm_pull = jax.vjp(norm_apply, residual, attn_gain, attn_shift)
    first_in = normed.astype(jnp.bfloat16)
    queries = (plain_dot(first_in, query_weight) + query_bias).astype(jnp.bfloat16)
    keys_local = plain_dot(first_in, key_weight).astype(jnp.bfloat16)
    values_local = (plain_dot(first_in, value_weight) + value_bias).astype(jnp.bfloat16)
    all_keys, all_values = (
        lax.all_gather(keys_local, "stream", axis=0, tiled=True),
        lax.all_gather(values_local, "stream", axis=0, tiled=True),
    )
    key_count = all_keys.shape[0]
    key_heads = all_keys.reshape(key_count, local_heads, HEAD_DIM)
    value_heads = all_values.reshape(key_count, local_heads, HEAD_DIM)
    blocks = row_count // 512
    block_rows = row_count // blocks
    query_blocks = queries.reshape(blocks, block_rows, local_heads, HEAD_DIM)
    seg_blocks = own_seg.reshape(blocks, block_rows)

    def forward_block(pieces):
        query_part, seg_part = pieces
        scores = (
            jnp.einsum("qhd,khd->hqk", query_part, key_heads, preferred_element_type=jnp.float32)
            * score_scale
        )
        same_mol = (seg_part[:, None] == key_seg[None, :])[None]
        scores = jnp.where(same_mol, scores, -1e30)
        row_top = jnp.max(scores, axis=-1, keepdims=True)
        shifted = jnp.exp(scores - row_top)
        row_total = jnp.sum(shifted, axis=-1, keepdims=True)
        prob_low = (shifted / row_total).astype(jnp.bfloat16)
        attended_part = jnp.einsum(
            "hqk,khd->qhd", prob_low, value_heads, preferred_element_type=jnp.float32
        )
        return (attended_part.astype(jnp.bfloat16), (row_top + jnp.log(row_total))[..., 0])

    attended_blocks, lse_blocks = lax.map(forward_block, (query_blocks, seg_blocks))
    attended = attended_blocks.reshape(row_count, local_width)
    attn_sum = lax.psum(plain_dot(attended, out_weight), "head")
    middle = residual + live_rows * (attn_sum + out_bias)
    second, second_pull = jax.vjp(norm_apply, middle, ffn_gain, ffn_shift)
    second_in = second.astype(jnp.bfloat16)
    inner_pre = plain_dot(second_in, up_weight) + up_bias.astype(jnp.float32)
    activated, gelu_pull = jax.vjp(gelu_exact, inner_pre)
    hidden = activated.astype(jnp.bfloat16)
    ffn_sum = lax.psum(plain_dot(hidden, down_weight).astype(jnp.bfloat16), "head").astype(
        jnp.float32
    )
    output = middle + live_rows * (ffn_sum + down_bias)
    down_cot = (live_rows * cotangent).astype(jnp.bfloat16)
    down_weight_grad = lead_dot(hidden, down_cot)
    down_bias_full = jnp.sum(down_cot.astype(jnp.float32), axis=0)
    inner_grad = gelu_pull(tail_dot(down_cot, down_weight))[0].astype(jnp.bfloat16)
    up_weight_grad = lead_dot(second_in, inner_grad)
    up_bias_grad = jnp.sum(inner_grad.astype(jnp.float32), axis=0)
    second_grad = lax.psum(tail_dot(inner_grad, up_weight), "head")
    middle_part, ffn_gain_full, ffn_shift_full = second_pull(second_grad)
    mid_grad = cotangent + middle_part
    ffn_gain_grad = head_piece(ffn_gain_full, head_rank, head_share)
    ffn_shift_grad = head_piece(ffn_shift_full, head_rank, head_share)
    down_bias_grad = head_piece(down_bias_full, head_rank, head_share)
    attn_cot = (live_rows * mid_grad).astype(jnp.bfloat16)
    out_weight_grad = lead_dot(attended, attn_cot)
    out_bias_full = jnp.sum(attn_cot.astype(jnp.float32), axis=0)
    attended_grad = tail_dot(attn_cot, out_weight).astype(jnp.bfloat16)
    grad_blocks = attended_grad.reshape(blocks, block_rows, local_heads, HEAD_DIM)

    def backward_block(running, pieces):
        key_acc, value_acc = running
        query_part, seg_part, lse_part, grad_part = pieces
        scores = (
            jnp.einsum("qhd,khd->hqk", query_part, key_heads, preferred_element_type=jnp.float32)
            * score_scale
        )
        same_mol = (seg_part[:, None] == key_seg[None, :])[None]
        prob_full = jnp.where(same_mol, jnp.exp(scores - lse_part[..., None]), 0.0)
        prob_low = prob_full.astype(jnp.bfloat16)
        prob_grad = jnp.einsum(
            "qhd,khd->hqk", grad_part, value_heads, preferred_element_type=jnp.float32
        )
        row_delta = jnp.sum(prob_grad * prob_full, axis=-1, keepdims=True)
        score_grad = (prob_full * (prob_grad - row_delta)).astype(jnp.bfloat16)
        query_part_grad = (
            jnp.einsum("hqk,khd->qhd", score_grad, key_heads, preferred_element_type=jnp.float32)
            * score_scale
        )
        key_acc = (
            key_acc
            + jnp.einsum("hqk,qhd->khd", score_grad, query_part, preferred_element_type=jnp.float32)
            * score_scale
        )
        value_acc = value_acc + jnp.einsum(
            "hqk,qhd->khd", prob_low, grad_part, preferred_element_type=jnp.float32
        )
        return ((key_acc, value_acc), query_part_grad.astype(jnp.bfloat16))

    zero_keys = jnp.zeros((key_count, local_heads, HEAD_DIM), jnp.float32)
    (key_acc, value_acc), query_grads = lax.scan(
        backward_block, (zero_keys, zero_keys), (query_blocks, seg_blocks, lse_blocks, grad_blocks)
    )
    key_sum, value_sum = (
        lax.psum_scatter(
            key_acc.reshape(key_count, local_width), "stream", scatter_dimension=0, tiled=True
        ),
        lax.psum_scatter(
            value_acc.reshape(key_count, local_width), "stream", scatter_dimension=0, tiled=True
        ),
    )
    key_grad = key_sum.astype(jnp.bfloat16)
    value_grad = value_sum.astype(jnp.bfloat16)
    query_grad = query_grads.reshape(row_count, local_width)
    query_weight_grad = lead_dot(first_in, query_grad)
    query_bias_grad = jnp.sum(query_grad.astype(jnp.float32), axis=0)
    key_weight_grad = lead_dot(first_in, key_grad)
    value_weight_grad = lead_dot(first_in, value_grad)
    value_bias_grad = jnp.sum(value_grad.astype(jnp.float32), axis=0)
    first_part = (
        tail_dot(query_grad, query_weight)
        + tail_dot(key_grad, key_weight)
        + tail_dot(value_grad, value_weight)
    )
    first_grad = lax.psum(first_part.astype(jnp.bfloat16), "head").astype(jnp.float32)
    resid_part, attn_gain_full, attn_shift_full = norm_pull(first_grad)
    tokens_grad = mid_grad + resid_part
    attn_gain_grad = head_piece(attn_gain_full, head_rank, head_share)
    attn_shift_grad = head_piece(attn_shift_full, head_rank, head_share)
    out_bias_grad = head_piece(out_bias_full, head_rank, head_share)
    (
        attn_gain_grad,
        attn_shift_grad,
        query_weight_grad,
        query_bias_grad,
        key_weight_grad,
        value_weight_grad,
        value_bias_grad,
        out_weight_grad,
        out_bias_grad,
        ffn_gain_grad,
        ffn_shift_grad,
        up_weight_grad,
        up_bias_grad,
        down_weight_grad,
        down_bias_grad,
    ) = lax.psum(
        (
            attn_gain_grad,
            attn_shift_grad,
            query_weight_grad,
            query_bias_grad,
            key_weight_grad,
            value_weight_grad,
            value_bias_grad,
            out_weight_grad,
            out_bias_grad,
            ffn_gain_grad,
            ffn_shift_grad,
            up_weight_grad,
            up_bias_grad,
            down_weight_grad,
            down_bias_grad,
        ),
        ("mol", "stream"),
    )
    return (
        output,
        tokens_grad,
        attn_gain_grad,
        attn_shift_grad,
        query_weight_grad,
        query_bias_grad,
        key_weight_grad,
        value_weight_grad,
        value_bias_grad,
        out_weight_grad,
        out_bias_grad,
        ffn_gain_grad,
        ffn_shift_grad,
        up_weight_grad,
        up_bias_grad,
        down_weight_grad,
        down_bias_grad,
    )


def solution(mesh):
    in_specs = (
        P(("mol", "stream"), None),
        P(("mol", "stream"), None),
        P(),
        P(),
        P(None, "head"),
        P("head"),
        P(None, "head"),
        P(None, "head"),
        P("head"),
        P("head", None),
        P(),
        P(),
        P(),
        P(None, "head"),
        P("head"),
        P("head", None),
        P(),
        P("mol", None),
        P("mol", None),
    )
    out_specs = (
        P(("mol", "stream"), None),
        P(("mol", "stream"), None),
        P("head"),
        P("head"),
        P(None, "head"),
        P("head"),
        P(None, "head"),
        P(None, "head"),
        P("head"),
        P("head", None),
        P("head"),
        P("head"),
        P("head"),
        P(None, "head"),
        P("head"),
        P("head", None),
        P("head"),
    )
    one_chip_pair = (
        mesh.shape["head"] == 2 and mesh.shape["stream"] == 2 and mesh.shape["mol"] == 8
    )
    return jax.shard_map(
        fast_layer if one_chip_pair else on_device, mesh=mesh, in_specs=in_specs, out_specs=out_specs, check_vma=False
    )
```

```python
import functools
import math

import jax
import jax.numpy as jnp
from jax import lax
from jax.experimental import pallas as pl
from jax.experimental.pallas import tpu as pltpu
from jax.sharding import PartitionSpec as P

HEAD_DIM = 24
BF = jnp.bfloat16
F32 = jnp.float32
MESH = pl.DeviceIdType.MESH
EDGES = 512
NODES = 192
TOTAL = EDGES + NODES
PADDED = 768
HEADS_HERE = 8
SCALE = HEAD_DIM ** (-0.5)
SCALE2 = SCALE * math.log2(math.e)
BLOCKS = (
    (0, 128, ((0, 256), (512, 256))),
    (128, 128, ((64, 256), (512, 256))),
    (256, 128, ((192, 256), (512, 256))),
    (384, 128, ((256, 256), (512, 256))),
    (512, 192, ((0, 768),)),
)
OWNERS = (((0, 0), 512, 192), ((1, 0), 0, 256), ((1, 1), 256, 256))


def nn(a, b):
    return jnp.dot(a, b, preferred_element_type=F32)


def nt(a, b):
    return lax.dot_general(a, b, (((1,), (1,)), ((), ())), preferred_element_type=F32)


def tn(a, b):
    return lax.dot_general(a, b, (((0,), (0,)), ((), ())), preferred_element_type=F32)


def row_loop(count, step, fn, init):
    def body(i, carry):
        return fn(pl.ds(pl.multiple_of(i * step, step), step), carry)

    return lax.fori_loop(0, count // step, body, init)


def normed(x):
    mu = jnp.mean(x, axis=-1, keepdims=True)
    xc = x - mu
    var = jnp.mean(xc * xc, axis=-1, keepdims=True)
    r = lax.rsqrt(var + 1e-05)
    return xc * r, r


def col_sum(x):
    return jnp.sum(x, axis=0, keepdims=True)


SEM = {}


def sem_id(name, count=1):
    if name not in SEM:
        SEM[name] = sum(n for _, n in SEM.values()), count
    return SEM[name][0]


N_SEMS = 160
N_LOCAL = 24


def layer_kernel(
    tokens, cot, wq, wk, wv, wo, wu, wd,
    atoms, edges,
    a_gain_v, a_shift_v, q_bias_v, v_bias_v, o_bias_v, f_gain_v, f_shift_v, u_bias_v, d_bias_v,
    d_out, d_tok, f1, f2, vec,
    dov, dtv, zb, fz1, fz2, dxp, tok, res, cotv, ww, fwo, fwu, fwd, ub, fin1, qkv, dxw, qm, dam,
    p0, p1, p2, p3, p4, bias, segc, attf, att, ain, da, delta,
    t0, t1, n2s, r2s, mid, sec, hid, dc, ig, ac, ato, ago, mgd,
    ds, dkf, dvf,
    g1, gs1, qr, xr, gx, yr, gq, zr1, g2, gs2, zr2, fp, fx, fs, fy,
    va, vq, vz, vc,
    ss, rs, ls,
):
    m, s, h = lax.axis_index("mol"), lax.axis_index("stream"), lax.axis_index("head")
    z, c = m // 2, lax.rem(m, 2)
    zc = lax.axis_size("mol") // 2
    me = 2 * s + h
    x_peer, y_peer, xy_peer = (m, s, 1 - h), (m, 1 - s, h), (m, 1 - s, 1 - h)
    quad = (x_peer, y_peer, xy_peer)
    twin = (2 * z + 1 - c, s, h)
    z_peers = [(2 * lax.rem(z + d, zc) + c, s, h) for d in range(1, zc)]

    def remote(name, src, dst, dev, k=0, count=1):
        i = sem_id(name, count) + k
        return pltpu.make_async_remote_copy(
            src_ref=src, dst_ref=dst, send_sem=ss.at[i], recv_sem=rs.at[i],
            device_id=dev, device_id_type=MESH,
        )

    def as_row(ref):
        return ref[...].astype(F32).reshape(1, -1)

    a_gain, a_shift, f_gain, f_shift = (as_row(r) for r in (a_gain_v, a_shift_v, f_gain_v, f_shift_v))
    o_bias, d_bias, q_bias, v_bias = (as_row(r) for r in (o_bias_v, d_bias_v, q_bias_v, v_bias_v))

    def local(k, src, dst):
        return pltpu.make_async_copy(src, dst, ls.at[k])

    own = pl.multiple_of(256 * h, 256)
    other = pl.multiple_of(256 * (1 - h), 256)
    window = pl.multiple_of(128 * s, 128)

    loads = [
        local(0, tokens.at[pl.ds(own, 256)], res),
        local(1, cot.at[pl.ds(own, 256)], cotv),
        local(2, wq.at[:, pl.ds(window, 256)], ww.at[:, 0:256]),
        local(3, wk.at[:, pl.ds(window, 256)], ww.at[:, 256:512]),
        local(4, wv.at[:, pl.ds(window, 256)], ww.at[:, 512:768]),
        local(5, wo, fwo.at[h]),
        local(6, wu, fwu.at[h]),
        local(7, wd, fwd.at[h]),
    ]
    edge_load = local(8, tokens, tok.at[0:EDGES])
    node_load = local(9, tokens.at[0:NODES], tok.at[EDGES:TOTAL])
    pl.when(s == 1)(edge_load.start)
    pl.when(s == 0)(node_load.start)
    for copy in loads:
        copy.start()
    ub[h] = jnp.broadcast_to(as_row(u_bias_v), (8, 384))

    barrier = pltpu.get_barrier_semaphore()
    greeted = [*quad, twin, *z_peers]
    for dev in greeted:
        pl.semaphore_signal(barrier, inc=1, device_id=dev, device_id_type=MESH)
    pl.semaphore_wait(barrier, len(greeted))

    def edge_part(k, half):
        rows = pl.ds(pl.multiple_of(256 * half + 64 * k, 64), 64)
        return rows

    tok_y = [
        remote("tok_y", tokens.at[edge_part(k, h)], tok.at[edge_part(k, h)], y_peer, k, 4)
        for k in range(4)
    ]
    tok_x = [
        remote("tok_x", tok.at[edge_part(k, h)], tok.at[edge_part(k, h)], x_peer, k, 4)
        for k in range(4)
    ]
    tok_x_in = [
        remote("tok_x", tok.at[edge_part(k, 1 - h)], tok.at[edge_part(k, 1 - h)], x_peer, k, 4)
        for k in range(4)
    ]
    tok_n = remote("tok_n", tokens.at[0:NODES], tok.at[EDGES:TOTAL], y_peer)

    @pl.when(s == 1)
    def _():
        for copy in tok_y:
            copy.start()

    pl.when(s == 0)(tok_n.start)
    u_send = remote("ub", ub.at[h], ub.at[h], x_peer)
    u_send.start()
    part_o = pl.ds(pl.multiple_of(192 * c, 192), 192)
    part_u = pl.ds(pl.multiple_of(384 * c, 384), 384)
    w_out = [
        remote("wo_x", wo.at[part_o], fwo.at[h, part_o], x_peer),
        remote("wu_x", wu.at[part_u], fwu.at[h, part_u], x_peer),
        remote("wd_x", wd.at[part_o], fwd.at[h, part_o], x_peer),
    ]

    @pl.when(s == 1)
    def _():
        for k in (0, 2, 1):
            w_out[k].start()

    w_in = [
        remote("wo_x", wo.at[part_o], fwo.at[1 - h, part_o], x_peer),
        remote("wu_x", wu.at[part_u], fwu.at[1 - h, part_u], x_peer),
        remote("wd_x", wd.at[part_o], fwd.at[1 - h, part_o], x_peer),
    ]
    w_twin = [
        remote("wo_c", fwo.at[1 - h, part_o], fwo.at[1 - h, part_o], twin),
        remote("wu_c", fwu.at[1 - h, part_u], fwu.at[1 - h, part_u], twin),
        remote("wd_c", fwd.at[1 - h, part_o], fwd.at[1 - h, part_o], twin),
    ]

    w_y = {
        0: remote("wo_y", fwo.at[1 - h, part_o], fwo.at[1 - h, part_o], y_peer),
        2: remote("wd_y", fwd.at[1 - h, part_o], fwd.at[1 - h, part_o], y_peer),
    }

    def pass_weight(k):
        w_in[k].wait_recv()
        w_y[k].start()
        w_twin[k].start()

    def share_weight(k):
        w_in[k].wait_recv()
        w_twin[k].start()

    def take_weight(k):
        w_y[k].wait_recv()
        w_twin[k].start()

    def ends_of(counts, added):
        total, ends = 0, []
        for j in range(counts.shape[1]):
            total = total + counts[0, j] + added
            ends.append(total)
        return ends

    node_ends, edge_ends = ends_of(atoms, 1), ends_of(edges, 0)
    live_count = jnp.where(s == 0, node_ends[-1], edge_ends[-1])

    def seg_of(position, ends):
        seg = jnp.zeros_like(position)
        for end in ends:
            seg = seg + jnp.where(position >= end, 1, 0)
        return seg

    segc[0:EDGES] = seg_of(lax.broadcasted_iota(jnp.int32, (EDGES, 1), 0), edge_ends)
    segc[EDGES:TOTAL] = seg_of(lax.broadcasted_iota(jnp.int32, (NODES, 1), 0), node_ends)
    at_row = lax.broadcasted_iota(jnp.int32, (1, PADDED), 1)
    seg_r = jnp.where(at_row < EDGES, seg_of(at_row, edge_ends), seg_of(at_row - EDGES, node_ends))
    seg_r = jnp.where(at_row < TOTAL, seg_r, -1)

    lane = lax.broadcasted_iota(jnp.int32, (1, 256), 1) - 64 * s
    head_of = jnp.where((lane >= 0) & (lane < 192), lane // HEAD_DIM, -1)
    zero = jnp.zeros((), BF)

    qkv[TOTAL:PADDED] = jnp.zeros((PADDED - TOTAL, 768), BF)
    bias_row = jnp.concatenate(
        [
            jnp.where(s == 0, q_bias[:, 0:256], q_bias[:, 128:384]),
            jnp.zeros((1, 256), F32),
            jnp.where(s == 0, v_bias[:, 0:256], v_bias[:, 128:384]),
        ],
        axis=1,
    )

    for who, slot in ((0, qr.at[0]), (3, qr.at[1]), (2, qr.at[2]), (3, yr.at[1, 0]), (3, yr.at[1, 1]), (0, xr.at[2])):

        @pl.when(me == who)
        def _():
            slot[...] = jnp.zeros_like(slot)

    def project(first, count):
        def norm_rows(i, carry):
            rows = pl.ds(pl.multiple_of(first + i * 64, 64), 64)
            n1, _ = normed(tok[rows].astype(F32))
            fin1[rows] = (n1 * a_gain + a_shift).astype(BF)
            return carry

        lax.fori_loop(0, count // 64, norm_rows, 0)
        rows = pl.ds(pl.multiple_of(first, 64), count)
        qkv[rows] = (nn(fin1[rows], ww[...]) + bias_row).astype(BF)

    for copy in loads[2:5]:
        copy.wait()

    @pl.when(s == 1)
    def _():
        edge_load.wait()
        project(0, EDGES)
        tok_n.wait_recv()
        project(EDGES, NODES)
        pass_weight(0)

    @pl.when(s == 0)
    def _():
        node_load.wait()
        project(EDGES, NODES)
        for k in range(4):
            tok_y[k].wait_recv()
            tok_x[k].start()
        w_out[1].start()
        project(own, 256)
        for k in range(4):
            tok_x_in[k].wait_recv()
        project(other, 256)

    for j in range(HEADS_HERE):
        qm[j] = jnp.where(head_of == j, qkv[0:TOTAL, 0:256], zero)

    def send_rows(name, src, dst, k):
        dev_sh, first, count = OWNERS[k]
        target = (m, *dev_sh)
        mine = 2 * dev_sh[0] + dev_sh[1]

        @pl.when(me != mine)
        def _():
            i = sem_id(name + "_s", 3) + k
            j = sem_id(name, 4) + me
            pltpu.make_async_remote_copy(
                src_ref=src.at[first:first + count], dst_ref=dst.at[me, 0:count],
                send_sem=ss.at[i], recv_sem=rs.at[j], device_id=target, device_id_type=MESH,
            ).start()

        @pl.when(me == mine)
        def _():
            dst[mine, 0:count] = src[first:first + count]

    def wait_rows(name, src, dst):
        for k, (dev_sh, first, count) in enumerate(OWNERS):
            mine = 2 * dev_sh[0] + dev_sh[1]

            @pl.when(me == mine)
            def _():
                for r in range(4):
                    if r != mine:
                        j = sem_id(name, 4) + r
                        pltpu.make_async_remote_copy(
                            src_ref=src.at[first:first + count], dst_ref=dst.at[r, 0:count],
                            send_sem=ss.at[j], recv_sem=rs.at[j], device_id=x_peer, device_id_type=MESH,
                        ).wait_recv()

    def wait_sent(name, src, dst):
        for k, (dev_sh, first, count) in enumerate(OWNERS):
            mine = 2 * dev_sh[0] + dev_sh[1]

            @pl.when(me != mine)
            def _():
                i = sem_id(name + "_s", 3) + k
                pltpu.make_async_remote_copy(
                    src_ref=src.at[first:first + count], dst_ref=dst.at[me, 0:count],
                    send_sem=ss.at[i], recv_sem=rs.at[i], device_id=(m, *dev_sh), device_id_type=MESH,
                ).wait_send()

    def pick_heads(stacked, rows):
        total = None
        for j in range(HEADS_HERE):
            part = jnp.where(head_of == j, stacked[j * rows:(j + 1) * rows], 0.0)
            total = part if total is None else total + part
        return total

    probs = (p0, p1, p2, p3, p4)
    to_owner = (None, 1, None, 2, 0)
    group = 4

    @pl.when(s == 0)
    def _():
        ain[:, NODES:256] = jnp.zeros((4, 256 - NODES, 256), BF)

    @pl.when((s == 0) & (h == 1))
    def _():
        ain[:, 0:NODES] = jnp.zeros((4, NODES, 256), BF)

    for b, (q0, qn, segs) in enumerate(BLOCKS):
        o = 0
        for a, n in segs:
            bias[0:qn, o:o + n] = jnp.where(segc[q0:q0 + qn] == seg_r[:, a:a + n], 0.0, -1e30)
            o += n
        for j0 in range(0, HEADS_HERE, group):
            qb = qm[j0:j0 + group, q0:q0 + qn, :].reshape(group * qn, 256)
            raw = [nt(qb, qkv[a:a + n, 256:512]) for a, n in segs]
            for g in range(group):
                j, o, parts = j0 + g, 0, []
                for piece, (a, n) in zip(raw, segs):
                    parts.append(piece[g * qn:(g + 1) * qn] * SCALE2 + bias[0:qn, o:o + n])
                    o += n
                top = functools.reduce(
                    jnp.maximum, [jnp.max(x, axis=1, keepdims=True) for x in parts]
                )
                parts = [jnp.exp2(x - top) for x in parts]
                inv = 1.0 / sum(jnp.sum(x, axis=1, keepdims=True) for x in parts)
                o = 0
                for x, (a, n) in zip(parts, segs):
                    probs[b][j * qn:(j + 1) * qn, o:o + n] = (x * inv).astype(BF)
                    o += n
        o, acc = 0, None
        for a, n in segs:
            part = nn(probs[b][:, o:o + n], qkv[a:a + n, 512:768])
            acc = part if acc is None else acc + part
            o += n
        picked = pick_heads(acc, qn)
        attf[q0:q0 + qn] = picked
        att[q0:q0 + qn] = picked.astype(BF)
        if to_owner[b] is not None:
            send_rows("att", att, ain, to_owner[b])

    @pl.when(s == 1)
    def _():
        pass_weight(2)

    @pl.when(s == 0)
    def _():
        take_weight(0)

    share_weight(1)

    cut = [slice(0, 384), slice(384, 768)]
    g1_of = (
        lambda cc, xh: tn(hid[:, cut[xh]], dc[:, cut[cc]]),
        lambda cc, xh: tn(sec[:, cut[cc]], ig[:, cut[xh]]),
        lambda cc, xh: tn(ato[:, cut[xh]], ac[:, cut[cc]]),
    )
    g1_twin = [remote("g1_c", g1.at[p, 1 - c], gs1.at[p], twin, p, 3) for p in range(3)]

    def g1_compute(p):
        for cc in range(2):
            for xh in range(2):
                g1[p, cc, xh] = g1_of[p](cc, xh).astype(BF)
        g1_twin[p].start()

    rows_y = pl.ds(pl.multiple_of(192 * (1 - s), 192), 192)
    rows_s = pl.ds(pl.multiple_of(192 * s, 192), 192)
    y_first = (None, True, False)
    g1_q = [
        remote("g1_q", gs1.at[0, 1 - h, rows_s], qr.at[0], x_peer, 0, 3),
        remote("g1_q", gs1.at[0, h, rows_y], qr.at[1], y_peer, 1, 3),
        remote("g1_q", gs1.at[0, 1 - h, rows_y], qr.at[2], xy_peer, 2, 3),
    ]
    g1_x = [
        remote("g1_x", gx.at[p, 1 - h, 0:192], xr.at[p, 0:192], x_peer, p, 3)
        if y_first[p] else remote("g1_x", gs1.at[p, 1 - h], xr.at[p], x_peer, p, 3)
        for p in range(3)
    ]
    g1_y = [
        remote("g1_y", gs1.at[p, :, rows_y], yr.at[p], y_peer, p, 3)
        if y_first[p] else remote("g1_y", gx.at[p, 0, rows_y], yr.at[p, 0], y_peer, p, 3)
        for p in range(3)
    ]
    zn1, zn2 = 192 // zc, 384 // zc

    def chunk(t, n):
        return pl.ds(pl.multiple_of(n * t, n), n)

    g1_z = [
        [
            remote("g1_z", gq.at[p, chunk(lax.rem(z + d, zc), zn1)], zr1.at[p, d - 1], z_peers[d - 1],
                   p * (zc - 1) + d - 1, 3 * (zc - 1))
            for d in range(1, zc)
        ]
        for p in range(3)
    ]

    def add_into(dst, *terms):
        x = terms[0].astype(F32)
        for t in terms[1:]:
            x = x + t.astype(F32)
        dst[...] = x.astype(BF)

    def g1_after_twin(p):
        g1_twin[p].wait_recv()
        for xh in range(2):
            add_into(gs1.at[p, xh], g1[p, c, xh], gs1[p, xh])

    def g1_after_quad():
        for copy, without in zip(g1_q, (0, 3, 2)):
            pl.when(me != without)(copy.wait_recv)
        add_into(gq.at[0], gs1[0, h, rows_s], qr[0], qr[1], qr[2])
        for copy in g1_z[0]:
            copy.start()

    def g1_after_x(p):
        if y_first[p]:
            g1_x[p].wait_recv()
        else:
            pl.when(me != 0)(g1_x[p].wait_recv)
        if y_first[p]:
            add_into(gq.at[p], gx[p, h, 0:192], xr[p, 0:192])
            for copy in g1_z[p]:
                copy.start()
        else:
            add_into(gx.at[p, 0], gs1[p, h], xr[p])
            g1_y[p].start()

    def g1_after_y(p):
        if y_first[p]:
            pl.when(me != 3)(g1_y[p].wait_recv)
        else:
            g1_y[p].wait_recv()
        if y_first[p]:
            for xh in range(2):
                add_into(gx.at[p, xh, 0:192], gs1[p, xh, rows_s], yr[p, xh])
            g1_x[p].start()
        else:
            add_into(gq.at[p], gx[p, 0, rows_s], yr[p, 0])
            for copy in g1_z[p]:
                copy.start()

    for copy in (loads[0], loads[1], *loads[5:8]):
        copy.wait()
    row_at = lax.broadcasted_iota(jnp.int32, (256, 1), 0) + own
    live_all = jnp.where(row_at < live_count, 1.0, 0.0)
    r2s[:, 1:2] = live_all
    wait_rows("att", att, ain)
    for x in range(2):
        ato[:, 384 * x:384 * x + 128] = ain[x, :, 0:128]
        ato[:, 384 * x + 128:384 * x + 256] = ain[x, :, 128:256] + ain[2 + x, :, 0:128]
        ato[:, 384 * x + 256:384 * x + 384] = ain[2 + x, :, 128:256]
    twin_o = pl.ds(pl.multiple_of(192 * (1 - c), 192), 192)
    twin_u = pl.ds(pl.multiple_of(384 * (1 - c), 384), 384)
    w_twin_in = [
        remote("wo_c", fwo.at[1 - h, twin_o], fwo.at[1 - h, twin_o], twin),
        remote("wu_c", fwu.at[1 - h, twin_u], fwu.at[1 - h, twin_u], twin),
        remote("wd_c", fwd.at[1 - h, twin_o], fwd.at[1 - h, twin_o], twin),
    ]
    w_twin_in[0].wait_recv()
    wo_all = fwo[...].reshape(768, 768)
    t0[...] = nn(ato[...], wo_all)
    pl.when(s == 0)(lambda: take_weight(2))
    live_of = lambda rows: r2s[rows, 1:2]

    def middle_rows(rows, carry):
        x = res[rows].astype(F32) + live_of(rows) * (t0[rows] + o_bias)
        mid[rows] = x
        n2, r2 = normed(x)
        n2s[rows] = n2
        r2s[rows, 0:1] = r2
        sec[rows] = (n2 * f_gain + f_shift).astype(BF)
        return carry

    row_loop(256, 64, middle_rows, 0)
    w_twin_in[1].wait_recv()
    u_recv = remote("ub", ub.at[1 - h], ub.at[1 - h], x_peer)
    u_recv.wait_recv()
    for x in range(2):
        t0[:, 384 * x:384 * (x + 1)] = nn(sec[...], fwu[x]) + ub[x, 0:1]

    def gelu_rows(rows, carry):
        u = t0[rows]
        cdf = 0.5 * (1.0 + lax.erf(u * math.sqrt(0.5)))
        hid[rows] = (u * cdf).astype(BF)
        t1[rows] = cdf + u * (jnp.exp(-0.5 * u * u) * (1.0 / math.sqrt(2.0 * math.pi)))
        return carry

    row_loop(256, 64, gelu_rows, 0)
    w_twin_in[2].wait_recv()
    wd_all = fwd[...].reshape(768, 768)
    t0[...] = nn(hid[...], wd_all)
    zero_row = jnp.zeros((1, 768), F32)

    def out_rows(rows, carry):
        live = live_of(rows)
        x = (mid[rows] + live * (t0[rows] + d_bias)) - res[rows].astype(F32)
        dov[rows] = x.astype(BF)
        down = (live * cotv[rows]).astype(BF)
        dc[rows] = down
        return carry + col_sum(down.astype(F32))

    down_bias_sum = row_loop(256, 64, out_rows, zero_row)
    own_rows = pl.ds(own, 256)
    other_rows = pl.ds(other, 256)
    out_send = remote("out", dov, d_out.at[own_rows], x_peer)
    out_node = remote("out", dov.at[0:NODES], d_out.at[0:NODES], x_peer)
    g1_compute(0)
    stores = [local(10, dov, d_out.at[own_rows])]
    stores[0].start()
    zb[...] = jnp.zeros_like(zb)
    far = [local(18 + k, zb, ref.at[256:512]) for k, ref in enumerate((d_out, d_tok))]
    near = [local(18 + k, zb.at[NODES:256], ref.at[NODES:256]) for k, ref in enumerate((d_out, d_tok))]

    @pl.when(me == 0)
    def _():
        for copy in far:
            copy.start()

    @pl.when(me == 1)
    def _():
        for copy in near:
            copy.start()

    t0[...] = nt(dc[...], wd_all)

    def inner_rows(rows, carry):
        x = (t0[rows] * t1[rows]).astype(BF)
        ig[rows] = x
        return carry + col_sum(x.astype(F32))

    up_bias_sum = row_loop(256, 64, inner_rows, zero_row)
    t0[...] = nt(ig[:, 0:384], fwu[0]) + nt(ig[:, 384:768], fwu[1])

    def second_rows(rows, carry):
        gain_sum, shift_sum, bias_sum = carry
        sg, n2 = t0[rows], n2s[rows]
        g = sg * f_gain
        back = r2s[rows, 0:1] * (
            g - jnp.mean(g, axis=-1, keepdims=True) - n2 * jnp.mean(g * n2, axis=-1, keepdims=True)
        )
        mgd[rows] = back
        x = (live_of(rows) * (cotv[rows] + back)).astype(BF)
        ac[rows] = x
        return gain_sum + col_sum(sg * n2), shift_sum + col_sum(sg), bias_sum + col_sum(x.astype(F32))

    f_gain_sum, f_shift_sum, out_bias_sum = row_loop(
        256, 64, second_rows, (zero_row, zero_row, zero_row)
    )
    ago[...] = nt(ac[...], wo_all).astype(BF)

    for k, (dev_sh, first, count) in enumerate(OWNERS):
        mine = 2 * dev_sh[0] + dev_sh[1]

        @pl.when(me == mine)
        def _():
            for r in range(4):
                cols = slice(384 * (r % 2) + 128 * (r // 2), 384 * (r % 2) + 128 * (r // 2) + 256)
                if r == mine:
                    da[first:first + count] = ago[0:count, cols]
                else:
                    i, j = sem_id("da_s", 4) + r, sem_id("da", 3) + k
                    pltpu.make_async_remote_copy(
                        src_ref=ago.at[0:count, cols], dst_ref=da.at[first:first + count],
                        send_sem=ss.at[i], recv_sem=rs.at[j],
                        device_id=(m, r // 2, r % 2), device_id_type=MESH,
                    ).start()

    g1_compute(1)
    g1_compute(2)
    for p in range(3):
        g1_after_twin(p)

    for k, (dev_sh, first, count) in enumerate(OWNERS):
        mine = 2 * dev_sh[0] + dev_sh[1]

        @pl.when(me != mine)
        def _():
            j = sem_id("da", 3) + k
            pltpu.make_async_remote_copy(
                src_ref=ago.at[0:count, 0:256], dst_ref=da.at[first:first + count],
                send_sem=ss.at[j], recv_sem=rs.at[j], device_id=x_peer, device_id_type=MESH,
            ).wait_recv()

    @pl.when(me != 1)
    def _():
        for copy in (*g1_q, g1_y[1], g1_x[2]):
            copy.start()

    head_col = lax.broadcasted_iota(jnp.int32, (256, 128), 1)
    lane_row = lax.broadcasted_iota(jnp.int32, (256, 128), 0) - 64 * s
    head_pick = jnp.where(
        (lane_row >= 0) & (lane_row < 192) & (lane_row // HEAD_DIM == head_col), 1.0, 0.0
    ).astype(BF)
    prod = da[0:TOTAL].astype(F32) * attf[...]
    prod_hi = prod.astype(BF)
    delta[...] = nn(prod_hi, head_pick) + nn((prod - prod_hi.astype(F32)).astype(BF), head_pick)
    for j in range(HEADS_HERE):
        dam[j] = jnp.where(head_of == j, da[0:TOTAL], zero)
    dkf[...] = jnp.zeros_like(dkf)
    dvf[...] = jnp.zeros_like(dvf)
    for (q0, qn, segs), pr in zip(BLOCKS, probs):
        o = 0
        for a, n in segs:
            dv = None
            for j in range(HEADS_HERE):
                pv = tn(pr[j * qn:(j + 1) * qn, o:o + n], dam[j, q0:q0 + qn])
                dv = pv if dv is None else dv + pv
            dvf[a:a + n] += dv
            o += n
    dxw[:, 512:768] = dvf[0:TOTAL].astype(BF)

    lanes2 = [slice(0, 256), slice(256, 512), slice(512, 640)]
    g2_twin = [
        remote("g2_c", g2.at[1 - c, :, lanes2[p]], gs2.at[:, lanes2[p]], twin, p, 3) for p in range(3)
    ]
    g2_z = [
        [
            remote("g2_z", gs2.at[chunk(lax.rem(z + d, zc), zn2), lanes2[p]], zr2.at[d - 1, :, lanes2[p]],
                   z_peers[d - 1], p * (zc - 1) + d - 1, 3 * (zc - 1))
            for d in range(1, zc)
        ]
        for p in range(3)
    ]

    def tiles_of(k):
        first = dxw[:, 256 * k:256 * k + 128]
        last = dxw[:, 256 * k + 128:256 * k + 256]
        return jnp.where(s == 0, first, last), jnp.where(s == 0, last, first)

    def g2_compute(p):
        for cc in range(2):
            g2[cc, :, lanes2[p]] = tn(fin1[0:TOTAL, cut[cc]], dxp[:, lanes2[p]]).astype(BF)
        g2_twin[p].start()

    def g2_after_twin(p):
        g2_twin[p].wait_recv()
        add_into(gs2.at[:, lanes2[p]], g2[c, :, lanes2[p]], gs2[:, lanes2[p]])
        for copy in g2_z[p]:
            copy.start()

    stores.append(local(11, dtv, d_tok.at[own_rows]))
    st1, st2 = [None] * 3, [None] * 3
    f1_z, f1_y, f1_c, f2_z, f2_y, f2_c = [], [], [], [], [], []

    def f1_at(p, cc, ss_, zz):
        return f1.at[p, cc, pl.ds(pl.multiple_of(192 * ss_ + zn1 * zz, 16), zn1)]

    def f1_half(p, ss_):
        return f1.at[p, c, pl.ds(pl.multiple_of(192 * ss_, 192), 192)]

    def f2_at(p, cc, ss_, zz):
        return f2.at[ss_, pl.ds(pl.multiple_of(384 * cc + zn2 * zz, 16), zn2), lanes2[p]]

    def f2_half(p, ss_):
        return f2.at[ss_, pl.ds(pl.multiple_of(384 * c, 384), 384), lanes2[p]]

    def g1_after_z(p):
        for copy in g1_z[p]:
            copy.wait_recv()
        add_into(fz1.at[p], gq[p, chunk(z, zn1)], *[zr1[p, d] for d in range(zc - 1)])
        f1_z.append([
            remote("f1_z", fz1.at[p], f1_at(p, c, s, z), z_peers[d], p * (zc - 1) + d, 3 * (zc - 1))
            for d in range(zc - 1)
        ])
        for copy in f1_z[p]:
            copy.start()
        stores.append(local(12 + p, fz1.at[p], f1_at(p, c, s, z)))
        stores[-1].start()
        return stores[-1]

    def f1_after_z(p, store):
        for copy in f1_z[p]:
            copy.wait_recv()
        store.wait()
        f1_y.append(remote("f1_y", f1_half(p, s), f1_half(p, s), y_peer, p, 3))
        f1_c.append(remote("f1_c", f1_half(p, s), f1_half(p, s), twin, 2 * p, 6))
        f1_y[p].start()
        f1_c[-1].start()

    def f1_after_y(p):
        f1_y[p].wait_recv()
        f1_c.append(remote("f1_c", f1_half(p, 1 - s), f1_half(p, 1 - s), twin, 2 * p + 1, 6))
        f1_c[-1].start()

    def g2_after_z(p):
        for copy in g2_z[p]:
            copy.wait_recv()
        add_into(
            fz2.at[:, lanes2[p]], gs2[chunk(z, zn2), lanes2[p]], *[zr2[d, :, lanes2[p]] for d in range(zc - 1)]
        )
        f2_z.append([
            remote("f2_z", fz2.at[:, lanes2[p]], f2_at(p, c, s, z), z_peers[d], p * (zc - 1) + d, 3 * (zc - 1))
            for d in range(zc - 1)
        ])
        for copy in f2_z[p]:
            copy.start()
        stores.append(local(15 + p, fz2.at[:, lanes2[p]], f2_at(p, c, s, z)))
        stores[-1].start()
        return stores[-1]

    def f2_after_z(p, store):
        for copy in f2_z[p]:
            copy.wait_recv()
        store.wait()
        f2_y.append(remote("f2_y", f2_half(p, s), f2_half(p, s), y_peer, p, 3))
        f2_c.append(remote("f2_c", f2_half(p, s), f2_half(p, s), twin, 2 * p, 6))
        f2_y[p].start()
        f2_c[-1].start()

    def f2_after_y(p):
        f2_y[p].wait_recv()
        f2_c.append(remote("f2_c", f2_half(p, 1 - s), f2_half(p, 1 - s), twin, 2 * p + 1, 6))
        f2_c[-1].start()


    dxp[:, 0:128], dxp[:, 128:256] = tiles_of(2)
    g2_compute(0)
    g1_after_quad()
    for b, (q0, qn, segs) in enumerate(BLOCKS):
        pr = probs[b]
        for j0 in range(0, HEADS_HERE, group):
            ab = dam[j0:j0 + group, q0:q0 + qn, :].reshape(group * qn, 256)
            o = 0
            for a, n in segs:
                pg = nt(ab, qkv[a:a + n, 512:768])
                for g in range(group):
                    j = j0 + g
                    r = slice(j * qn, (j + 1) * qn)
                    ds[r, o:o + n] = (
                        pr[r, o:o + n].astype(F32)
                        * (pg[g * qn:(g + 1) * qn] - delta[q0:q0 + qn, j:j + 1])
                    ).astype(BF)
                o += n
        o, acc = 0, None
        for a, n in segs:
            part = nn(ds[0:HEADS_HERE * qn, o:o + n], qkv[a:a + n, 256:512])
            acc = part if acc is None else acc + part
            o += n
        dxw[q0:q0 + qn, 0:256] = (pick_heads(acc, qn) * SCALE).astype(BF)
        o = 0
        for a, n in segs:
            dk = None
            for j in range(HEADS_HERE):
                pk = tn(ds[j * qn:(j + 1) * qn, o:o + n], qm[j, q0:q0 + qn])
                dk = pk if dk is None else dk + pk
            dkf[a:a + n] += dk
            o += n
        if b == 0:
            g2_after_twin(0)
        if b == 1:
            g1_after_y(1)
        if b == 2:
            g1_after_x(2)
        if b == 3:
            st1[0] = g1_after_z(0)
        if b == 4:
            g1_after_x(1)
            st2[0] = g2_after_z(0)
    g1_after_y(2)
    dxw[:, 256:512] = (dkf[0:TOTAL] * SCALE).astype(BF)
    q_full, q_half = tiles_of(0)
    k_full, k_half = tiles_of(1)
    dxp[:, 256:384], dxp[:, 384:512] = q_full, k_full
    dxp[:, 512:640] = (q_half.astype(F32) + pltpu.roll(k_half.astype(F32), 64, 1)).astype(BF)

    fp_x = [
        remote("fp_x", fp.at[chunk(2 * (1 - h) + k, 128)], fx.at[chunk(k, 128)], x_peer, k, 3)
        for k in range(2)
    ]
    fp_xn = [
        remote("fp_xn", fs.at[256 + 96 * k:256 + 96 * (k + 1)], fx.at[256 + 96 * k:256 + 96 * (k + 1)], x_peer, k, 2)
        for k in range(2)
    ]
    fp_y = [
        remote("fp_y", fs.at[chunk(k, 128)], fy.at[chunk(k, 128)], y_peer, k, 2) for k in range(2)
    ]
    fp_yn = [
        remote("fp_yn", fp.at[EDGES + 96 * k:EDGES + 96 * (k + 1)], fy.at[96 * k:96 * (k + 1)], y_peer, k, 2)
        for k in range(2)
    ]
    def fp_after_x(k):
        fp_x[k].wait_recv()
        add_into(fs.at[chunk(k, 128)], fp[chunk(2 * h + k, 128)], fx[chunk(k, 128)])
        pl.when(s == 0)(fp_y[k].start)

    g2_compute(1)
    g2_compute(2)
    for k in range(2):
        rows = chunk(2 * (1 - h) + k, 128)
        fp[rows] = nt(dxw[rows], ww[...]).astype(BF)
        fp_x[k].start()
    g2_after_twin(1)
    g2_after_twin(2)
    fp[EDGES:TOTAL] = nt(dxw[EDGES:TOTAL], ww[...]).astype(BF)

    @pl.when(s == 1)
    def _():
        for copy in fp_yn:
            copy.start()

    fp[pl.ds(own, 256)] = nt(dxw[pl.ds(own, 256)], ww[...]).astype(BF)
    st1[1] = g1_after_z(1)
    f1_after_z(0, st1[0])
    fp_after_x(0)
    fp_after_x(1)
    pl.when(s == 1)(out_send.start)
    pl.when(me == 0)(out_node.start)
    f2_after_z(0, st2[0])

    @pl.when(s == 0)
    def _():
        for k in range(2):
            fp_yn[k].wait_recv()
            at = slice(256 + 96 * k, 256 + 96 * (k + 1))
            add_into(fs.at[at], fp[EDGES + 96 * k:EDGES + 96 * (k + 1)], fy[96 * k:96 * (k + 1)])
            pl.when(h == 1)(fp_xn[k].start)

    qkv_bias_sum = col_sum(dxw[...].astype(F32))

    st2[1] = g2_after_z(1)
    st2[2] = g2_after_z(2)

    def first_rows(rows, fg):
        n1, r1 = normed(res[rows].astype(F32))
        g = fg * a_gain
        back = r1 * (
            g - jnp.mean(g, axis=-1, keepdims=True) - n1 * jnp.mean(g * n1, axis=-1, keepdims=True)
        )
        dtv[rows] = (mgd[rows] + back).astype(BF)
        return jnp.concatenate([col_sum(fg * n1), col_sum(fg)], axis=0)

    def own_chunk(k, n):
        return pl.ds(pl.multiple_of(own + n * k, n), n)

    dt_e = [
        remote("dt", dtv.at[128 * k:128 * (k + 1)], d_tok.at[own_chunk(k, 128)], x_peer, k, 2)
        for k in range(2)
    ]
    dt_n = remote("dt", dtv.at[0:NODES], d_tok.at[0:NODES], x_peer, 0, 2)
    va[...] = jnp.zeros_like(va)

    @pl.when(s == 1)
    def _():
        for k in range(2):
            fp_y[k].wait_recv()

            def edge_rows(i, carry):
                rows = pl.ds(pl.multiple_of(128 * k + 64 * i, 64), 64)
                return carry + first_rows(rows, fs[rows].astype(F32) + fy[rows].astype(F32))

            got = lax.fori_loop(0, 2, edge_rows, jnp.zeros((2, 768), F32))
            va[0:2] += got
            dt_e[k].start()

    @pl.when((s == 0) & (h == 0))
    def _():
        for k in range(2):
            fp_xn[k].wait_recv()

            def node_rows(i, carry):
                rows = pl.ds(pl.multiple_of(96 * k + 32 * i, 32), 32)
                from_fs = pl.ds(pl.multiple_of(256 + 96 * k + 32 * i, 32), 32)
                return carry + first_rows(rows, fs[from_fs].astype(F32) + fx[from_fs].astype(F32))

            got = lax.fori_loop(0, 3, node_rows, jnp.zeros((2, 768), F32))
            va[0:2] += got
        dtv[NODES:256] = mgd[NODES:256].astype(BF)
        dt_n.start()

    @pl.when((s == 0) & (h == 1))
    def _():
        dtv[...] = mgd[...].astype(BF)

    stores[1].start()

    sums = [f_gain_sum, f_shift_sum, out_bias_sum, down_bias_sum, up_bias_sum, va[0:1], va[1:2], zero_row]
    sums += [jnp.where(me == r, qkv_bias_sum, 0.0) for r in range(4)] + [zero_row] * 4
    vq[me] = jnp.concatenate(sums, axis=0)
    v1 = [remote("v_q", vq.at[me], vq.at[me], dev, k, 3) for k, dev in enumerate(quad)]
    for copy in v1:
        copy.start()

    st1[2] = g1_after_z(2)
    f2_after_z(1, st2[1])
    f2_after_z(2, st2[2])
    f1_after_z(1, st1[1])
    f1_after_y(0)
    f2_after_y(0)
    v1_in = [
        remote("v_q", vq.at[r], vq.at[r], dev, k, 3)
        for k, (dev, r) in enumerate(zip(quad, (2 * s + 1 - h, 2 - 2 * s + h, 3 - 2 * s - h)))
    ]
    for copy in v1_in:
        copy.wait_recv()
    vz[z] = vq[0] + vq[1] + vq[2] + vq[3]
    v2 = [remote("v_z", vz.at[z], vz.at[z], z_peers[d], d, zc - 1) for d in range(zc - 1)]
    for copy in v2:
        copy.start()
    f1_after_z(2, st1[2])
    f1_after_y(1)
    f2_after_y(1)
    f2_after_y(2)
    for copy in v2:
        copy.wait_recv()
    vsum = vz[0]
    for d in range(1, zc):
        vsum = vsum + vz[d]
    vc[c] = vsum
    v3 = remote("v_c", vc.at[c], vc.at[c], twin)
    v3.start()
    f1_after_y(2)
    v3.wait_recv()
    vec[...] = vc[0] + vc[1]
    for copy in (*f1_c, *f2_c):
        copy.wait_recv()
    for copy in stores[0:2]:
        copy.wait()

    @pl.when(s == 1)
    def _():
        for copy in (*dt_e, out_send):
            copy.wait()

    @pl.when(me == 0)
    def _():
        for copy in (dt_n, out_node):
            copy.wait_send()
        for copy in far:
            copy.wait()

    @pl.when(me == 1)
    def _():
        for copy in (dt_n, out_node):
            copy.wait_recv()
        for copy in near:
            copy.wait()

    @pl.when(s == 1)
    def _():
        for copy in tok_y:
            copy.wait_send()

    @pl.when(s == 0)
    def _():
        tok_n.wait_send()
        for copy in tok_x:
            copy.wait_send()

    @pl.when(me != 1)
    def _():
        for copy in (*g1_q, g1_y[1], g1_x[2]):
            copy.wait_send()

    wait_sent("att", att, ain)

    @pl.when(s == 0)
    def _():
        for copy in fp_y:
            copy.wait_send()

    @pl.when(me == 1)
    def _():
        for copy in fp_xn:
            copy.wait_send()

    @pl.when(s == 1)
    def _():
        for copy in fp_yn:
            copy.wait_send()

    @pl.when(s == 1)
    def _():
        w_out[0].wait_send()
        w_out[2].wait_send()
        w_y[0].wait_send()
        w_y[2].wait_send()

    for k, (dev_sh, first, count) in enumerate(OWNERS):
        mine = 2 * dev_sh[0] + dev_sh[1]

        @pl.when(me == mine)
        def _():
            for r in range(4):
                if r != mine:
                    i = sem_id("da_s", 4) + r
                    pltpu.make_async_remote_copy(
                        src_ref=ago.at[0:count, 0:256], dst_ref=da.at[first:first + count],
                        send_sem=ss.at[i], recv_sem=rs.at[i], device_id=x_peer, device_id_type=MESH,
                    ).wait_send()

    for copy in (
        u_send, w_out[1], *w_twin, *g1_twin, g1_x[1], g1_y[2], *sum(g1_z, []), *fp_x, *g2_twin,
        *sum(g2_z, []), *v1, *sum(f1_z, []), *f1_y, *f1_c, *sum(f2_z, []), *f2_y, *f2_c, *v2, v3,
    ):
        copy.wait_send()


def finish_kernel(
    tokens, cot, d_out, d_tok, f1, f2, vec,
    output, tokens_grad, a_gain, a_shift, wq, bq, wk, wv, bv, wo, bo, f_gain, f_shift, wu, bu, wd, bd,
):
    h = lax.axis_index("head")
    output[...] = tokens[...].astype(F32) + d_out[...].astype(F32)
    tokens_grad[...] = cot[...] + d_tok[...].astype(F32)
    for k in range(2):
        lanes = slice(384 * k, 384 * (k + 1))
        wd[:, lanes] = f1[0, k].astype(F32)
        wo[:, lanes] = f1[2, k].astype(F32)
        wu[k] = f1[1, k].astype(F32)
    low_half = lax.broadcasted_iota(jnp.int32, (1, 128), 1) < 64
    tile = lambda k, t: f2[k, :, 128 * t:128 * (t + 1)].astype(F32)
    for t, out in ((0, wv), (2, wq), (3, wk)):
        out[:, 0:128] = tile(0, t)
        out[:, 256:384] = tile(1, t)
    wq[:, 128:256] = jnp.where(low_half, tile(0, 4), tile(1, 4))
    wk[:, 128:256] = pltpu.roll(jnp.where(low_half, tile(1, 4), tile(0, 4)), 64, 1)
    wv[:, 128:256] = jnp.where(low_half, tile(0, 1), tile(1, 1))

    @pl.when(pl.program_id(0) == 0)
    def _():
        mine = pl.ds(pl.multiple_of(384 * h, 384), 384)
        for row, out in ((0, f_gain), (1, f_shift), (2, bo), (3, bd), (4, bu), (5, a_gain), (6, a_shift)):
            out[...] = vec[row:row + 1, mine].reshape(384)
        low = jnp.where(h == 0, vec[8:9], vec[9:10])
        high = jnp.where(h == 0, vec[10:11], vec[11:12])
        for first, out in ((0, bq), (512, bv)):
            a, b = low[:, first:first + 256], high[:, first:first + 256]
            parts = [a[:, 0:128], a[:, 128:256] + b[:, 0:128], b[:, 128:256]]
            out[...] = jnp.concatenate(parts, axis=1).reshape(384)


def fast_layer(
    tokens, cotangent, attn_gain, attn_shift, query_weight, query_bias, key_weight, value_weight,
    value_bias, out_weight, out_bias, ffn_gain, ffn_shift, up_weight, up_bias, down_weight,
    down_bias, atom_counts, edge_counts,
):
    zc = lax.axis_size("mol") // 2
    anywhere = pl.BlockSpec(memory_space=pl.ANY)
    vmem = pl.BlockSpec(memory_space=pltpu.VMEM)
    smem = pl.BlockSpec(memory_space=pltpu.SMEM)
    shape = jax.ShapeDtypeStruct
    SEM.clear()
    buf = lambda dtype, *dims: pltpu.VMEM(dims, dtype)
    scratch = [
        buf(BF, 256, 768), buf(BF, 256, 768), buf(BF, 256, 768), buf(BF, 3, 192 // zc, 384), buf(BF, 384 // zc, 640), buf(BF, TOTAL, 640),
        buf(BF, PADDED, 768), buf(BF, 256, 768), buf(F32, 256, 768), buf(BF, 768, 768),
        buf(BF, 2, 384, 768), buf(BF, 2, 768, 384), buf(BF, 2, 384, 768), buf(F32, 2, 8, 384),
        buf(BF, PADDED, 768), buf(BF, PADDED, 768), buf(BF, TOTAL, 768),
        buf(BF, HEADS_HERE, TOTAL, 256), buf(BF, HEADS_HERE, TOTAL, 256),
        buf(BF, 1024, 512), buf(BF, 1024, 512), buf(BF, 1024, 512), buf(BF, 1024, 512), buf(BF, 1536, 768),
        buf(F32, 256, 768), buf(jnp.int32, TOTAL, 1),
        buf(F32, TOTAL, 256), buf(BF, TOTAL, 256), buf(BF, 4, 256, 256), buf(BF, TOTAL, 256), buf(F32, TOTAL, 128),
        buf(F32, 256, 768), buf(F32, 256, 768), buf(F32, 256, 768), buf(F32, 256, 128), buf(F32, 256, 768),
        buf(BF, 256, 768), buf(BF, 256, 768), buf(BF, 256, 768), buf(BF, 256, 768), buf(BF, 256, 768),
        buf(BF, 256, 768), buf(BF, 256, 768), buf(F32, 256, 768),
        buf(BF, 1536, 768), buf(F32, PADDED, 256), buf(F32, PADDED, 256),
        buf(BF, 3, 2, 2, 384, 384), buf(BF, 3, 2, 384, 384), buf(BF, 3, 192, 384), buf(BF, 3, 384, 384), buf(BF, 3, 2, 384, 384),
        buf(BF, 3, 2, 192, 384), buf(BF, 3, 192, 384), buf(BF, 3, zc - 1, 192 // zc, 384),
        buf(BF, 2, 384, 640), buf(BF, 384, 640), buf(BF, zc - 1, 384 // zc, 640),
        buf(BF, TOTAL, 768), buf(BF, 256 + NODES, 768), buf(BF, 256 + NODES, 768), buf(BF, 256, 768),
        buf(F32, 8, 768), buf(F32, 4, 16, 768), buf(F32, zc, 16, 768), buf(F32, 2, 16, 768),
        pltpu.SemaphoreType.DMA((N_SEMS,)), pltpu.SemaphoreType.DMA((N_SEMS,)), pltpu.SemaphoreType.DMA((N_LOCAL,)),
    ]
    d_out, d_tok, f1, f2, vec = pl.pallas_call(
        layer_kernel,
        out_shape=[
            shape((512, 768), BF), shape((512, 768), BF), shape((3, 2, 384, 384), BF),
            shape((2, 768, 640), BF), shape((16, 768), F32),
        ],
        in_specs=[anywhere] * 8 + [smem] * 2 + [vmem] * 9,
        out_specs=[anywhere] * 4 + [vmem],
        scratch_shapes=scratch,
        compiler_params=pltpu.CompilerParams(
            collective_id=0, has_side_effects=True, vmem_limit_bytes=61 * 2**20
        ),
        name="layer",
    )(
        tokens, cotangent, query_weight, key_weight, value_weight, out_weight, up_weight, down_weight,
        atom_counts, edge_counts, attn_gain, attn_shift, query_bias, value_bias, out_bias,
        ffn_gain, ffn_shift, up_bias, down_bias,
    )
    assert sum(n for _, n in SEM.values()) <= N_SEMS
    steps = 2
    mat, tall, line = shape((384, 768), F32), shape((768, 384), F32), shape((384,), F32)
    big, pair = shape((512, 768), F32), shape((2, 384, 384), F32)
    by_rows = lambda rows, cols: pl.BlockSpec((rows // steps, cols), lambda i: (i, 0))
    big_spec, mat_spec, tall_spec = by_rows(512, 768), by_rows(384, 768), by_rows(768, 384)
    line_spec = pl.BlockSpec((384,), lambda i: (0,))
    pair_spec = pl.BlockSpec((2, 384 // steps, 384), lambda i: (0, i, 0))
    outs = pl.pallas_call(
        finish_kernel,
        grid=(steps,),
        out_shape=[big, big, line, line, tall, line, tall, tall, line, mat, line, line, line, pair, line, mat, line],
        in_specs=[
            big_spec, big_spec, big_spec, big_spec,
            pl.BlockSpec((3, 2, 384 // steps, 384), lambda i: (0, 0, i, 0)),
            pl.BlockSpec((2, 768 // steps, 640), lambda i: (0, i, 0)),
            pl.BlockSpec((16, 768), lambda i: (0, 0)),
        ],
        out_specs=[
            big_spec, big_spec, line_spec, line_spec, tall_spec, line_spec, tall_spec, tall_spec, line_spec,
            mat_spec, line_spec, line_spec, line_spec, pair_spec, line_spec, mat_spec, line_spec,
        ],
        compiler_params=pltpu.CompilerParams(vmem_limit_bytes=60 * 2**20),
        name="finish",
    )(tokens, cotangent, d_out, d_tok, f1, f2, vec)
    return tuple(o.reshape(768, 384) if o.ndim == 3 else o for o in outs)


def plain_dot(operand, partner):
    return jnp.dot(operand, partner, preferred_element_type=jnp.float32)


def lead_dot(operand, partner):
    return lax.dot_general(
        operand, partner, (((0,), (0,)), ((), ())), preferred_element_type=jnp.float32
    )


def tail_dot(operand, partner):
    return lax.dot_general(
        operand, partner, (((1,), (1,)), ((), ())), preferred_element_type=jnp.float32
    )


def norm_apply(values, gain_vec, shift_vec):
    row_mean = jnp.mean(values, axis=-1, keepdims=True)
    centered = values - row_mean
    variance = jnp.mean(centered * centered, axis=-1, keepdims=True)
    return centered * lax.rsqrt(variance + 1e-05) * gain_vec + shift_vec


def gelu_exact(values):
    return jax.nn.gelu(values, approximate=False)


def segment_ids(counts, added, slot_count):
    members = jnp.arange(counts.shape[0])
    earlier = members[:, None] <= members[None, :]
    seg_ends = jnp.sum(jnp.where(earlier, (counts + added)[:, None], 0), axis=0)
    positions = jnp.arange(slot_count, dtype=jnp.int32)
    return jnp.sum((positions[:, None] >= seg_ends[None, :]).astype(jnp.int32), axis=1)


def head_piece(vector, head_rank, head_share):
    return lax.dynamic_slice_in_dim(vector, head_rank * head_share, head_share)


def on_device(
    tokens,
    cotangent,
    attn_gain,
    attn_shift,
    query_weight,
    query_bias,
    key_weight,
    value_weight,
    value_bias,
    out_weight,
    out_bias,
    ffn_gain,
    ffn_shift,
    up_weight,
    up_bias,
    down_weight,
    down_bias,
    atom_counts,
    edge_counts,
):
    row_count = tokens.shape[0]
    model_width = tokens.shape[1]
    local_width = query_weight.shape[1]
    local_heads = local_width // HEAD_DIM
    head_count = lax.axis_size("head")
    head_rank = lax.axis_index("head")
    stream_rank = lax.axis_index("stream")
    molecules = atom_counts.shape[1]
    head_share = model_width // head_count
    score_scale = HEAD_DIM ** (-0.5)
    seg_node = segment_ids(atom_counts[0], 1, row_count)
    seg_edge = segment_ids(edge_counts[0], 0, row_count)
    key_seg = jnp.concatenate([seg_node, seg_edge])
    own_seg = jnp.where(stream_rank == 0, seg_node, seg_edge)
    live_rows = (own_seg < molecules).astype(jnp.float32)[:, None]
    residual = tokens.astype(jnp.float32)
    normed, norm_pull = jax.vjp(norm_apply, residual, attn_gain, attn_shift)
    first_in = normed.astype(jnp.bfloat16)
    queries = (plain_dot(first_in, query_weight) + query_bias).astype(jnp.bfloat16)
    keys_local = plain_dot(first_in, key_weight).astype(jnp.bfloat16)
    values_local = (plain_dot(first_in, value_weight) + value_bias).astype(jnp.bfloat16)
    all_keys, all_values = (
        lax.all_gather(keys_local, "stream", axis=0, tiled=True),
        lax.all_gather(values_local, "stream", axis=0, tiled=True),
    )
    key_count = all_keys.shape[0]
    key_heads = all_keys.reshape(key_count, local_heads, HEAD_DIM)
    value_heads = all_values.reshape(key_count, local_heads, HEAD_DIM)
    blocks = row_count // 512
    block_rows = row_count // blocks
    query_blocks = queries.reshape(blocks, block_rows, local_heads, HEAD_DIM)
    seg_blocks = own_seg.reshape(blocks, block_rows)

    def forward_block(pieces):
        query_part, seg_part = pieces
        scores = (
            jnp.einsum("qhd,khd->hqk", query_part, key_heads, preferred_element_type=jnp.float32)
            * score_scale
        )
        same_mol = (seg_part[:, None] == key_seg[None, :])[None]
        scores = jnp.where(same_mol, scores, -1e30)
        row_top = jnp.max(scores, axis=-1, keepdims=True)
        shifted = jnp.exp(scores - row_top)
        row_total = jnp.sum(shifted, axis=-1, keepdims=True)
        prob_low = (shifted / row_total).astype(jnp.bfloat16)
        attended_part = jnp.einsum(
            "hqk,khd->qhd", prob_low, value_heads, preferred_element_type=jnp.float32
        )
        return (attended_part.astype(jnp.bfloat16), (row_top + jnp.log(row_total))[..., 0])

    attended_blocks, lse_blocks = lax.map(forward_block, (query_blocks, seg_blocks))
    attended = attended_blocks.reshape(row_count, local_width)
    attn_sum = lax.psum(plain_dot(attended, out_weight), "head")
    middle = residual + live_rows * (attn_sum + out_bias)
    second, second_pull = jax.vjp(norm_apply, middle, ffn_gain, ffn_shift)
    second_in = second.astype(jnp.bfloat16)
    inner_pre = plain_dot(second_in, up_weight) + up_bias.astype(jnp.float32)
    activated, gelu_pull = jax.vjp(gelu_exact, inner_pre)
    hidden = activated.astype(jnp.bfloat16)
    ffn_sum = lax.psum(plain_dot(hidden, down_weight).astype(jnp.bfloat16), "head").astype(
        jnp.float32
    )
    output = middle + live_rows * (ffn_sum + down_bias)
    down_cot = (live_rows * cotangent).astype(jnp.bfloat16)
    down_weight_grad = lead_dot(hidden, down_cot)
    down_bias_full = jnp.sum(down_cot.astype(jnp.float32), axis=0)
    inner_grad = gelu_pull(tail_dot(down_cot, down_weight))[0].astype(jnp.bfloat16)
    up_weight_grad = lead_dot(second_in, inner_grad)
    up_bias_grad = jnp.sum(inner_grad.astype(jnp.float32), axis=0)
    second_grad = lax.psum(tail_dot(inner_grad, up_weight), "head")
    middle_part, ffn_gain_full, ffn_shift_full = second_pull(second_grad)
    mid_grad = cotangent + middle_part
    ffn_gain_grad = head_piece(ffn_gain_full, head_rank, head_share)
    ffn_shift_grad = head_piece(ffn_shift_full, head_rank, head_share)
    down_bias_grad = head_piece(down_bias_full, head_rank, head_share)
    attn_cot = (live_rows * mid_grad).astype(jnp.bfloat16)
    out_weight_grad = lead_dot(attended, attn_cot)
    out_bias_full = jnp.sum(attn_cot.astype(jnp.float32), axis=0)
    attended_grad = tail_dot(attn_cot, out_weight).astype(jnp.bfloat16)
    grad_blocks = attended_grad.reshape(blocks, block_rows, local_heads, HEAD_DIM)

    def backward_block(running, pieces):
        key_acc, value_acc = running
        query_part, seg_part, lse_part, grad_part = pieces
        scores = (
            jnp.einsum("qhd,khd->hqk", query_part, key_heads, preferred_element_type=jnp.float32)
            * score_scale
        )
        same_mol = (seg_part[:, None] == key_seg[None, :])[None]
        prob_full = jnp.where(same_mol, jnp.exp(scores - lse_part[..., None]), 0.0)
        prob_low = prob_full.astype(jnp.bfloat16)
        prob_grad = jnp.einsum(
            "qhd,khd->hqk", grad_part, value_heads, preferred_element_type=jnp.float32
        )
        row_delta = jnp.sum(prob_grad * prob_full, axis=-1, keepdims=True)
        score_grad = (prob_full * (prob_grad - row_delta)).astype(jnp.bfloat16)
        query_part_grad = (
            jnp.einsum("hqk,khd->qhd", score_grad, key_heads, preferred_element_type=jnp.float32)
            * score_scale
        )
        key_acc = (
            key_acc
            + jnp.einsum("hqk,qhd->khd", score_grad, query_part, preferred_element_type=jnp.float32)
            * score_scale
        )
        value_acc = value_acc + jnp.einsum(
            "hqk,qhd->khd", prob_low, grad_part, preferred_element_type=jnp.float32
        )
        return ((key_acc, value_acc), query_part_grad.astype(jnp.bfloat16))

    zero_keys = jnp.zeros((key_count, local_heads, HEAD_DIM), jnp.float32)
    (key_acc, value_acc), query_grads = lax.scan(
        backward_block, (zero_keys, zero_keys), (query_blocks, seg_blocks, lse_blocks, grad_blocks)
    )
    key_sum, value_sum = (
        lax.psum_scatter(
            key_acc.reshape(key_count, local_width), "stream", scatter_dimension=0, tiled=True
        ),
        lax.psum_scatter(
            value_acc.reshape(key_count, local_width), "stream", scatter_dimension=0, tiled=True
        ),
    )
    key_grad = key_sum.astype(jnp.bfloat16)
    value_grad = value_sum.astype(jnp.bfloat16)
    query_grad = query_grads.reshape(row_count, local_width)
    query_weight_grad = lead_dot(first_in, query_grad)
    query_bias_grad = jnp.sum(query_grad.astype(jnp.float32), axis=0)
    key_weight_grad = lead_dot(first_in, key_grad)
    value_weight_grad = lead_dot(first_in, value_grad)
    value_bias_grad = jnp.sum(value_grad.astype(jnp.float32), axis=0)
    first_part = (
        tail_dot(query_grad, query_weight)
        + tail_dot(key_grad, key_weight)
        + tail_dot(value_grad, value_weight)
    )
    first_grad = lax.psum(first_part.astype(jnp.bfloat16), "head").astype(jnp.float32)
    resid_part, attn_gain_full, attn_shift_full = norm_pull(first_grad)
    tokens_grad = mid_grad + resid_part
    attn_gain_grad = head_piece(attn_gain_full, head_rank, head_share)
    attn_shift_grad = head_piece(attn_shift_full, head_rank, head_share)
    out_bias_grad = head_piece(out_bias_full, head_rank, head_share)
    (
        attn_gain_grad,
        attn_shift_grad,
        query_weight_grad,
        query_bias_grad,
        key_weight_grad,
        value_weight_grad,
        value_bias_grad,
        out_weight_grad,
        out_bias_grad,
        ffn_gain_grad,
        ffn_shift_grad,
        up_weight_grad,
        up_bias_grad,
        down_weight_grad,
        down_bias_grad,
    ) = lax.psum(
        (
            attn_gain_grad,
            attn_shift_grad,
            query_weight_grad,
            query_bias_grad,
            key_weight_grad,
            value_weight_grad,
            value_bias_grad,
            out_weight_grad,
            out_bias_grad,
            ffn_gain_grad,
            ffn_shift_grad,
            up_weight_grad,
            up_bias_grad,
            down_weight_grad,
            down_bias_grad,
        ),
        ("mol", "stream"),
    )
    return (
        output,
        tokens_grad,
        attn_gain_grad,
        attn_shift_grad,
        query_weight_grad,
        query_bias_grad,
        key_weight_grad,
        value_weight_grad,
        value_bias_grad,
        out_weight_grad,
        out_bias_grad,
        ffn_gain_grad,
        ffn_shift_grad,
        up_weight_grad,
        up_bias_grad,
        down_weight_grad,
        down_bias_grad,
    )


def solution(mesh):
    in_specs = (
        P(("mol", "stream"), None),
        P(("mol", "stream"), None),
        P(),
        P(),
        P(None, "head"),
        P("head"),
        P(None, "head"),
        P(None, "head"),
        P("head"),
        P("head", None),
        P(),
        P(),
        P(),
        P(None, "head"),
        P("head"),
        P("head", None),
        P(),
        P("mol", None),
        P("mol", None),
    )
    out_specs = (
        P(("mol", "stream"), None),
        P(("mol", "stream"), None),
        P("head"),
        P("head"),
        P(None, "head"),
        P("head"),
        P(None, "head"),
        P(None, "head"),
        P("head"),
        P("head", None),
        P("head"),
        P("head"),
        P("head"),
        P(None, "head"),
        P("head"),
        P("head", None),
        P("head"),
    )
    one_chip_pair = (
        mesh.shape["head"] == 2 and mesh.shape["stream"] == 2 and mesh.shape["mol"] == 8
    )
    return jax.shard_map(
        fast_layer if one_chip_pair else on_device, mesh=mesh, in_specs=in_specs, out_specs=out_specs, check_vma=False
    )
```
